32 devices in a mesh: dp: 16 (over z, x, core), step: 2 (over y).
Axes of the slice: x: 2, y: 2, z: 4, core: 2. Of those that a mesh axis runs over, the one named last changes fastest.
Arguments:
- tokens: bfloat16 [16, 512, 1024], P('dp'), may hold values from -6 to 6
- cotangent: bfloat16 [16, 512, 1024], P('dp'), may hold values from -6 to 6
- domains: int32 [16], replicated, may hold values from 0 to 7
- doc_ids: int32 [16, 512], P('dp'), may hold values from 0 to 3, never falling along the last dimension, each value on 1 to 256 neighbouring positions
- norm_gain: float32 [1024], replicated, may hold values from 0.5 to 1.5
- w_query: bfloat16 [1024, 1024], P('dp', 'step'), may hold values from -0.1875 to 0.1875
- w_outgate: bfloat16 [1024, 1024], P('dp', 'step'), may hold values from -0.1875 to 0.1875
- w_key: bfloat16 [2, 1024, 1024], P('step', 'dp'), may hold values from -0.1875 to 0.1875
- w_value: bfloat16 [2, 1024, 1024], P('step', 'dp'), may hold values from -0.1875 to 0.1875
- w_beta: bfloat16 [2, 1024, 8], P('step', 'dp'), may hold values from -0.1875 to 0.1875
- w_alpha: bfloat16 [1024, 8], P('dp', 'step'), may hold values from -0.1875 to 0.1875
- decay_log: float32 [8], P('step'), may hold values from -4 to 0.5
- decay_bias: float32 [8], P('step'), may hold values from -4 to -1
- conv_query: float32 [4, 1024], P(None, 'step'), may hold values from -0.6 to 0.6
- conv_key: float32 [2, 4, 1024], P('step'), may hold values from -0.6 to 0.6
- conv_value: float32 [2, 4, 1024], P('step'), may hold values from -0.6 to 0.6
- mix_gain: float32 [128], replicated, may hold values from 0.5 to 1.5
- w_out: bfloat16 [1024, 1024], P('step', 'dp'), may hold values from -0.25 to 0.25
- ffn_gain: float32 [1024], replicated, may hold values from 0.5 to 1.5
- w_gate: bfloat16 [1024, 2816], P('dp', 'step'), may hold values from -0.1875 to 0.1875
- w_up: bfloat16 [1024, 2816], P('dp', 'step'), may hold values from -0.1875 to 0.1875
- w_down: bfloat16 [2816, 1024], P('step', 'dp'), may hold values from -0.15625 to 0.15625
Outputs:
- output: bfloat16 [16, 512, 1024], P('dp')
- input_grad: bfloat16 [16, 512, 1024], P('dp')
- grad_norm_gain: float32 [1024], replicated
- grad_query: float32 [1024, 1024], P('dp', 'step')
- grad_outgate: float32 [1024, 1024], P('dp', 'step')
- grad_key: float32 [2, 1024, 1024], P('step', 'dp')
- grad_value: float32 [2, 1024, 1024], P('step', 'dp')
- grad_beta: float32 [2, 1024, 8], P('step', 'dp')
- grad_alpha: float32 [1024, 8], P('dp', 'step')
- grad_decay_log: float32 [8], P('step')
- grad_decay_bias: float32 [8], P('step')
- grad_conv_query: float32 [4, 1024], P(None, 'step')
- grad_conv_key: float32 [2, 4, 1024], P('step')
- grad_conv_value: float32 [2, 4, 1024], P('step')
- grad_mix_gain: float32 [128], replicated
- grad_out: float32 [1024, 1024], P('step', 'dp')
- grad_ffn_gain: float32 [1024], replicated
- grad_gate: float32 [1024, 2816], P('dp', 'step')
- grad_up: float32 [1024, 2816], P('dp', 'step')
- grad_down: float32 [2816, 1024], P('step', 'dp')
The draws below stay inside these ranges and needn't reach their ends.
Inputs may be any that keep to these rules, and one draw needn't show every extreme that they name: `doc_ids`: document numbers within a row start at 0 and never fall.
All inputs are finite; a program needn't handle non-finite values.
Results may differ from the reference program's by a relative error of at most 0.018.
Values may be sent and summed in bfloat16 or wider, within the bound.
A program may use at most 192 MiB of HBM per device.

```python
import math
import jax
import jax.numpy as jnp
import numpy as np
from jax import lax

D = 1024
HEADS = 8
DK = 128
FF = 2816
NH = 2
KW = 4
STRETCH = 64
GROUPS = 8
SEQ = 512
ROWS = 16


def place_ends(entries, rng, least, top_value):
    place = [jax.random.randint(jax.random.fold_in(rng, axis), (), 0, length) for axis, length in enumerate(entries.shape)]
    longest = entries.shape.index(max(entries.shape))
    next_to = place[:longest] + [(place[longest] + 1) % entries.shape[longest]] + place[longest + 1:]
    return entries.at[tuple(place)].set(least).at[tuple(next_to)].set(top_value)


def block_levels(rng, extent, cuts, least, largest):
    loudness = 1.0
    for dim, parts in cuts:
        draws = jax.random.uniform(jax.random.fold_in(jax.random.fold_in(rng, 6), dim), (parts,), jnp.float32, least / len(cuts), largest / len(cuts))
        loudness = loudness * jnp.repeat(jnp.exp(draws), extent[dim] // parts).reshape((-1,) + (1,) * (len(extent) - 1 - dim))
    return loudness


def cumulative_ranks(number_of, slope):
    weights = [(1 << 20) // math.isqrt(standing ** slope) + 1 for standing in range(1, number_of + 1)]
    spread = 1 + sum(weights) // (1 << 30)
    return np.cumsum(np.array([max(1, weight // spread) for weight in weights]))


def skewed_ids(rng, extent, number_of, lean):
    listing = cumulative_ranks(number_of, lean)
    pick = jax.random.randint(jax.random.fold_in(rng, 1), extent, 0, int(listing[number_of - 1]))
    rank = jnp.searchsorted(jnp.asarray(listing, jnp.int32), pick, side="right")
    return jax.random.permutation(jax.random.fold_in(rng, 2), number_of)[rank].astype(jnp.int32)


def split_up(count, total, most, lean):
    weights = [(1 << 20) // math.isqrt(rank ** lean) + 1 for rank in range(2, count + 1)]
    surplus, counts = total - most - (count - 1), [1] * (count - 1)
    while surplus > 0:
        candidates = [i for i in range(count - 1) if counts[i] < most]
        whole, left = sum([weights[i] for i in candidates]), surplus
        for i in candidates:
            addition = min(most - counts[i], max(1, left * weights[i] // whole), surplus)
            counts[i] = counts[i] + addition
            surplus = surplus - addition
    return np.array([most] + counts)


def ragged(own_key, count, total, bound, skew):
    if count == 2:
        one = jax.random.randint(own_key, (), max(1, total - bound), min(bound, total - 1) + 1)
        return jnp.stack([one, total - one])
    sizes = jnp.asarray(split_up(count, total, bound, skew), jnp.int32)
    pairs = (count - 1) // 2
    giver, taker = sizes[1:1 + 2 * pairs:2], sizes[2:2 + 2 * pairs:2]
    margin = jnp.minimum(giver - 1, bound - taker)
    passed = jax.random.randint(jax.random.fold_in(own_key, 1), (pairs,), 0, 1 << 20) % (margin + 1)
    sizes = sizes.at[1:1 + 2 * pairs:2].set(giver - passed).at[2:2 + 2 * pairs:2].set(taker + passed)
    return sizes[jax.random.permutation(jax.random.fold_in(own_key, 2), count)]


def gaussian(stream_key, shape, scale, bound, shards=(), held_as=jnp.bfloat16):
    level = block_levels(stream_key, shape, shards, -0.22, 0.18) if shards else 1.0
    drawn = jax.random.normal(stream_key, shape, jnp.float32) * scale * level
    return jnp.minimum(jnp.maximum(drawn, -bound), bound).astype(held_as)


def setup_inputs(seed: int = 0) -> dict:
    key_list = jax.random.split(jax.random.key(seed), 23)
    return {
        "tokens": gaussian(key_list[0], (ROWS, SEQ, D), 1.0, 6.0, ((0, 16),)),
        "cotangent": gaussian(key_list[1], (ROWS, SEQ, D), 1.0, 6.0, ((0, 16),)),
        "domains": place_ends(skewed_ids(key_list[2], (ROWS,), GROUPS, 2), jax.random.fold_in(key_list[2], 3), 0, GROUPS - 1).astype(jnp.int32),
        "doc_ids": jax.vmap(lambda own: jnp.searchsorted(jnp.cumsum(ragged(own, 4, SEQ, SEQ // 2, 0)), jnp.arange(SEQ), side="right"))(jax.random.split(key_list[3], ROWS)).reshape((ROWS, SEQ)).astype(jnp.int32),
        "norm_gain": jnp.clip(1.0 + 0.1 * jax.random.normal(key_list[4], (D,), jnp.float32), 0.5, 1.5),
        "w_query": gaussian(key_list[5], (D, D), D ** -0.5, 0.1875, ((0, 16), (1, 2))),
        "w_outgate": gaussian(key_list[6], (D, D), D ** -0.5, 0.1875, ((0, 16), (1, 2))),
        "w_key": gaussian(key_list[7], (NH, D, D), D ** -0.5, 0.1875, ((0, 2), (1, 16))),
        "w_value": gaussian(key_list[8], (NH, D, D), D ** -0.5, 0.1875, ((0, 2), (1, 16))),
        "w_beta": gaussian(key_list[9], (NH, D, HEADS), D ** -0.5, 0.1875, ((0, 2), (1, 16))),
        "w_alpha": gaussian(key_list[10], (D, HEADS), D ** -0.5, 0.1875, ((0, 16), (1, 2))),
        "decay_log": jnp.clip(-4.0 + 4.5 * jax.random.uniform(key_list[11], (HEADS,), jnp.float32) ** block_levels(key_list[11], (HEADS,), ((0, 2),), -0.2, 0.2), -4.0, 0.5),
        "decay_bias": jnp.clip(-4.0 + 3.0 * jax.random.uniform(key_list[12], (HEADS,), jnp.float32) ** block_levels(key_list[12], (HEADS,), ((0, 2),), -0.2, 0.2), -4.0, -1.0),
        "conv_query": jnp.clip(jax.random.uniform(key_list[13], (KW, D), jnp.float32, -0.6, 0.6) * block_levels(key_list[13], (KW, D), ((1, 2),), -0.4, 0.0), -0.6, 0.6),
        "conv_key": jnp.clip(jax.random.uniform(key_list[14], (NH, KW, D), jnp.float32, -0.6, 0.6) * block_levels(key_list[14], (NH, KW, D), ((0, 2),), -0.4, 0.0), -0.6, 0.6),
        "conv_value": jnp.clip(jax.random.uniform(key_list[15], (NH, KW, D), jnp.float32, -0.6, 0.6) * block_levels(key_list[15], (NH, KW, D), ((0, 2),), -0.4, 0.0), -0.6, 0.6),
        "mix_gain": jnp.clip(1.0 + 0.1 * jax.random.normal(key_list[16], (DK,), jnp.float32), 0.5, 1.5),
        "w_out": gaussian(key_list[17], (D, D), (D // 2) ** -0.5, 0.25, ((0, 2), (1, 16))),
        "ffn_gain": jnp.clip(1.0 + 0.1 * jax.random.normal(key_list[18], (D,), jnp.float32), 0.5, 1.5),
        "w_gate": gaussian(key_list[19], (D, FF), D ** -0.5, 0.1875, ((0, 16), (1, 2))),
        "w_up": gaussian(key_list[20], (D, FF), D ** -0.5, 0.1875, ((0, 16), (1, 2))),
        "w_down": gaussian(key_list[21], (FF, D), (FF // 2) ** -0.5, 0.15625, ((0, 2), (1, 16))),
    }


PRECISE = lax.Precision.HIGHEST

@jax.custom_vjp
def low(v):
    return lax.optimization_barrier(v.astype(jnp.bfloat16)).astype(jnp.float32)

@jax.custom_vjp
def low_back(v):
    return v

def low_keep(v):
    return (low(v), None)

def low_pass(kept, grad):
    return (grad,)

def back_keep(v):
    return (v, None)

def back_low(kept, grad):
    return (low(grad),)
low.defvjp(low_keep, low_pass)
low_back.defvjp(back_keep, back_low)

def matmul(first, second):
    return jnp.dot(first, second, precision=PRECISE)

def rms_scale(values, scales):
    return values * lax.rsqrt(lax.optimization_barrier(jnp.mean(values * values, axis=-1, keepdims=True)) + 1e-06) * scales

def unit_rows(values):
    return values * lax.rsqrt(lax.optimization_barrier(jnp.sum(values * values, axis=-1, keepdims=True)) + 1e-06)

def short_conv(signal, kernel, doc_ids):
    seq_len = signal.shape[0]
    summed = signal * kernel[0]
    for offset in range(1, kernel.shape[0]):
        shifted = jnp.pad(signal, ((offset, 0), (0, 0)))[:seq_len]
        shifted_docs = jnp.pad(doc_ids, (offset, 0), constant_values=-1)[:seq_len]
        same_doc = (shifted_docs == doc_ids).astype(jnp.float32)[:, None]
        summed = summed + shifted * same_doc * kernel[offset]
    return summed

def block_pass(memory, pieces):
    query_block, key_block, value_block, beta_block, decay_block, doc_block, prior_doc = pieces
    block_len = key_block.shape[0]
    cumulative = jnp.cumsum(decay_block)
    row_pos = lax.broadcasted_iota(jnp.int32, (block_len, block_len), 0)
    col_pos = lax.broadcasted_iota(jnp.int32, (block_len, block_len), 1)
    inside = (row_pos >= col_pos) & (doc_block[:, None] == doc_block[None, :])
    decay_mat = jnp.where(inside, jnp.exp(jnp.where(inside, cumulative[:, None] - cumulative[None, :], 0.0)), 0.0)
    carried = jnp.where(doc_block == prior_doc, jnp.exp(cumulative), 0.0)
    strict = jnp.where(row_pos > col_pos, decay_mat * matmul(key_block, key_block.T), 0.0)
    system = jnp.eye(block_len, dtype=jnp.float32) + beta_block[:, None] * strict
    target = beta_block[:, None] * (value_block - carried[:, None] * matmul(key_block, memory))
    pseudo = jax.scipy.linalg.solve_triangular(system, target, lower=True, unit_diagonal=True)
    query_decay = decay_mat[1::2]
    query_carry = carried[1::2]
    result = query_carry[:, None] * matmul(query_block, memory) + matmul(query_decay * matmul(query_block, key_block.T), pseudo)
    updated = carried[-1] * memory + matmul(key_block.T, decay_mat[-1][:, None] * pseudo)
    return (updated, result)

def head_sequence(queries, keys, values, betas, decays, doc_ids):
    seq_len = queries.shape[0]
    blocks = seq_len // STRETCH
    span_len = 2 * STRETCH
    key_line = jnp.transpose(keys, (1, 0, 2)).reshape(blocks, span_len, keys.shape[-1])
    value_line = jnp.transpose(values, (1, 0, 2)).reshape(blocks, span_len, values.shape[-1])
    beta_line = jnp.transpose(betas).reshape(blocks, span_len)
    decay_line = jnp.stack([decays, jnp.zeros_like(decays)], axis=1).reshape(blocks, span_len)
    doc_line = jnp.repeat(doc_ids, 2).reshape(blocks, span_len)
    prior_docs = jnp.concatenate([jnp.full((1,), -1, doc_ids.dtype), doc_line[:-1, -1]])
    initial = jnp.zeros((keys.shape[-1], values.shape[-1]), queries.dtype)
    last_state, outputs = lax.scan(jax.checkpoint(block_pass), initial, (queries.reshape(blocks, STRETCH, -1), key_line, value_line, beta_line, decay_line, doc_line, prior_docs))
    return outputs.reshape(seq_len, -1)

def gated_norm(mixed, gate_pre, mix_gain):
    seq_len = mixed.shape[0]
    gates = jax.nn.silu(gate_pre.reshape(mixed.shape))
    scaled = mixed * lax.rsqrt(lax.optimization_barrier(jnp.mean(mixed * mixed, axis=-1, keepdims=True)) + 1e-05)
    return (scaled * mix_gain * gates).reshape(seq_len, -1)

def query_inputs(query_pre, conv_query, doc_ids):
    seq_len = query_pre.shape[0]
    activated = jax.nn.silu(short_conv(query_pre, conv_query, doc_ids))
    return unit_rows(activated.reshape(seq_len, -1, DK)) * DK ** (-0.5)

def step_inputs(key_pre, value_pre, conv_key, conv_value, doc_ids):
    seq_len = key_pre.shape[0]
    activated = jax.nn.silu(short_conv(key_pre, conv_key, doc_ids))
    keys = unit_rows(activated.reshape(seq_len, -1, DK)).reshape(seq_len, -1)
    values = jax.nn.silu(short_conv(value_pre, conv_value, doc_ids))
    return (keys, values)

def decay_rates(alpha_pre, decay_log, decay_bias):
    return -jnp.exp(decay_log) * jax.nn.softplus(alpha_pre + decay_bias)

def block_forward(inputs, doc_ids, norm_gain, w_query, w_outgate, w_key, w_value, w_beta, w_alpha, decay_log, decay_bias, conv_query, conv_key, conv_value, mix_gain, w_out, ffn_gain, w_gate, w_up, w_down):
    seq_len = inputs.shape[0]
    normed = low(rms_scale(inputs, norm_gain))
    query_pre = low_back(matmul(normed, w_query))
    gate_pre = low_back(matmul(normed, w_outgate))
    alpha_pre = low_back(matmul(normed, w_alpha))
    key_pre = low_back(jnp.einsum('ld,sde->sle', normed, w_key, precision=PRECISE))
    value_pre = low_back(jnp.einsum('ld,sde->sle', normed, w_value, precision=PRECISE))
    beta_pre = low_back(jnp.einsum('ld,sdh->slh', normed, w_beta, precision=PRECISE))
    queries = query_inputs(query_pre, conv_query, doc_ids)
    keys, values = jax.vmap(step_inputs, in_axes=(0, 0, 0, 0, None))(key_pre, value_pre, conv_key, conv_value, doc_ids)
    step_count = keys.shape[0]
    keys = low_back(low(keys)).reshape(step_count, seq_len, -1, DK)
    values = low_back(low(values)).reshape(step_count, seq_len, -1, DK)
    betas = low_back(low(2.0 * jax.nn.sigmoid(beta_pre)))
    decays = decay_rates(alpha_pre, decay_log, decay_bias)

    def one_head(query_head, key_head, value_head, beta_head, decay_head):
        return head_sequence(query_head, key_head, value_head, beta_head, decay_head, doc_ids)
    mixed = jax.vmap(one_head, in_axes=(1, 2, 2, 2, 1), out_axes=1)(queries, keys, values, betas, decays)
    gated = low(gated_norm(mixed, gate_pre, mix_gain))
    attention = low_back(matmul(gated, w_out))
    middle = inputs + attention
    normed_ffn = low(rms_scale(middle, ffn_gain))
    gate_in = low_back(matmul(normed_ffn, w_gate))
    up_in = low_back(matmul(normed_ffn, w_up))
    hidden = low(jax.nn.silu(gate_in) * up_in)
    return middle + low_back(matmul(hidden, w_down))

def reference(tokens, cotangent, domains, doc_ids, norm_gain, w_query, w_outgate, w_key, w_value, w_beta, w_alpha, decay_log, decay_bias, conv_query, conv_key, conv_value, mix_gain, w_out, ffn_gain, w_gate, w_up, w_down):
    params = tuple((param.astype(jnp.float32) for param in (norm_gain, w_query, w_outgate, w_key, w_value, w_beta, w_alpha, decay_log, decay_bias, conv_query, conv_key, conv_value, mix_gain, w_out, ffn_gain, w_gate, w_up, w_down)))
    group_ids = lax.broadcasted_iota(jnp.int32, (ROWS, GROUPS), 1)
    member = (domains[:, None] == group_ids).astype(jnp.float32)
    group_sizes = lax.optimization_barrier(jnp.sum(member, axis=0))
    row_sizes = lax.optimization_barrier(jnp.sum(member * group_sizes[None, :], axis=1))
    row_weights = 2.0 / (1.0 + row_sizes * (GROUPS / ROWS))

    def one_row(totals, pieces):
        row_tokens, row_cot, row_weight, row_docs = pieces

        def forward(row_in, *weights):
            return block_forward(row_in, row_docs, *weights)
        result, pullback = jax.vjp(forward, row_tokens.astype(jnp.float32), *params)
        grads = pullback(row_cot.astype(jnp.float32) * row_weight)
        totals = tuple((running + extra for running, extra in zip(totals, grads[1:])))
        return (totals, (result.astype(jnp.bfloat16), grads[0].astype(jnp.bfloat16)))
    zeros = tuple((jnp.zeros_like(param) for param in params))
    totals, (outputs, input_grads) = lax.scan(one_row, zeros, (tokens, cotangent, row_weights, doc_ids))
    return (outputs, input_grads, totals[0], totals[1], totals[2], totals[3], totals[4], totals[5], totals[6], totals[7], totals[8], totals[9], totals[10], totals[11], totals[12], totals[13], totals[14], totals[15], totals[16], totals[17])
```

```python
import functools

import jax
import jax.numpy as jnp
from jax import lax
from jax.experimental import pallas as pl
from jax.experimental.pallas import tpu as pltpu
from jax.sharding import PartitionSpec as P

STRETCH = 64
DK = 128
F32 = jnp.float32
BF = jnp.bfloat16
NN = ((1,), (0,))
NT = ((1,), (1,))
TN = ((0,), (0,))


def split(a):
    if a.dtype == BF:
        return (a,)
    hi = a.astype(BF)
    return (hi, (a - hi.astype(F32)).astype(BF))


def dot1(a, b, dims=NN):
    return lax.dot_general(a.astype(BF), b.astype(BF), (dims, ((), ())), preferred_element_type=F32)


def dot3(a, b, dims=NN):
    a = a if isinstance(a, tuple) else split(a)
    b = b if isinstance(b, tuple) else split(b)
    one = lambda x, y: lax.dot_general(x, y, (dims, ((), ())), preferred_element_type=F32)
    out = one(a[0], b[0])
    if len(a) > 1:
        out = out + one(a[1], b[0])
    if len(b) > 1:
        out = out + one(a[0], b[1])
    return out


def dot6(a, b, dims=NN):
    return lax.dot_general(
        a, b, (dims, ((), ())), precision=lax.Precision.HIGHEST, preferred_element_type=F32
    )


def iota(shape, dim):
    return lax.broadcasted_iota(jnp.int32, shape, dim)


def block_masks():
    span = 2 * STRETCH
    row, col = iota((span, span), 0), iota((span, span), 1)
    t_row, t_col = row % STRETCH, col % STRETCH
    p_row, p_col = 2 * t_row + row // STRETCH, 2 * t_col + col // STRETCH
    return t_row, t_col, p_row, p_col


def twice(block):
    return jnp.concatenate([block, block], axis=0)


def block_scalars(aux):
    low = (iota((STRETCH, STRETCH), 0) >= iota((STRETCH, STRETCH), 1)).astype(F32)
    running = dot6(low, aux)
    aux2, run2 = twice(aux), twice(running)
    return aux2, run2, aux2.T, run2.T


def head_terms(aux, aux2, run2, aux_t, run_t, head, heads):
    beta = jnp.concatenate(
        [aux[:, head : head + 1], aux[:, heads + head : heads + head + 1]], axis=0
    )
    lane = 2 * heads + head
    run_col = run2[:, lane : lane + 1]
    run_row = run_t[lane : lane + 1, :]
    doc_lane = 3 * heads
    doc_col = aux2[:, doc_lane : doc_lane + 1]
    doc_row = aux_t[doc_lane : doc_lane + 1, :]
    fresh = aux2[:, doc_lane + 1 : doc_lane + 2]
    span = 2 * STRETCH
    carried = jnp.where(fresh > 0.5, jnp.exp(run_col), 0.0)
    last_run = run_col[span - 1 : span, :]
    to_last = jnp.where(doc_col == doc_col[span - 1 : span, :], jnp.exp(last_run - run_col), 0.0)
    return beta, run_col, run_row, doc_col, doc_row, carried, to_last


def decay_matrix(run_col, run_row, doc_col, doc_row, p_row, p_col):
    inside = (p_row >= p_col) & (doc_col == doc_row)
    return jnp.where(inside, jnp.exp(jnp.where(inside, run_col - run_row, 0.0)), 0.0)


def inverse(mats, masks):
    t_row, t_col, p_row, p_col = masks
    eye = (p_row == p_col).astype(F32)
    pair = (t_row == t_col) & (p_row > p_col)
    out = [eye - jnp.where(pair, a, 0.0) for a in mats]
    level = 1
    while (1 << level) <= STRETCH:
        merge = (
            ((t_row >> level) == (t_col >> level))
            & (((t_row >> (level - 1)) & 1) == 1)
            & (((t_col >> (level - 1)) & 1) == 0)
        )
        low = [x.astype(BF) for x in out]
        half = [dot1(x, jnp.where(merge, a, 0.0)) for x, a in zip(low, mats)]
        out = [o - dot1(h, x) for o, h, x in zip(out, half, low)]
        level += 1
    rest = [eye - x - dot3(a, x) for a, x in zip(mats, out)]
    return [x + dot1(x, r) for x, r in zip(out, rest)]


def mixer_fwd_kernel(heads, q_ref, k_ref, v_ref, aux_ref, gate_ref, gain_ref,
                     gated_ref, mixed_ref, inv_ref, state_ref, pseudo_ref, attn_ref):
    blocks = q_ref.shape[0] // STRETCH
    span = 2 * STRETCH
    masks = block_masks()
    t_row, t_col, p_row, p_col = masks

    def keys_of(rows, cols):
        return jnp.concatenate([k_ref[0, rows, cols], k_ref[1, rows, cols]], axis=0)

    def prepare(block, carry):
        rows = pl.ds(pl.multiple_of(block * STRETCH, STRETCH), STRETCH)
        aux = aux_ref[rows, :]
        aux2, run2, aux_t, run_t = block_scalars(aux)
        mats = []
        for head in range(heads):
            cols = slice(head * DK, (head + 1) * DK)
            beta, run_col, run_row, doc_col, doc_row, carried, to_last = head_terms(
                aux, aux2, run2, aux_t, run_t, head, heads
            )
            decay = decay_matrix(run_col, run_row, doc_col, doc_row, p_row, p_col)
            keys = keys_of(rows, cols)
            gram = dot1(keys, keys, NT)
            mats.append(beta * jnp.where(p_row > p_col, decay * gram, 0.0))
            attn_ref[block * heads + head] = decay[STRETCH:] * dot3(q_ref[rows, cols], keys, NT)
        for head, inv in enumerate(inverse(mats, masks)):
            inv_ref[block * heads + head] = inv
        return carry

    lax.fori_loop(0, blocks, prepare, 0)
    for head in range(heads):
        state_ref[head] = jnp.zeros((DK, DK), F32)

    def advance(block, carry):
        rows = pl.ds(pl.multiple_of(block * STRETCH, STRETCH), STRETCH)
        aux = aux_ref[rows, :]
        aux2, run2, aux_t, run_t = block_scalars(aux)
        for head in range(heads):
            cols = slice(head * DK, (head + 1) * DK)
            beta, run_col, run_row, doc_col, doc_row, carried, to_last = head_terms(
                aux, aux2, run2, aux_t, run_t, head, heads
            )
            keys = keys_of(rows, cols)
            values = jnp.concatenate([v_ref[0, rows, cols], v_ref[1, rows, cols]], axis=0).astype(F32)
            state = state_ref[block * heads + head]
            state_parts = split(state)
            target = beta * (values - carried * dot3(keys, state_parts))
            pseudo = dot3(inv_ref[block * heads + head], target)
            pseudo_ref[block * heads + head] = pseudo
            mixed = carried[STRETCH:] * dot3(q_ref[rows, cols], state_parts) + dot3(
                attn_ref[block * heads + head], pseudo
            )
            state_ref[(block + 1) * heads + head] = carried[span - 1 : span] * state + dot3(
                keys, to_last * pseudo, TN
            )
            mixed_ref[rows, cols] = mixed
            scale = lax.rsqrt(jnp.mean(mixed * mixed, axis=-1, keepdims=True) + 1e-05)
            gate = gate_ref[rows, cols]
            gated_ref[rows, cols] = (mixed * scale * gain_ref[...] * (gate * jax.nn.sigmoid(gate))).astype(BF)
        return carry

    lax.fori_loop(0, blocks, advance, 0)


def mixer_bwd_kernel(heads, q_ref, k_ref, v_ref, aux_ref, gate_ref, gain_ref, mixed_ref, inv_ref,
                     state_ref, pseudo_ref, dgated_ref,
                     dq_ref, dk_ref, dv_ref, daux_ref, dgate_ref, dgain_ref, dstate):
    blocks = q_ref.shape[0] // STRETCH
    span = 2 * STRETCH
    masks = block_masks()
    t_row, t_col, p_row, p_col = masks
    for head in range(heads):
        dstate[head] = jnp.zeros((DK, DK), F32)
    dgain_ref[...] = jnp.zeros_like(dgain_ref)
    upper = (iota((STRETCH, STRETCH), 0) <= iota((STRETCH, STRETCH), 1)).astype(F32)
    lanes = iota((STRETCH, DK), 1)
    wide_lanes = iota((span, DK), 1)
    wide_rows = iota((span, DK), 0)

    def back(step, carry):
        block = blocks - 1 - step
        rows = pl.ds(pl.multiple_of(block * STRETCH, STRETCH), STRETCH)
        aux = aux_ref[rows, :]
        aux2, run2, aux_t, run_t = block_scalars(aux)
        dbeta_all = jnp.zeros((STRETCH, DK), F32)
        drun_all = jnp.zeros((STRETCH, DK), F32)
        column_sums = jnp.zeros((span, DK), F32)
        for head in range(heads):
            cols = slice(head * DK, (head + 1) * DK)
            beta, run_col, run_row, doc_col, doc_row, carried, to_last = head_terms(
                aux, aux2, run2, aux_t, run_t, head, heads
            )
            decay = decay_matrix(run_col, run_row, doc_col, doc_row, p_row, p_col)
            keys = keys = jnp.concatenate([k_ref[0, rows, cols], k_ref[1, rows, cols]], axis=0)
            queries = q_ref[rows, cols]
            mixed = mixed_ref[rows, cols]
            gate = gate_ref[rows, cols]
            sigmoid = jax.nn.sigmoid(gate)
            silu = gate * sigmoid
            scale = lax.rsqrt(jnp.mean(mixed * mixed, axis=-1, keepdims=True) + 1e-05)
            scaled = mixed * scale
            dgated = dgated_ref[rows, cols]
            part = dgated * scaled
            dgate_ref[rows, cols] = (
                part * gain_ref[...] * (sigmoid * (1.0 + gate * (1.0 - sigmoid)))
            ).astype(BF)
            dgain_ref[...] += jnp.sum(part * silu, axis=0, keepdims=True)
            dscaled = dgated * gain_ref[...] * silu
            dout = scale * (dscaled - scaled * jnp.mean(dscaled * scaled, axis=-1, keepdims=True))

            index = block * heads + head
            state, pseudo = state_ref[index], pseudo_ref[index]
            dnext = dstate[head]
            dnext_parts, state_parts, pseudo_parts = split(dnext), split(state), split(pseudo)
            dout_parts, q_parts = split(dout), split(queries)
            gram = dot1(keys, keys, NT)
            strict = p_row > p_col
            core = jnp.where(strict, decay * gram, 0.0)
            amat = beta * core
            qdecay = decay[STRETCH:]
            attn = qdecay * dot3(q_parts, keys, NT)
            dattn = dot3(dout_parts, pseudo_parts, NT)
            dqk = split(qdecay * dattn)
            dpseudo = dot3(attn, dout_parts, TN) + to_last * dot3(keys, dnext_parts)
            dtarget = dot3(inv_ref[index], dpseudo, TN)
            dtarget_parts = split(dtarget)
            damat = jnp.where(strict, -dot3(dtarget_parts, pseudo_parts, NT), 0.0)
            e_a, e_m = damat * amat, dattn * attn
            dgram = split(beta * decay * damat)
            dbeta = jnp.sum(dtarget * pseudo, axis=-1, keepdims=True) / jnp.maximum(beta, 1e-30)
            dvalues = beta * dtarget
            dread = -(beta * carried) * dtarget
            dout_c = carried[STRETCH:] * dout
            dread_parts, dout_c_parts = split(dread), split(dout_c)
            last = carried[span - 1 : span]
            dstate[head] = last * dnext + dot3(keys, dread_parts, TN) + dot3(q_parts, dout_c_parts, TN)
            dq_state = dot3(dout_c_parts, state_parts, NT)
            dk_state = dot3(dread_parts, state_parts, NT)
            dk_last = dot3(to_last * pseudo, dnext_parts, NT)
            dq_ref[rows, cols] = dq_state + dot3(dqk, keys)
            dkeys = (
                dk_state + dk_last + dot3(dgram, keys) + dot3(dgram, keys, TN) + dot3(dqk, q_parts, TN)
            )
            dk_ref[0, rows, cols] = dkeys[:STRETCH].astype(BF)
            dk_ref[1, rows, cols] = dkeys[STRETCH:].astype(BF)
            dv_ref[0, rows, cols] = dvalues[:STRETCH].astype(BF)
            dv_ref[1, rows, cols] = dvalues[STRETCH:].astype(BF)

            wide = keys.astype(F32)
            e_last = jnp.sum(wide * dk_last, axis=-1, keepdims=True)
            drun = jnp.sum(e_a, axis=-1, keepdims=True) - e_last + jnp.sum(wide * dk_state, axis=-1, keepdims=True)
            drun_q = jnp.sum(e_m, axis=-1, keepdims=True) + jnp.sum(queries * dq_state, axis=-1, keepdims=True)
            at_last = jnp.sum(e_last, axis=0, keepdims=True) + last * jnp.sum(
                jnp.sum(dnext * state, axis=-1, keepdims=True), axis=0, keepdims=True
            )
            drun = drun[:STRETCH] + drun[STRETCH:] + drun_q
            drun = drun + jnp.where(iota((STRETCH, 1), 0) == STRETCH - 1, at_last, 0.0)
            lane = 2 * heads + head
            drun_all = jnp.where(lanes == lane, drun, drun_all)
            dbeta_all = jnp.where(lanes == head, dbeta[:STRETCH], dbeta_all)
            dbeta_all = jnp.where(lanes == heads + head, dbeta[STRETCH:], dbeta_all)
            sums = jnp.sum(e_a, axis=0, keepdims=True) + jnp.sum(e_m, axis=0, keepdims=True)
            column_sums = jnp.where(wide_rows == lane, sums, column_sums)
        down = column_sums.T
        drun_all = drun_all - down[:STRETCH] - down[STRETCH:]
        daux_ref[rows, :] = jnp.where(lanes < 2 * heads, dbeta_all, dot6(upper, drun_all))
        return carry

    lax.fori_loop(0, blocks, back, 0)


VMEM = pl.BlockSpec(memory_space=pltpu.VMEM)


def mixer_fwd(q, k, v, aux, gate, gain):
    seq, width = q.shape
    heads, blocks = width // DK, seq // STRETCH
    units = heads * blocks
    span = 2 * STRETCH
    shape = jax.ShapeDtypeStruct
    return pl.pallas_call(
        functools.partial(mixer_fwd_kernel, heads),
        out_shape=(
            shape((seq, width), BF),
            shape((seq, width), F32),
            shape((units, span, span), F32),
            shape((units + heads, DK, DK), F32),
            shape((units, span, DK), F32),
        ),
        in_specs=[VMEM] * 6,
        out_specs=(VMEM,) * 5,
        scratch_shapes=[pltpu.VMEM((units, STRETCH, span), F32)],
        compiler_params=pltpu.CompilerParams(vmem_limit_bytes=48 << 20),
        name="mixer_forward",
    )(q, k, v, aux, gate, gain)


def mixer_bwd(q, k, v, aux, gate, gain, mixed, inv, state, pseudo, dgated):
    seq, width = q.shape
    heads = width // DK
    shape = jax.ShapeDtypeStruct
    return pl.pallas_call(
        functools.partial(mixer_bwd_kernel, heads),
        out_shape=(
            shape((seq, width), F32),
            shape(k.shape, BF),
            shape(v.shape, BF),
            shape((seq, DK), F32),
            shape((seq, width), BF),
            shape((1, DK), F32),
        ),
        in_specs=[VMEM] * 11,
        out_specs=(VMEM,) * 6,
        scratch_shapes=[pltpu.VMEM((heads, DK, DK), F32)],
        compiler_params=pltpu.CompilerParams(vmem_limit_bytes=48 << 20),
        name="mixer_backward",
    )(q, k, v, aux, gate, gain, mixed, inv, state, pseudo, dgated)


GROUPS = 8


def product(first, second, dims=NN):
    return lax.dot_general(first, second, (dims, ((), ())), preferred_element_type=F32)


def rms_scale(values, scales):
    return values * lax.rsqrt(jnp.mean(values * values, axis=-1, keepdims=True) + 1e-06) * scales


def unit_rows(values):
    return values * lax.rsqrt(jnp.sum(values * values, axis=-1, keepdims=True) + 1e-06)


def silu_grad(values):
    sigmoid = jax.nn.sigmoid(values)
    return sigmoid * (1.0 + values * (1.0 - sigmoid))


def short_conv(signal, kernel, doc_ids):
    seq_len = signal.shape[0]
    summed = signal * kernel[0]
    for offset in range(1, kernel.shape[0]):
        shifted = jnp.pad(signal, ((offset, 0), (0, 0)))[:seq_len]
        shifted_docs = jnp.pad(doc_ids, (offset, 0), constant_values=-1)[:seq_len]
        same_doc = (shifted_docs == doc_ids).astype(F32)[:, None]
        summed = summed + shifted * same_doc * kernel[offset]
    return summed


def unit_heads(values):
    seq_len = values.shape[0]
    return unit_rows(values.reshape(seq_len, -1, DK)).reshape(seq_len, -1)


def per_device(
    tokens,
    cotangent,
    domains,
    doc_ids,
    norm_gain,
    w_query,
    w_outgate,
    w_key,
    w_value,
    w_beta,
    w_alpha,
    decay_log,
    decay_bias,
    conv_query,
    conv_key,
    conv_value,
    mix_gain,
    w_out,
    ffn_gain,
    w_gate,
    w_up,
    w_down,
):
    row_total = domains.shape[0]
    group_ids = lax.broadcasted_iota(jnp.int32, (row_total, GROUPS), 1)
    member = (domains[:, None] == group_ids).astype(F32)
    group_sizes = jnp.sum(member, axis=0)
    row_sizes = jnp.sum(member * group_sizes[None, :], axis=1)
    row_weights = 2.0 / (1.0 + row_sizes * (GROUPS / row_total))
    own_row = (lax.broadcasted_iota(jnp.int32, (row_total,), 0) == lax.axis_index("dp")).astype(F32)
    weight_here = jnp.sum(own_row * row_weights)

    depth = w_query.shape[0]
    half = w_query.shape[1]
    heads = w_alpha.shape[1]
    side = lax.axis_index("step")

    def by_step(own, other):
        first = side == 0
        return [jnp.where(first, own, other), jnp.where(first, other, own)]

    def swap(array):
        return lax.ppermute(array, "step", [(0, 1), (1, 0)])

    def parts_for(array, width):
        return (
            lax.dynamic_slice_in_dim(array, side * width, width, 1),
            lax.dynamic_slice_in_dim(array, (1 - side) * width, width, 1),
        )

    key_mine, key_theirs = parts_for(w_key[0], half)
    value_mine, value_theirs = parts_for(w_value[0], half)
    beta_mine, beta_theirs = parts_for(w_beta[0], heads)
    got = swap(jnp.concatenate([key_theirs, value_theirs, beta_theirs], axis=1))
    conv_k_mine, conv_k_theirs = parts_for(conv_key[0], half)
    conv_v_mine, conv_v_theirs = parts_for(conv_value[0], half)
    got_conv = swap(jnp.concatenate([conv_k_theirs, conv_v_theirs], axis=1))
    keys_w = by_step(key_mine, got[:, :half])
    values_w = by_step(value_mine, got[:, half : 2 * half])
    betas_w = by_step(beta_mine, got[:, 2 * half :])
    kernels_k = by_step(conv_k_mine, got_conv[:, :half])
    kernels_v = by_step(conv_v_mine, got_conv[:, half:])
    pad = jnp.zeros((depth, DK - 3 * heads), BF)
    front_w = lax.all_gather(
        jnp.concatenate([w_query, w_outgate] + keys_w + values_w + betas_w + [w_alpha, pad], axis=1),
        "dp", axis=0, tiled=True,
    )
    back_w = lax.all_gather(
        jnp.concatenate([w_out.T, w_gate, w_up, w_down.T], axis=1), "dp", axis=0, tiled=True
    )
    ff = w_gate.shape[1]

    inputs = tokens[0].astype(F32)
    docs = doc_ids[0]
    seq_len = inputs.shape[0]
    normed_f, pull_first = jax.vjp(rms_scale, inputs, norm_gain)
    normed = normed_f.astype(BF)
    pre = product(normed, front_w)
    gate_pre = pre[:, half : 2 * half]

    def prepare(pre_in, query_kernel, key_0, key_1, value_0, value_1, log_rates, rate_bias):
        queries = unit_heads(jax.nn.silu(short_conv(pre_in[:, :half], query_kernel, docs))) * DK ** (-0.5)
        keys = [
            unit_heads(jax.nn.silu(short_conv(pre_in[:, (2 + i) * half : (3 + i) * half], kernel, docs)))
            for i, kernel in enumerate((key_0, key_1))
        ]
        values = [
            jax.nn.silu(short_conv(pre_in[:, (4 + i) * half : (5 + i) * half], kernel, docs))
            for i, kernel in enumerate((value_0, value_1))
        ]
        scalars = pre_in[:, 6 * half :]
        betas = 2.0 * jax.nn.sigmoid(scalars[:, : 2 * heads])
        decays = -jnp.exp(log_rates) * jax.nn.softplus(scalars[:, 2 * heads : 3 * heads] + rate_bias)
        return (queries, jnp.stack(keys), jnp.stack(values), betas, decays)

    (queries, keys, values, betas, decays), pull_prepare = jax.vjp(
        prepare, pre, conv_query, kernels_k[0], kernels_k[1], kernels_v[0], kernels_v[1], decay_log, decay_bias
    )
    prior = jnp.concatenate([jnp.full((1,), -1, docs.dtype), docs[STRETCH - 1 : -1 : STRETCH]])
    fresh = (docs.reshape(-1, STRETCH) == prior[:, None]).reshape(seq_len, 1).astype(F32)
    aux = jnp.concatenate(
        [betas.astype(BF).astype(F32), decays, docs.astype(F32)[:, None], fresh,
         jnp.zeros((seq_len, DK - 3 * heads - 2), F32)],
        axis=1,
    )
    keys, values = keys.astype(BF), values.astype(BF)
    gain_row = mix_gain[None]
    gated, mixed, inv, state, pseudo = mixer_fwd(queries, keys, values, aux, gate_pre, gain_row)

    attention = lax.psum(product(gated, back_w[:, :half], NT).astype(BF), "step").astype(F32)
    middle = inputs + attention
    normed_ffn_f, pull_second = jax.vjp(rms_scale, middle, ffn_gain)
    normed_ffn = normed_ffn_f.astype(BF)
    gate_w, up_w, down_w = (back_w[:, half + i * ff : half + (i + 1) * ff] for i in range(3))
    gate_in = product(normed_ffn, gate_w)
    up_in = product(normed_ffn, up_w)
    hidden = (jax.nn.silu(gate_in) * up_in).astype(BF)
    ffn_out = lax.psum(product(hidden, down_w, NT).astype(BF), "step").astype(F32)
    output = (middle + ffn_out).astype(BF)[None]

    seed = cotangent[0].astype(F32) * weight_here
    seed_low = seed.astype(BF)
    grad_down = product(seed_low, hidden, TN)
    hidden_back = product(seed_low, down_w)
    gate_back = (hidden_back * up_in * silu_grad(gate_in)).astype(BF)
    up_back = (hidden_back * jax.nn.silu(gate_in)).astype(BF)
    grad_gate = product(normed_ffn, gate_back, TN)
    grad_up = product(normed_ffn, up_back, TN)
    ffn_in_back = lax.psum(
        (product(gate_back, gate_w, NT) + product(up_back, up_w, NT)).astype(BF), "step"
    ).astype(F32)
    middle_norm_back, grad_ffn_gain = pull_second(ffn_in_back)
    middle_back = seed + middle_norm_back
    attn_back = middle_back.astype(BF)
    grad_out = product(attn_back, gated, TN)
    sum_back = lax.psum_scatter(
        jnp.concatenate([grad_out, grad_gate, grad_up, grad_down], axis=1).astype(BF),
        "dp", scatter_dimension=0, tiled=True,
    ).astype(F32)
    gated_back = product(attn_back, back_w[:, :half])
    dq, dk, dv, daux, dgate, dgain = mixer_bwd(
        queries, keys, values, aux, gate_pre, gain_row, mixed, inv, state, pseudo, gated_back
    )
    dbetas = daux[:, : 2 * heads].astype(BF).astype(F32)
    ddecays = daux[:, 2 * heads : 3 * heads]
    dpre, d_cq, d_k0, d_k1, d_v0, d_v1, d_log, d_bias = pull_prepare(
        (dq, dk.astype(F32), dv.astype(F32), dbetas, ddecays)
    )
    dpre_low = jnp.concatenate([dpre[:, :half].astype(BF), dgate, dpre[:, 2 * half :].astype(BF)], axis=1)
    grad_front = product(normed, dpre_low, TN)
    normed_back = lax.psum(product(dpre_low, front_w, NT).astype(BF), "step").astype(F32)
    input_back, grad_norm_gain = pull_first(normed_back)
    input_grad = (middle_back + input_back).astype(BF)[None]
    sum_front = lax.psum_scatter(grad_front.astype(BF), "dp", scatter_dimension=0, tiled=True)

    def home(parts):
        mine = jnp.where(side == 0, parts[0], parts[1])
        other = swap(jnp.where(side == 0, parts[1], parts[0]))
        return jnp.where(
            side == 0, jnp.concatenate([mine, other], axis=1), jnp.concatenate([other, mine], axis=1)
        )

    col = lambda i: sum_front[:, i * half : (i + 1) * half]
    sum_key, sum_value = home([col(2), col(3)]), home([col(4), col(5)])
    tail = sum_front[:, 6 * half :]
    sum_beta = home([tail[:, :heads], tail[:, heads : 2 * heads]])
    small = lax.psum(
        (grad_norm_gain, d_log, d_bias, d_cq, d_k0, d_k1, d_v0, d_v1, grad_ffn_gain), "dp"
    )
    sum_norm_gain, sum_log, sum_bias, sum_cq, s_k0, s_k1, s_v0, s_v1, sum_ffn_gain = small
    sum_mix_gain = lax.psum(dgain[0], ("dp", "step"))
    f32 = lambda a: a.astype(F32)
    return (
        output,
        input_grad,
        sum_norm_gain,
        f32(col(0)),
        f32(col(1)),
        f32(sum_key)[None],
        f32(sum_value)[None],
        f32(sum_beta)[None],
        f32(tail[:, 2 * heads : 3 * heads]),
        sum_log,
        sum_bias,
        sum_cq,
        home([s_k0, s_k1])[None],
        home([s_v0, s_v1])[None],
        sum_mix_gain,
        sum_back[:, :half].T,
        sum_ffn_gain,
        sum_back[:, half : half + ff],
        sum_back[:, half + ff : half + 2 * ff],
        sum_back[:, half + 2 * ff :].T,
    )


def solution(mesh):
    return jax.shard_map(
        per_device,
        mesh=mesh,
        in_specs=(
            P("dp", None, None),
            P("dp", None, None),
            P(),
            P("dp", None),
            P(),
            P("dp", "step"),
            P("dp", "step"),
            P("step", "dp", None),
            P("step", "dp", None),
            P("step", "dp", None),
            P("dp", "step"),
            P("step"),
            P("step"),
            P(None, "step"),
            P("step", None, None),
            P("step", None, None),
            P(),
            P("step", "dp"),
            P(),
            P("dp", "step"),
            P("dp", "step"),
            P("step", "dp"),
        ),
        out_specs=(
            P("dp", None, None),
            P("dp", None, None),
            P(),
            P("dp", "step"),
            P("dp", "step"),
            P("step", "dp", None),
            P("step", "dp", None),
            P("step", "dp", None),
            P("dp", "step"),
            P("step"),
            P("step"),
            P(None, "step"),
            P("step", None, None),
            P("step", None, None),
            P(),
            P("step", "dp"),
            P(),
            P("dp", "step"),
            P("dp", "step"),
            P("step", "dp"),
        ),
        check_vma=False,
    )
```

```python
import functools

import jax
import jax.numpy as jnp
from jax import lax
from jax.experimental import pallas as pl
from jax.experimental.pallas import tpu as pltpu
from jax.sharding import PartitionSpec as P

STRETCH = 64
DK = 128
F32 = jnp.float32
BF = jnp.bfloat16
NN = ((1,), (0,))
NT = ((1,), (1,))
TN = ((0,), (0,))


def split(a):
    if a.dtype == BF:
        return (a,)
    hi = a.astype(BF)
    return (hi, (a - hi.astype(F32)).astype(BF))


def dot1(a, b, dims=NN):
    return lax.dot_general(a.astype(BF), b.astype(BF), (dims, ((), ())), preferred_element_type=F32)


def dot3(a, b, dims=NN):
    a = a if isinstance(a, tuple) else split(a)
    b = b if isinstance(b, tuple) else split(b)
    one = lambda x, y: lax.dot_general(x, y, (dims, ((), ())), preferred_element_type=F32)
    out = one(a[0], b[0])
    if len(a) > 1:
        out = out + one(a[1], b[0])
    if len(b) > 1:
        out = out + one(a[0], b[1])
    return out


def dot6(a, b, dims=NN):
    return lax.dot_general(
        a, b, (dims, ((), ())), precision=lax.Precision.HIGHEST, preferred_element_type=F32
    )


def iota(shape, dim):
    return lax.broadcasted_iota(jnp.int32, shape, dim)


def block_masks():
    span = 2 * STRETCH
    row, col = iota((span, span), 0), iota((span, span), 1)
    t_row, t_col = row % STRETCH, col % STRETCH
    p_row, p_col = 2 * t_row + row // STRETCH, 2 * t_col + col // STRETCH
    return t_row, t_col, p_row, p_col


def twice(block):
    return jnp.concatenate([block, block], axis=0)


def block_scalars(aux):
    low = (iota((STRETCH, STRETCH), 0) >= iota((STRETCH, STRETCH), 1)).astype(F32)
    running = dot6(low, aux)
    aux2, run2 = twice(aux), twice(running)
    return aux2, run2, aux2.T, run2.T


def head_terms(aux, aux2, run2, aux_t, run_t, head, heads):
    beta = jnp.concatenate(
        [aux[:, head : head + 1], aux[:, heads + head : heads + head + 1]], axis=0
    )
    lane = 2 * heads + head
    run_col = run2[:, lane : lane + 1]
    run_row = run_t[lane : lane + 1, :]
    doc_lane = 3 * heads
    doc_col = aux2[:, doc_lane : doc_lane + 1]
    doc_row = aux_t[doc_lane : doc_lane + 1, :]
    fresh = aux2[:, doc_lane + 1 : doc_lane + 2]
    span = 2 * STRETCH
    carried = jnp.where(fresh > 0.5, jnp.exp(run_col), 0.0)
    last_run = run_col[span - 1 : span, :]
    to_last = jnp.where(doc_col == doc_col[span - 1 : span, :], jnp.exp(last_run - run_col), 0.0)
    return beta, run_col, run_row, doc_col, doc_row, carried, to_last


def decay_matrix(run_col, run_row, doc_col, doc_row, p_row, p_col):
    inside = (p_row >= p_col) & (doc_col == doc_row)
    return jnp.where(inside, jnp.exp(jnp.where(inside, run_col - run_row, 0.0)), 0.0)


def inverse(mats, masks):
    t_row, t_col, p_row, p_col = masks
    eye = (p_row == p_col).astype(F32)
    pair = (t_row == t_col) & (p_row > p_col)
    out = [eye - jnp.where(pair, a, 0.0) for a in mats]
    level = 1
    while (1 << level) <= STRETCH:
        merge = (
            ((t_row >> level) == (t_col >> level))
            & (((t_row >> (level - 1)) & 1) == 1)
            & (((t_col >> (level - 1)) & 1) == 0)
        )
        low = [x.astype(BF) for x in out]
        half = [dot1(x, jnp.where(merge, a, 0.0)) for x, a in zip(low, mats)]
        out = [o - dot1(h, x) for o, h, x in zip(out, half, low)]
        level += 1
    rest = [eye - x - dot3(a, x) for a, x in zip(mats, out)]
    return [x + dot1(x, r) for x, r in zip(out, rest)]


def mixer_bwd_kernel(heads, q_ref, k_ref, v_ref, aux_ref, gate_ref, gain_ref, mixed_ref, inv_ref,
                     state_ref, pseudo_ref, dgated_ref,
                     dq_ref, dk_ref, dv_ref, daux_ref, dgate_ref, dgain_ref, dstate):
    blocks = q_ref.shape[0] // STRETCH
    span = 2 * STRETCH
    masks = block_masks()
    t_row, t_col, p_row, p_col = masks
    for head in range(heads):
        dstate[head] = jnp.zeros((DK, DK), F32)
    dgain_ref[...] = jnp.zeros_like(dgain_ref)
    upper = (iota((STRETCH, STRETCH), 0) <= iota((STRETCH, STRETCH), 1)).astype(F32)
    lanes = iota((STRETCH, DK), 1)
    wide_lanes = iota((span, DK), 1)
    wide_rows = iota((span, DK), 0)

    def back(step, carry):
        block = blocks - 1 - step
        rows = pl.ds(pl.multiple_of(block * STRETCH, STRETCH), STRETCH)
        aux = aux_ref[rows, :]
        aux2, run2, aux_t, run_t = block_scalars(aux)
        dbeta_all = jnp.zeros((STRETCH, DK), F32)
        drun_all = jnp.zeros((STRETCH, DK), F32)
        column_sums = jnp.zeros((span, DK), F32)
        for head in range(heads):
            cols = slice(head * DK, (head + 1) * DK)
            beta, run_col, run_row, doc_col, doc_row, carried, to_last = head_terms(
                aux, aux2, run2, aux_t, run_t, head, heads
            )
            decay = decay_matrix(run_col, run_row, doc_col, doc_row, p_row, p_col)
            keys = keys = jnp.concatenate([k_ref[0, rows, cols], k_ref[1, rows, cols]], axis=0)
            queries = q_ref[rows, cols]
            mixed = mixed_ref[rows, cols]
            gate = gate_ref[rows, cols]
            sigmoid = jax.nn.sigmoid(gate)
            silu = gate * sigmoid
            scale = lax.rsqrt(jnp.mean(mixed * mixed, axis=-1, keepdims=True) + 1e-05)
            scaled = mixed * scale
            dgated = dgated_ref[rows, cols]
            part = dgated * scaled
            dgate_ref[rows, cols] = (
                part * gain_ref[...] * (sigmoid * (1.0 + gate * (1.0 - sigmoid)))
            ).astype(BF)
            dgain_ref[...] += jnp.sum(part * silu, axis=0, keepdims=True)
            dscaled = dgated * gain_ref[...] * silu
            dout = scale * (dscaled - scaled * jnp.mean(dscaled * scaled, axis=-1, keepdims=True))

            index = block * heads + head
            state, pseudo = state_ref[index], pseudo_ref[index]
            dnext = dstate[head]
            dnext_parts, state_parts, pseudo_parts = split(dnext), split(state), split(pseudo)
            dout_parts, q_parts = split(dout), split(queries)
            gram = dot1(keys, keys, NT)
            strict = p_row > p_col
            core = jnp.where(strict, decay * gram, 0.0)
            amat = beta * core
            qdecay = decay[STRETCH:]
            attn = qdecay * dot3(q_parts, keys, NT)
            dattn = dot3(dout_parts, pseudo_parts, NT)
            dqk = split(qdecay * dattn)
            dpseudo = dot3(attn, dout_parts, TN) + to_last * dot3(keys, dnext_parts)
            dtarget = dot3(inv_ref[index], dpseudo, TN)
            dtarget_parts = split(dtarget)
            damat = jnp.where(strict, -dot3(dtarget_parts, pseudo_parts, NT), 0.0)
            e_a, e_m = damat * amat, dattn * attn
            dgram = split(beta * decay * damat)
            dbeta = jnp.sum(dtarget * pseudo, axis=-1, keepdims=True) / jnp.maximum(beta, 1e-30)
            dvalues = beta * dtarget
            dread = -(beta * carried) * dtarget
            dout_c = carried[STRETCH:] * dout
            dread_parts, dout_c_parts = split(dread), split(dout_c)
            last = carried[span - 1 : span]
            dstate[head] = last * dnext + dot3(keys, dread_parts, TN) + dot3(q_parts, dout_c_parts, TN)
            dq_state = dot3(dout_c_parts, state_parts, NT)
            dk_state = dot3(dread_parts, state_parts, NT)
            dk_last = dot3(to_last * pseudo, dnext_parts, NT)
            dq_ref[rows, cols] = dq_state + dot3(dqk, keys)
            dkeys = (
                dk_state + dk_last + dot3(dgram, keys) + dot3(dgram, keys, TN) + dot3(dqk, q_parts, TN)
            )
            dk_ref[0, rows, cols] = dkeys[:STRETCH].astype(BF)
            dk_ref[1, rows, cols] = dkeys[STRETCH:].astype(BF)
            dv_ref[0, rows, cols] = dvalues[:STRETCH].astype(BF)
            dv_ref[1, rows, cols] = dvalues[STRETCH:].astype(BF)

            wide = keys.astype(F32)
            e_last = jnp.sum(wide * dk_last, axis=-1, keepdims=True)
            drun = jnp.sum(e_a, axis=-1, keepdims=True) - e_last + jnp.sum(wide * dk_state, axis=-1, keepdims=True)
            drun_q = jnp.sum(e_m, axis=-1, keepdims=True) + jnp.sum(queries * dq_state, axis=-1, keepdims=True)
            at_last = jnp.sum(e_last, axis=0, keepdims=True) + last * jnp.sum(
                jnp.sum(dnext * state, axis=-1, keepdims=True), axis=0, keepdims=True
            )
            drun = drun[:STRETCH] + drun[STRETCH:] + drun_q
            drun = drun + jnp.where(iota((STRETCH, 1), 0) == STRETCH - 1, at_last, 0.0)
            lane = 2 * heads + head
            drun_all = jnp.where(lanes == lane, drun, drun_all)
            dbeta_all = jnp.where(lanes == head, dbeta[:STRETCH], dbeta_all)
            dbeta_all = jnp.where(lanes == heads + head, dbeta[STRETCH:], dbeta_all)
            sums = jnp.sum(e_a, axis=0, keepdims=True) + jnp.sum(e_m, axis=0, keepdims=True)
            column_sums = jnp.where(wide_rows == lane, sums, column_sums)
        down = column_sums.T
        drun_all = drun_all - down[:STRETCH] - down[STRETCH:]
        daux_ref[rows, :] = jnp.where(lanes < 2 * heads, dbeta_all, dot6(upper, drun_all))
        return carry

    lax.fori_loop(0, blocks, back, 0)


VMEM = pl.BlockSpec(memory_space=pltpu.VMEM)


def mixer_bwd(q, k, v, aux, gate, gain, mixed, inv, state, pseudo, dgated):
    seq, width = q.shape
    heads = width // DK
    shape = jax.ShapeDtypeStruct
    return pl.pallas_call(
        functools.partial(mixer_bwd_kernel, heads),
        out_shape=(
            shape((seq, width), F32),
            shape(k.shape, BF),
            shape(v.shape, BF),
            shape((seq, DK), F32),
            shape((seq, width), BF),
            shape((1, DK), F32),
        ),
        in_specs=[VMEM] * 11,
        out_specs=(VMEM,) * 6,
        scratch_shapes=[pltpu.VMEM((heads, DK, DK), F32)],
        compiler_params=pltpu.CompilerParams(vmem_limit_bytes=48 << 20),
        name="mixer_backward",
    )(q, k, v, aux, gate, gain, mixed, inv, state, pseudo, dgated)


MESH = pl.DeviceIdType.MESH


class Place:
    def __init__(self, line):
        self.line = line
        self.dp, self.side = lax.axis_index("dp"), lax.axis_index("step")
        self.z, self.x, self.c = self.dp // 4, (self.dp // 2) % 2, self.dp % 2
        self.sibling = (self.dp + 1 - 2 * self.c, self.side)
        self.across = (self.dp + 2 - 4 * self.x, self.side)
        self.ahead = (
            (lax.rem(self.dp + 4, 4 * line), self.side),
            (lax.rem(self.dp + 4 * line - 4, 4 * line), self.side),
        )
        self.peer = (self.dp, 1 - self.side)
        self.can_send = (self.z + 1 < line, self.z > 0)

    def reaches(self, way, far):
        return self.z - far >= 0 if way == 0 else self.z + far < self.line

    def behind(self, way, far):
        return self.dp - 4 * far if way == 0 else self.dp + 4 * far

    def enter(self, plane=True, peer=True):
        barrier = pltpu.get_barrier_semaphore()

        def greet(device):
            pl.semaphore_signal(barrier, inc=1, device_id=device, device_id_type=MESH)

        count = 0
        if peer:
            greet(self.peer)
            count = 1
        if plane:
            greet(self.sibling)
            greet(self.across)
            for way in (0, 1):
                pl.when(self.can_send[way])(functools.partial(greet, self.ahead[way]))
            count = count + 2 + self.can_send[0].astype(jnp.int32) + self.can_send[1].astype(jnp.int32)
        pl.semaphore_wait(barrier, count)


def remote(src, dst, send_sem, recv_sem, device):
    return pltpu.make_async_remote_copy(
        src_ref=src, dst_ref=dst, send_sem=send_sem, recv_sem=recv_sem,
        device_id=device, device_id_type=MESH,
    )


def gather_sems(line, parts):
    dma = pltpu.SemaphoreType.DMA
    return [
        dma((2, line, parts)), dma((2, line, parts)),
        dma((2, line, parts)), dma((2, line, parts)),
        dma((2, 2, line, parts)), dma((2, 2, line, parts)),
    ]


class Gather:
    def __init__(self, place, buf, cuts, sems):
        self.place, self.buf, self.cuts = place, buf, cuts
        self.zs, self.zr, self.xs, self.xr, self.cs, self.cr = sems

    def block(self, index, part):
        start, width = self.cuts[part]
        return self.buf.at[index, :, pl.ds(start, width)]

    def line_copy(self, index, way, far, part):
        ref = self.block(index, part)
        return remote(ref, ref, self.zs.at[way, far, part], self.zr.at[way, far, part], self.place.ahead[way])

    def across_copy(self, index, way, far, part):
        ref = self.block(index, part)
        return remote(ref, ref, self.xs.at[way, far, part], self.xr.at[way, far, part], self.place.across)

    def sibling_copy(self, index, column, way, far, part):
        ref = self.block(index, part)
        return remote(
            ref, ref, self.cs.at[column, way, far, part], self.cr.at[column, way, far, part], self.place.sibling
        )

    def spread(self, index, way, far, part):
        place = self.place
        for to in (0, 1) if far == 0 else (way,):
            pl.when(place.can_send[to])(lambda to=to: self.line_copy(index, to, far + 1, part).start())
        self.across_copy(index, way, far, part).start()
        self.sibling_copy(index, 0, way, far, part).start()

    def ways(self, far):
        return (0,) if far == 0 else (0, 1)

    def each(self, far, act):
        if far == 0:
            act(0)
            return
        for way in (0, 1):
            pl.when(self.place.reaches(way, far))(functools.partial(act, way))

    def step(self, far, part):
        place = self.place
        if far == 0:
            self.spread(place.dp, 0, 0, part)
            return

        def from_line(way):
            index = place.behind(way, far)
            self.line_copy(index, way, far, part).wait_recv()
            self.spread(index, way, far, part)

        def from_across(way):
            index = place.behind(way, far - 1) + 2 - 4 * place.x
            self.across_copy(index, way, far - 1, part).wait_recv()
            self.sibling_copy(index, 1, way, far - 1, part).start()

        if far < place.line:
            self.each(far, from_line)
        self.each(far - 1, from_across)

    def steps(self):
        return [
            functools.partial(self.step, far, part)
            for far in range(self.place.line + 1)
            for part in range(len(self.cuts))
        ]

    def ready(self, part):
        place = self.place
        for far in range(place.line):
            for column in (0, 1):

                def from_sibling(way):
                    index = place.behind(way, far) + 1 - 2 * place.c + column * (2 - 4 * place.x)
                    self.sibling_copy(index, column, way, far, part).wait_recv()

                self.each(far, from_sibling)

    def drain(self, part):
        place = self.place
        for far in range(place.line):

            def sent(way):
                index = place.behind(way, far)
                for to in (0, 1) if far == 0 else (way,):
                    pl.when(place.can_send[to])(
                        lambda to=to: self.line_copy(index, to, far + 1, part).wait_send()
                    )
                self.across_copy(index, way, far, part).wait_send()
                self.sibling_copy(index, 0, way, far, part).wait_send()
                self.sibling_copy(index + 2 - 4 * place.x, 1, way, far, part).wait_send()

            self.each(far, sent)


def run_slot(slots, turn):
    for index, steps in enumerate(slots):
        if steps:

            def go(steps=steps):
                for step in steps:
                    step()

            pl.when(turn == index)(go)


def deal(steps, turns):
    return [steps[len(steps) * i // turns : len(steps) * (i + 1) // turns] for i in range(turns)]


KW = 4
PAD = 8


def conv_window(window, kernel, same):
    rows = window.shape[0] - PAD
    out = window[PAD:] * kernel[0:1]
    for offset in range(1, KW):
        out = out + jnp.where(same[offset - 1], window[PAD - offset : PAD - offset + rows], 0.0) * kernel[offset : offset + 1]
    return out


def same_documents(window):
    rows = window.shape[0] - PAD
    return [window[PAD:] == window[PAD - offset : PAD - offset + rows] for offset in range(1, KW)]


def rows_of(ref, block, count, extra=0):
    return ref[pl.ds(pl.multiple_of(block * STRETCH, STRETCH), count + extra), :]


def scalar_select(side, heads):
    src, dst = iota((DK, DK), 0), iota((DK, DK), 1)
    kind, head = dst // heads, dst % heads
    first = jnp.where(kind == side, 0, 2 * heads)
    source = jnp.where(kind < 2, first + side * heads + head, 4 * heads + head)
    return ((src == source) & (kind < 3)).astype(F32)


def softplus(values):
    return jnp.maximum(values, 0.0) + jnp.log1p(jnp.exp(-jnp.abs(values)))


def front_kernel(
    line, heads, x_ref, docs_ref, norm_ref, wq_ref, wg_ref, wk_ref, wv_ref, scal_ref, rest_ref, rates_ref,
    cq_ref, ck_ref, cv_ref, mix_ref,
    gated_ref, mixed_ref, inv_ref, state_ref, pseudo_ref, pre_ref, q_ref, k_ref, v_ref, aux_ref, conv_ref,
    front_out, rest_out,
    front, normed, doc_cols, attn, scal_in, local_sem, y_send, y_recv, *sems,
):
    place = Place(line)
    side = place.side
    seq = x_ref.shape[0]
    depth, half = wq_ref.shape
    span = 2 * STRETCH
    blocks = seq // STRETCH
    scal_at = 6 * half
    me = place.dp
    place.enter()

    own_cols = pl.ds(pl.multiple_of(side * half, half), half)
    other_cols = pl.ds(pl.multiple_of((1 - side) * half, half), half)

    def at(first):
        return pl.ds(pl.multiple_of((first + side) * half, half), half)

    swaps = [
        remote(wk_ref.at[:, other_cols], front.at[me, :, at(2)], y_send.at[0], y_recv.at[0], place.peer),
        remote(wv_ref.at[:, other_cols], front.at[me, :, at(4)], y_send.at[1], y_recv.at[1], place.peer),
        remote(scal_ref, scal_in, y_send.at[2], y_recv.at[2], place.peer),
        remote(ck_ref.at[:, other_cols], conv_ref.at[1 + side], y_send.at[3], y_recv.at[3], place.peer),
        remote(cv_ref.at[:, other_cols], conv_ref.at[3 + side], y_send.at[4], y_recv.at[4], place.peer),
    ]
    for swap in swaps:
        swap.start()
    own_rest = pltpu.make_async_copy(rest_ref, rest_out.at[me], local_sem.at[0])
    own_rest.start()
    front[me, :, 0:half] = wq_ref[...]
    front[me, :, half : 2 * half] = wg_ref[...]
    front[me, :, at(2)] = wk_ref[:, own_cols]
    front[me, :, at(4)] = wv_ref[:, own_cols]
    conv_ref[0] = cq_ref[...]
    conv_ref[1 + side] = ck_ref[:, own_cols]
    conv_ref[3 + side] = cv_ref[:, own_cols]

    head_cuts = [(0, 2 * half), (2 * half, 2 * half), (4 * half, 2 * half + DK)]
    first = Gather(place, front, head_cuts, sems[:6])
    tail = rest_out.shape[-1]
    ff = (tail - half) // 3
    rest_cuts = [(0, half)] + [(half + i * ff, ff) for i in range(3)]
    second = Gather(place, rest_out, rest_cuts, sems[6:])

    first.step(0, 0)
    for swap in swaps:
        swap.wait_recv()
    lanes = iota((depth, DK), 1)
    theirs = pltpu.roll(scal_in[...].astype(F32), 2 * heads, 1)
    ours = scal_ref[...].astype(F32)
    swapped = (lanes >= 2 * heads) & (lanes < 4 * heads)
    front[me, :, scal_at : scal_at + DK] = jnp.where(swapped, theirs, ours).astype(BF)
    for part in (1, 2):
        first.step(0, part)
    own_rest.wait()

    def normalise(block, carry):
        rows = pl.ds(pl.multiple_of(block * STRETCH, STRETCH), STRETCH)
        x = x_ref[rows, :].astype(F32)
        scale = lax.rsqrt(jnp.mean(x * x, axis=-1, keepdims=True) + 1e-06)
        normed[rows, :] = (x * scale * norm_ref[...]).astype(BF)
        return carry

    lax.fori_loop(0, blocks, normalise, 0)
    doc_cols[0:PAD, :] = jnp.full((PAD, DK), -1.0, F32)
    for i in range(seq // DK):
        lane_docs = docs_ref[:, i * DK : (i + 1) * DK].astype(F32)
        doc_cols[PAD + i * DK : PAD + (i + 1) * DK, :] = jnp.broadcast_to(lane_docs, (DK, DK)).T
    pre_ref[0:PAD, :] = jnp.zeros((PAD, pre_ref.shape[1]), F32)

    steps = first.steps()[3:]
    for step in steps:
        step()
    for part in range(4):
        second.step(0, part)
    tile = 2 * DK
    for part, (start, width) in enumerate(head_cuts):
        first.ready(part)

        def project(index, carry, start=start):
            cols = pl.ds(pl.multiple_of(start + index * tile, DK), tile)
            weights = front[:, :, cols].reshape(-1, tile)
            pre_ref[PAD:, cols] = jnp.dot(normed[...], weights, preferred_element_type=F32)
            return carry

        lax.fori_loop(0, 2 * half // tile, project, 0)
    scal_cols = slice(scal_at, scal_at + DK)
    pre_ref[PAD:, scal_cols] = jnp.dot(
        normed[...], front[:, :, scal_cols].reshape(-1, DK), preferred_element_type=F32
    )
    keep_front = pltpu.make_async_copy(front, front_out, local_sem.at[1])
    keep_front.start()

    select = scalar_select(side, heads)
    rate = -jnp.exp(rates_ref[0:1, :])
    masks = block_masks()
    t_row, t_col, p_row, p_col = masks
    later = second.steps()[4:]
    together = 2
    slots = deal(later, blocks // together + blocks)

    def keys_of(rows, cols):
        return jnp.concatenate([k_ref[0, rows, cols], k_ref[1, rows, cols]], axis=0)

    def prepare_block(block):
        rows = pl.ds(pl.multiple_of(block * STRETCH, STRETCH), STRETCH)
        doc_window = rows_of(doc_cols, block, STRETCH, PAD)
        same = same_documents(doc_window)
        raw = dot6(pre_ref[pl.ds(pl.multiple_of(block * STRETCH, STRETCH) + PAD, STRETCH), scal_cols], select)
        lane = iota((STRETCH, DK), 1)
        beta = (2.0 * jax.nn.sigmoid(raw)).astype(BF).astype(F32)
        decay = rate * softplus(raw + rates_ref[1:2, :])
        docs = doc_window[PAD:]
        fresh = (docs == doc_window[PAD - 1 : PAD]).astype(F32)
        aux = jnp.where(lane < 2 * heads, beta, jnp.where(lane < 3 * heads, decay, 0.0))
        aux = jnp.where(lane == 3 * heads, docs, jnp.where(lane == 3 * heads + 1, fresh, aux))
        aux_ref[rows, :] = aux
        for head in range(heads):
            cols = slice(head * DK, (head + 1) * DK)
            for kind in (1, 2, 0, 3, 4):
                first_col = (0, 2, 3, 4, 5)[kind] * half + head * DK
                window = pre_ref[
                    pl.ds(pl.multiple_of(block * STRETCH, STRETCH), STRETCH + PAD), first_col : first_col + DK
                ]
                value = conv_window(window, conv_ref[kind, :, cols], same)
                value = value * jax.nn.sigmoid(value)
                if kind < 3:
                    value = value * lax.rsqrt(jnp.sum(value * value, axis=-1, keepdims=True) + 1e-06)
                if kind == 0:
                    q_ref[rows, cols] = value * DK ** (-0.5)
                elif kind < 3:
                    k_ref[kind - 1, rows, cols] = value.astype(BF)
                else:
                    v_ref[kind - 3, rows, cols] = value.astype(BF)
        aux2, run2, aux_t, run_t = block_scalars(aux)
        mats = []
        for head in range(heads):
            cols = slice(head * DK, (head + 1) * DK)
            beta, run_col, run_row, doc_col, doc_row, carried, to_last = head_terms(
                aux, aux2, run2, aux_t, run_t, head, heads
            )
            decay = decay_matrix(run_col, run_row, doc_col, doc_row, p_row, p_col)
            keys = keys_of(rows, cols)
            gram = dot1(keys, keys, NT)
            mats.append(beta * jnp.where(p_row > p_col, decay * gram, 0.0))
            attn[block * heads + head] = decay[STRETCH:] * dot3(q_ref[rows, cols], keys, NT)
        return mats

    def prepare(turn, carry):
        mats = []
        for i in range(together):
            mats += prepare_block(turn * together + i)
        for i, inv in enumerate(inverse(mats, masks)):
            inv_ref[turn * together * heads + i] = inv
        run_slot(slots[: blocks // together], turn)
        return carry

    lax.fori_loop(0, blocks // together, prepare, 0)
    for head in range(heads):
        state_ref[head] = jnp.zeros((DK, DK), F32)

    def advance(block, carry):
        rows = pl.ds(pl.multiple_of(block * STRETCH, STRETCH), STRETCH)
        aux = aux_ref[rows, :]
        aux2, run2, aux_t, run_t = block_scalars(aux)
        for head in range(heads):
            cols = slice(head * DK, (head + 1) * DK)
            beta, run_col, run_row, doc_col, doc_row, carried, to_last = head_terms(
                aux, aux2, run2, aux_t, run_t, head, heads
            )
            keys = keys_of(rows, cols)
            values = jnp.concatenate([v_ref[0, rows, cols], v_ref[1, rows, cols]], axis=0).astype(F32)
            state = state_ref[block * heads + head]
            state_parts = split(state)
            target = beta * (values - carried * dot3(keys, state_parts))
            pseudo = dot3(inv_ref[block * heads + head], target)
            pseudo_ref[block * heads + head] = pseudo
            mixed = carried[STRETCH:] * dot3(q_ref[rows, cols], state_parts) + dot3(
                attn[block * heads + head], pseudo
            )
            state_ref[(block + 1) * heads + head] = carried[span - 1 : span] * state + dot3(
                keys, to_last * pseudo, TN
            )
            mixed_ref[rows, cols] = mixed
            scale = lax.rsqrt(jnp.mean(mixed * mixed, axis=-1, keepdims=True) + 1e-05)
            gate = pre_ref[
                pl.ds(pl.multiple_of(block * STRETCH, STRETCH) + PAD, STRETCH),
                half + head * DK : half + (head + 1) * DK,
            ]
            gated_ref[rows, cols] = (mixed * scale * mix_ref[...] * (gate * jax.nn.sigmoid(gate))).astype(BF)
        run_slot(slots[blocks // together :], block)
        return carry

    lax.fori_loop(0, blocks, advance, 0)
    for part in range(4):
        second.ready(part)
    for swap in swaps:
        swap.wait_send()
    for part in range(3):
        first.drain(part)
    for part in range(4):
        second.drain(part)
    keep_front.wait()


def front_call(line, x, docs, norm, wq, wg, wk, wv, scal, rest, rates, cq, ck, cv, mix):
    seq, half = x.shape[0], wq.shape[1]
    depth, tail = rest.shape
    heads, blocks = half // DK, seq // STRETCH
    units, span = heads * blocks, 2 * STRETCH
    width = 6 * half + DK
    shape = jax.ShapeDtypeStruct
    anywhere = pl.BlockSpec(memory_space=pl.ANY)
    dma = pltpu.SemaphoreType.DMA
    return pl.pallas_call(
        functools.partial(front_kernel, line, heads),
        out_shape=(
            shape((seq, half), BF),
            shape((seq, half), F32),
            shape((units, span, span), F32),
            shape((units + heads, DK, DK), F32),
            shape((units, span, DK), F32),
            shape((seq + PAD, width), F32),
            shape((seq, half), F32),
            shape((2, seq, half), BF),
            shape((2, seq, half), BF),
            shape((seq, DK), F32),
            shape((5, KW, half), F32),
            shape((4 * line, depth, width), BF),
            shape((4 * line, depth, tail), BF),
        ),
        in_specs=[VMEM] * 8 + [anywhere] + [VMEM] * 5,
        out_specs=(VMEM,) * 11 + (anywhere,) * 2,
        scratch_shapes=[
            pltpu.VMEM((4 * line, depth, width), BF),
            pltpu.VMEM(x.shape, BF),
            pltpu.VMEM((seq + PAD, DK), F32),
            pltpu.VMEM((units, STRETCH, span), F32),
            pltpu.VMEM((depth, DK), BF),
            dma((2,)),
            dma((5,)),
            dma((5,)),
        ]
        + gather_sems(line, 3)
        + gather_sems(line, 4),
        compiler_params=pltpu.CompilerParams(
            collective_id=0, has_side_effects=True, vmem_limit_bytes=56 << 20
        ),
        name="front",
    )(x, docs, norm, wq, wg, wk, wv, scal, rest, rates, cq, ck, cv, mix)


GROUPS = 8


def product(first, second, dims=NN):
    return lax.dot_general(first, second, (dims, ((), ())), preferred_element_type=F32)


def rms_scale(values, scales):
    return values * lax.rsqrt(jnp.mean(values * values, axis=-1, keepdims=True) + 1e-06) * scales


def unit_rows(values):
    return values * lax.rsqrt(jnp.sum(values * values, axis=-1, keepdims=True) + 1e-06)


def silu_grad(values):
    sigmoid = jax.nn.sigmoid(values)
    return sigmoid * (1.0 + values * (1.0 - sigmoid))


def short_conv(signal, kernel, doc_ids):
    seq_len = signal.shape[0]
    summed = signal * kernel[0]
    for offset in range(1, kernel.shape[0]):
        shifted = jnp.pad(signal, ((offset, 0), (0, 0)))[:seq_len]
        shifted_docs = jnp.pad(doc_ids, (offset, 0), constant_values=-1)[:seq_len]
        same_doc = (shifted_docs == doc_ids).astype(F32)[:, None]
        summed = summed + shifted * same_doc * kernel[offset]
    return summed


def unit_heads(values):
    seq_len = values.shape[0]
    return unit_rows(values.reshape(seq_len, -1, DK)).reshape(seq_len, -1)


def per_device(
    tokens,
    cotangent,
    domains,
    doc_ids,
    norm_gain,
    w_query,
    w_outgate,
    w_key,
    w_value,
    w_beta,
    w_alpha,
    decay_log,
    decay_bias,
    conv_query,
    conv_key,
    conv_value,
    mix_gain,
    w_out,
    ffn_gain,
    w_gate,
    w_up,
    w_down,
):
    row_total = domains.shape[0]
    group_ids = lax.broadcasted_iota(jnp.int32, (row_total, GROUPS), 1)
    member = (domains[:, None] == group_ids).astype(F32)
    group_sizes = jnp.sum(member, axis=0)
    row_sizes = jnp.sum(member * group_sizes[None, :], axis=1)
    row_weights = 2.0 / (1.0 + row_sizes * (GROUPS / row_total))
    own_row = (lax.broadcasted_iota(jnp.int32, (row_total,), 0) == lax.axis_index("dp")).astype(F32)
    weight_here = jnp.sum(own_row * row_weights)

    depth = w_query.shape[0]
    half = w_query.shape[1]
    heads = w_alpha.shape[1]
    side = lax.axis_index("step")

    def swap(array):
        return lax.ppermute(array, "step", [(0, 1), (1, 0)])

    rest = jnp.concatenate([w_out.T, w_gate, w_up, w_down.T], axis=1)
    scal = jnp.concatenate(
        [w_beta[0], jnp.zeros((depth, 2 * heads), BF), w_alpha, jnp.zeros((depth, DK - 5 * heads), BF)], axis=1
    )
    rates = jnp.pad(jnp.stack([decay_log, decay_bias]), ((0, 0), (2 * heads, DK - 3 * heads)))
    gain_row = mix_gain[None]
    (gated, mixed, inv, state, pseudo, pre, queries, keys, values, aux, conv, front_w, back_w) = front_call(
        lax.axis_size("dp") // 4, tokens[0], doc_ids, norm_gain[None], w_query, w_outgate, w_key[0], w_value[0],
        scal, rest, rates, conv_query, conv_key[0], conv_value[0], gain_row,
    )
    ff = w_gate.shape[1]
    front_w = front_w.reshape(-1, front_w.shape[-1])
    back_w = back_w.reshape(-1, back_w.shape[-1])
    inputs = tokens[0].astype(F32)
    docs = doc_ids[0]
    seq_len = inputs.shape[0]
    normed_f, pull_first = jax.vjp(rms_scale, inputs, norm_gain)
    normed = normed_f.astype(BF)
    pre = pre[PAD:]
    gate_pre = pre[:, half : 2 * half]

    def prepare(pre_in, query_kernel, key_0, key_1, value_0, value_1, log_rates, rate_bias):
        queries = unit_heads(jax.nn.silu(short_conv(pre_in[:, :half], query_kernel, docs))) * DK ** (-0.5)
        keys = [
            unit_heads(jax.nn.silu(short_conv(pre_in[:, (2 + i) * half : (3 + i) * half], kernel, docs)))
            for i, kernel in enumerate((key_0, key_1))
        ]
        values = [
            jax.nn.silu(short_conv(pre_in[:, (4 + i) * half : (5 + i) * half], kernel, docs))
            for i, kernel in enumerate((value_0, value_1))
        ]
        scalars = pre_in[:, 6 * half :] @ scalar_select(side, heads)
        betas = 2.0 * jax.nn.sigmoid(scalars[:, : 2 * heads])
        decays = -jnp.exp(log_rates) * jax.nn.softplus(scalars[:, 2 * heads : 3 * heads] + rate_bias)
        return (queries, jnp.stack(keys), jnp.stack(values), betas, decays)

    _, pull_prepare = jax.vjp(
        prepare, pre, conv[0], conv[1], conv[2], conv[3], conv[4], decay_log, decay_bias
    )

    attention = lax.psum(product(gated, back_w[:, :half], NT).astype(BF), "step").astype(F32)
    middle = inputs + attention
    normed_ffn_f, pull_second = jax.vjp(rms_scale, middle, ffn_gain)
    normed_ffn = normed_ffn_f.astype(BF)
    gate_w, up_w, down_w = (back_w[:, half + i * ff : half + (i + 1) * ff] for i in range(3))
    gate_in = product(normed_ffn, gate_w)
    up_in = product(normed_ffn, up_w)
    hidden = (jax.nn.silu(gate_in) * up_in).astype(BF)
    ffn_out = lax.psum(product(hidden, down_w, NT).astype(BF), "step").astype(F32)
    output = (middle + ffn_out).astype(BF)[None]

    seed = cotangent[0].astype(F32) * weight_here
    seed_low = seed.astype(BF)
    grad_down = product(seed_low, hidden, TN)
    hidden_back = product(seed_low, down_w)
    gate_back = (hidden_back * up_in * silu_grad(gate_in)).astype(BF)
    up_back = (hidden_back * jax.nn.silu(gate_in)).astype(BF)
    grad_gate = product(normed_ffn, gate_back, TN)
    grad_up = product(normed_ffn, up_back, TN)
    ffn_in_back = lax.psum(
        (product(gate_back, gate_w, NT) + product(up_back, up_w, NT)).astype(BF), "step"
    ).astype(F32)
    middle_norm_back, grad_ffn_gain = pull_second(ffn_in_back)
    middle_back = seed + middle_norm_back
    attn_back = middle_back.astype(BF)
    grad_out = product(attn_back, gated, TN)
    sum_back = lax.psum_scatter(
        jnp.concatenate([grad_out, grad_gate, grad_up, grad_down], axis=1).astype(BF),
        "dp", scatter_dimension=0, tiled=True,
    ).astype(F32)
    gated_back = product(attn_back, back_w[:, :half])
    dq, dk, dv, daux, dgate, dgain = mixer_bwd(
        queries, keys, values, aux, gate_pre, gain_row, mixed, inv, state, pseudo, gated_back
    )
    dbetas = daux[:, : 2 * heads].astype(BF).astype(F32)
    ddecays = daux[:, 2 * heads : 3 * heads]
    dpre, d_cq, d_k0, d_k1, d_v0, d_v1, d_log, d_bias = pull_prepare(
        (dq, dk.astype(F32), dv.astype(F32), dbetas, ddecays)
    )
    dpre_low = jnp.concatenate([dpre[:, :half].astype(BF), dgate, dpre[:, 2 * half :].astype(BF)], axis=1)
    grad_front = product(normed, dpre_low, TN)
    normed_back = lax.psum(product(dpre_low, front_w, NT).astype(BF), "step").astype(F32)
    input_back, grad_norm_gain = pull_first(normed_back)
    input_grad = (middle_back + input_back).astype(BF)[None]
    sum_front = lax.psum_scatter(grad_front.astype(BF), "dp", scatter_dimension=0, tiled=True)

    def home(parts):
        mine = jnp.where(side == 0, parts[0], parts[1])
        other = swap(jnp.where(side == 0, parts[1], parts[0]))
        return jnp.where(
            side == 0, jnp.concatenate([mine, other], axis=1), jnp.concatenate([other, mine], axis=1)
        )

    col = lambda i: sum_front[:, i * half : (i + 1) * half]
    sum_key, sum_value = home([col(2), col(3)]), home([col(4), col(5)])
    tail = sum_front[:, 6 * half :]
    sum_beta = tail[:, : 2 * heads] + swap(tail[:, 2 * heads : 4 * heads])
    small = lax.psum(
        (grad_norm_gain, d_log, d_bias, d_cq, d_k0, d_k1, d_v0, d_v1, grad_ffn_gain), "dp"
    )
    sum_norm_gain, sum_log, sum_bias, sum_cq, s_k0, s_k1, s_v0, s_v1, sum_ffn_gain = small
    sum_mix_gain = lax.psum(dgain[0], ("dp", "step"))
    f32 = lambda a: a.astype(F32)
    return (
        output,
        input_grad,
        sum_norm_gain,
        f32(col(0)),
        f32(col(1)),
        f32(sum_key)[None],
        f32(sum_value)[None],
        f32(sum_beta)[None],
        f32(tail[:, 4 * heads : 5 * heads]),
        sum_log,
        sum_bias,
        sum_cq,
        home([s_k0, s_k1])[None],
        home([s_v0, s_v1])[None],
        sum_mix_gain,
        sum_back[:, :half].T,
        sum_ffn_gain,
        sum_back[:, half : half + ff],
        sum_back[:, half + ff : half + 2 * ff],
        sum_back[:, half + 2 * ff :].T,
    )


def solution(mesh):
    return jax.shard_map(
        per_device,
        mesh=mesh,
        in_specs=(
            P("dp", None, None),
            P("dp", None, None),
            P(),
            P("dp", None),
            P(),
            P("dp", "step"),
            P("dp", "step"),
            P("step", "dp", None),
            P("step", "dp", None),
            P("step", "dp", None),
            P("dp", "step"),
            P("step"),
            P("step"),
            P(None, "step"),
            P("step", None, None),
            P("step", None, None),
            P(),
            P("step", "dp"),
            P(),
            P("dp", "step"),
            P("dp", "step"),
            P("step", "dp"),
        ),
        out_specs=(
            P("dp", None, None),
            P("dp", None, None),
            P(),
            P("dp", "step"),
            P("dp", "step"),
            P("step", "dp", None),
            P("step", "dp", None),
            P("step", "dp", None),
            P("dp", "step"),
            P("step"),
            P("step"),
            P(None, "step"),
            P("step", None, None),
            P("step", None, None),
            P(),
            P("step", "dp"),
            P(),
            P("dp", "step"),
            P("dp", "step"),
            P("step", "dp"),
        ),
        check_vma=False,
    )
```

```python
import functools

import jax
import jax.numpy as jnp
from jax import lax
from jax.experimental import pallas as pl
from jax.experimental.pallas import tpu as pltpu
from jax.sharding import PartitionSpec as P

STRETCH = 64
DK = 128
F32 = jnp.float32
BF = jnp.bfloat16
NN = ((1,), (0,))
NT = ((1,), (1,))
TN = ((0,), (0,))


def split(a):
    if a.dtype == BF:
        return (a,)
    hi = a.astype(BF)
    return (hi, (a - hi.astype(F32)).astype(BF))


def dot1(a, b, dims=NN):
    return lax.dot_general(a.astype(BF), b.astype(BF), (dims, ((), ())), preferred_element_type=F32)


def dot3(a, b, dims=NN):
    a = a if isinstance(a, tuple) else split(a)
    b = b if isinstance(b, tuple) else split(b)
    one = lambda x, y: lax.dot_general(x, y, (dims, ((), ())), preferred_element_type=F32)
    out = one(a[0], b[0])
    if len(a) > 1:
        out = out + one(a[1], b[0])
    if len(b) > 1:
        out = out + one(a[0], b[1])
    return out


def dot6(a, b, dims=NN):
    return lax.dot_general(
        a, b, (dims, ((), ())), precision=lax.Precision.HIGHEST, preferred_element_type=F32
    )


def iota(shape, dim):
    return lax.broadcasted_iota(jnp.int32, shape, dim)


def product(first, second, dims=NN):
    return lax.dot_general(first, second, (dims, ((), ())), preferred_element_type=F32)


def block_masks():
    span = 2 * STRETCH
    row, col = iota((span, span), 0), iota((span, span), 1)
    t_row, t_col = row % STRETCH, col % STRETCH
    p_row, p_col = 2 * t_row + row // STRETCH, 2 * t_col + col // STRETCH
    return t_row, t_col, p_row, p_col


def twice(block):
    return jnp.concatenate([block, block], axis=0)


def block_scalars(aux):
    low = (iota((STRETCH, STRETCH), 0) >= iota((STRETCH, STRETCH), 1)).astype(F32)
    running = dot6(low, aux)
    aux2, run2 = twice(aux), twice(running)
    return aux2, run2, aux2.T, run2.T


def head_terms(aux, aux2, run2, aux_t, run_t, head, heads):
    beta = jnp.concatenate(
        [aux[:, head : head + 1], aux[:, heads + head : heads + head + 1]], axis=0
    )
    lane = 2 * heads + head
    run_col = run2[:, lane : lane + 1]
    run_row = run_t[lane : lane + 1, :]
    doc_lane = 3 * heads
    doc_col = aux2[:, doc_lane : doc_lane + 1]
    doc_row = aux_t[doc_lane : doc_lane + 1, :]
    fresh = aux2[:, doc_lane + 1 : doc_lane + 2]
    span = 2 * STRETCH
    carried = jnp.where(fresh > 0.5, jnp.exp(run_col), 0.0)
    last_run = run_col[span - 1 : span, :]
    to_last = jnp.where(doc_col == doc_col[span - 1 : span, :], jnp.exp(last_run - run_col), 0.0)
    return beta, run_col, run_row, doc_col, doc_row, carried, to_last


def decay_matrix(run_col, run_row, doc_col, doc_row, p_row, p_col):
    inside = (p_row >= p_col) & (doc_col == doc_row)
    return jnp.where(inside, jnp.exp(jnp.where(inside, run_col - run_row, 0.0)), 0.0)


def inverse(mats, masks):
    t_row, t_col, p_row, p_col = masks
    eye = (p_row == p_col).astype(F32)
    pair = (t_row == t_col) & (p_row > p_col)
    out = [eye - jnp.where(pair, a, 0.0) for a in mats]
    level = 1
    while (1 << level) <= STRETCH:
        merge = (
            ((t_row >> level) == (t_col >> level))
            & (((t_row >> (level - 1)) & 1) == 1)
            & (((t_col >> (level - 1)) & 1) == 0)
        )
        low = [x.astype(BF) for x in out]
        half = [dot1(x, jnp.where(merge, a, 0.0)) for x, a in zip(low, mats)]
        out = [o - dot1(h, x) for o, h, x in zip(out, half, low)]
        level += 1
    rest = [eye - x - dot3(a, x) for a, x in zip(mats, out)]
    return [x + dot1(x, r) for x, r in zip(out, rest)]


VMEM = pl.BlockSpec(memory_space=pltpu.VMEM)


MESH = pl.DeviceIdType.MESH


class Place:
    def __init__(self, line):
        self.line = line
        self.dp, self.side = lax.axis_index("dp"), lax.axis_index("step")
        self.z, self.x, self.c = self.dp // 4, (self.dp // 2) % 2, self.dp % 2
        self.sibling = (self.dp + 1 - 2 * self.c, self.side)
        self.across = (self.dp + 2 - 4 * self.x, self.side)
        self.ahead = (
            (lax.rem(self.dp + 4, 4 * line), self.side),
            (lax.rem(self.dp + 4 * line - 4, 4 * line), self.side),
        )
        self.peer = (self.dp, 1 - self.side)
        self.can_send = (self.z + 1 < line, self.z > 0)

    def reaches(self, way, far):
        return self.z - far >= 0 if way == 0 else self.z + far < self.line

    def behind(self, way, far):
        return self.dp - 4 * far if way == 0 else self.dp + 4 * far

    def enter(self, plane=True, peer=True, everyone=False):
        barrier = pltpu.get_barrier_semaphore()

        def greet(device):
            pl.semaphore_signal(barrier, inc=1, device_id=device, device_id_type=MESH)

        count = 0
        if peer:
            greet(self.peer)
            count = 1
        if plane:
            greet(self.sibling)
            greet(self.across)
            count = count + 2
        if everyone:
            for z in range(self.line):
                device = (z * 4 + self.x * 2 + self.c, self.side)
                pl.when(z != self.z)(functools.partial(greet, device))
            count = count + self.line - 1
        elif plane:
            for way in (0, 1):
                pl.when(self.can_send[way])(functools.partial(greet, self.ahead[way]))
            count = count + self.can_send[0].astype(jnp.int32) + self.can_send[1].astype(jnp.int32)
        pl.semaphore_wait(barrier, count)


def remote(src, dst, send_sem, recv_sem, device):
    return pltpu.make_async_remote_copy(
        src_ref=src, dst_ref=dst, send_sem=send_sem, recv_sem=recv_sem,
        device_id=device, device_id_type=MESH,
    )


def gather_sems(line, parts):
    dma = pltpu.SemaphoreType.DMA
    return [
        dma((2, line, parts)), dma((2, line, parts)),
        dma((2, line, parts)), dma((2, line, parts)),
        dma((2, 2, line, parts)), dma((2, 2, line, parts)),
    ]


class Gather:
    def __init__(self, place, buf, cuts, sems):
        self.place, self.buf, self.cuts = place, buf, cuts
        self.zs, self.zr, self.xs, self.xr, self.cs, self.cr = sems

    def block(self, index, part):
        start, width = self.cuts[part]
        return self.buf.at[index, :, pl.ds(start, width)]

    def line_copy(self, index, way, far, part):
        ref = self.block(index, part)
        return remote(ref, ref, self.zs.at[way, far, part], self.zr.at[way, far, part], self.place.ahead[way])

    def across_copy(self, index, way, far, part):
        ref = self.block(index, part)
        return remote(ref, ref, self.xs.at[way, far, part], self.xr.at[way, far, part], self.place.across)

    def sibling_copy(self, index, column, way, far, part):
        ref = self.block(index, part)
        return remote(
            ref, ref, self.cs.at[column, way, far, part], self.cr.at[column, way, far, part], self.place.sibling
        )

    def spread(self, index, way, far, part):
        place = self.place
        for to in (0, 1) if far == 0 else (way,):
            pl.when(place.can_send[to])(lambda to=to: self.line_copy(index, to, far + 1, part).start())
        self.across_copy(index, way, far, part).start()
        self.sibling_copy(index, 0, way, far, part).start()

    def ways(self, far):
        return (0,) if far == 0 else (0, 1)

    def each(self, far, act):
        if far == 0:
            act(0)
            return
        for way in (0, 1):
            pl.when(self.place.reaches(way, far))(functools.partial(act, way))

    def step(self, far, part):
        place = self.place
        if far == 0:
            self.spread(place.dp, 0, 0, part)
            return

        def from_line(way):
            index = place.behind(way, far)
            self.line_copy(index, way, far, part).wait_recv()
            self.spread(index, way, far, part)

        def from_across(way):
            index = place.behind(way, far - 1) + 2 - 4 * place.x
            self.across_copy(index, way, far - 1, part).wait_recv()
            self.sibling_copy(index, 1, way, far - 1, part).start()

        if far < place.line:
            self.each(far, from_line)
        self.each(far - 1, from_across)

    def steps(self):
        return [
            functools.partial(self.step, far, part)
            for far in range(self.place.line + 1)
            for part in range(len(self.cuts))
        ]

    def ready(self, part):
        place = self.place
        for far in range(place.line):
            for column in (0, 1):

                def from_sibling(way):
                    index = place.behind(way, far) + 1 - 2 * place.c + column * (2 - 4 * place.x)
                    self.sibling_copy(index, column, way, far, part).wait_recv()

                self.each(far, from_sibling)

    def drain(self, part):
        place = self.place
        for far in range(place.line):

            def sent(way):
                index = place.behind(way, far)
                for to in (0, 1) if far == 0 else (way,):
                    pl.when(place.can_send[to])(
                        lambda to=to: self.line_copy(index, to, far + 1, part).wait_send()
                    )
                self.across_copy(index, way, far, part).wait_send()
                self.sibling_copy(index, 0, way, far, part).wait_send()
                self.sibling_copy(index + 2 - 4 * place.x, 1, way, far, part).wait_send()

            self.each(far, sent)


def run_slot(slots, turn):
    for index, steps in enumerate(slots):
        if steps:

            def go(steps=steps):
                for step in steps:
                    step()

            pl.when(turn == index)(go)


def deal(steps, turns):
    return [steps[len(steps) * i // turns : len(steps) * (i + 1) // turns] for i in range(turns)]


KW = 4
PAD = 8


def conv_window(window, kernel, same):
    rows = window.shape[0] - PAD
    out = window[PAD:] * kernel[0:1]
    for offset in range(1, KW):
        out = out + jnp.where(same[offset - 1], window[PAD - offset : PAD - offset + rows], 0.0) * kernel[offset : offset + 1]
    return out


def same_documents(window):
    rows = window.shape[0] - PAD
    return [window[PAD:] == window[PAD - offset : PAD - offset + rows] for offset in range(1, KW)]


def rows_of(ref, block, count, extra=0):
    return ref[pl.ds(pl.multiple_of(block * STRETCH, STRETCH), count + extra), :]


def scalar_select(side, heads):
    src, dst = iota((DK, DK), 0), iota((DK, DK), 1)
    kind, head = dst // heads, dst % heads
    first = jnp.where(kind == side, 0, 2 * heads)
    source = jnp.where(kind < 2, first + side * heads + head, 4 * heads + head)
    return ((src == source) & (kind < 3)).astype(F32)


def softplus(values):
    return jnp.maximum(values, 0.0) + jnp.log1p(jnp.exp(-jnp.abs(values)))


def front_kernel(
    line, heads, x_ref, docs_ref, norm_ref, wq_ref, wg_ref, wk_ref, wv_ref, scal_ref, rest_ref, rates_ref,
    cq_ref, ck_ref, cv_ref, mix_ref,
    gated_ref, mixed_ref, inv_ref, state_ref, pseudo_ref, pre_ref, q_ref, k_ref, v_ref, aux_ref, conv_ref,
    front_out, rest_out,
    front, normed, doc_cols, attn, scal_in, local_sem, y_send, y_recv, *sems,
):
    place = Place(line)
    side = place.side
    seq = x_ref.shape[0]
    depth, half = wq_ref.shape
    span = 2 * STRETCH
    blocks = seq // STRETCH
    scal_at = 6 * half
    me = place.dp
    place.enter()

    own_cols = pl.ds(pl.multiple_of(side * half, half), half)
    other_cols = pl.ds(pl.multiple_of((1 - side) * half, half), half)

    def at(first):
        return pl.ds(pl.multiple_of((first + side) * half, half), half)

    swaps = [
        remote(wk_ref.at[:, other_cols], front.at[me, :, at(2)], y_send.at[0], y_recv.at[0], place.peer),
        remote(wv_ref.at[:, other_cols], front.at[me, :, at(4)], y_send.at[1], y_recv.at[1], place.peer),
        remote(scal_ref, scal_in, y_send.at[2], y_recv.at[2], place.peer),
        remote(ck_ref.at[:, other_cols], conv_ref.at[1 + side], y_send.at[3], y_recv.at[3], place.peer),
        remote(cv_ref.at[:, other_cols], conv_ref.at[3 + side], y_send.at[4], y_recv.at[4], place.peer),
    ]
    for swap in swaps:
        swap.start()
    own_rest = pltpu.make_async_copy(rest_ref, rest_out.at[me], local_sem.at[0])
    own_rest.start()
    front[me, :, 0:half] = wq_ref[...]
    front[me, :, half : 2 * half] = wg_ref[...]
    front[me, :, at(2)] = wk_ref[:, own_cols]
    front[me, :, at(4)] = wv_ref[:, own_cols]
    conv_ref[0] = cq_ref[...]
    conv_ref[1 + side] = ck_ref[:, own_cols]
    conv_ref[3 + side] = cv_ref[:, own_cols]

    head_cuts = [(0, 2 * half), (2 * half, 2 * half), (4 * half, 2 * half + DK)]
    first = Gather(place, front, head_cuts, sems[:6])
    tail = rest_out.shape[-1]
    ff = (tail - half) // 3
    rest_cuts = [(0, half)] + [(half + i * ff, ff) for i in range(3)]
    second = Gather(place, rest_out, rest_cuts, sems[6:])

    first.step(0, 0)
    for swap in swaps:
        swap.wait_recv()
    lanes = iota((depth, DK), 1)
    theirs = pltpu.roll(scal_in[...].astype(F32), 2 * heads, 1)
    ours = scal_ref[...].astype(F32)
    swapped = (lanes >= 2 * heads) & (lanes < 4 * heads)
    front[me, :, scal_at : scal_at + DK] = jnp.where(swapped, theirs, ours).astype(BF)
    for part in (1, 2):
        first.step(0, part)
    own_rest.wait()

    def normalise(block, carry):
        rows = pl.ds(pl.multiple_of(block * STRETCH, STRETCH), STRETCH)
        x = x_ref[rows, :].astype(F32)
        scale = lax.rsqrt(jnp.mean(x * x, axis=-1, keepdims=True) + 1e-06)
        normed[rows, :] = (x * scale * norm_ref[...]).astype(BF)
        return carry

    lax.fori_loop(0, blocks, normalise, 0)
    doc_cols[0:PAD, :] = jnp.full((PAD, DK), -1.0, F32)
    for i in range(seq // DK):
        lane_docs = docs_ref[:, i * DK : (i + 1) * DK].astype(F32)
        doc_cols[PAD + i * DK : PAD + (i + 1) * DK, :] = jnp.broadcast_to(lane_docs, (DK, DK)).T
    pre_ref[0:PAD, :] = jnp.zeros((PAD, pre_ref.shape[1]), F32)

    steps = first.steps()[3:]
    for step in steps:
        step()
    for part in range(4):
        second.step(0, part)
    tile = 2 * DK
    for part, (start, width) in enumerate(head_cuts):
        first.ready(part)

        def project(index, carry, start=start):
            cols = pl.ds(pl.multiple_of(start + index * tile, DK), tile)
            weights = front[:, :, cols].reshape(-1, tile)
            pre_ref[PAD:, cols] = jnp.dot(normed[...], weights, preferred_element_type=F32)
            return carry

        lax.fori_loop(0, 2 * half // tile, project, 0)
    scal_cols = slice(scal_at, scal_at + DK)
    pre_ref[PAD:, scal_cols] = jnp.dot(
        normed[...], front[:, :, scal_cols].reshape(-1, DK), preferred_element_type=F32
    )
    keep_front = pltpu.make_async_copy(front, front_out, local_sem.at[1])
    keep_front.start()

    select = scalar_select(side, heads)
    rate = -jnp.exp(rates_ref[0:1, :])
    masks = block_masks()
    t_row, t_col, p_row, p_col = masks
    later = second.steps()[4:]
    together = 2
    slots = deal(later, blocks // together + blocks)

    def keys_of(rows, cols):
        return jnp.concatenate([k_ref[0, rows, cols], k_ref[1, rows, cols]], axis=0)

    def prepare_block(block):
        rows = pl.ds(pl.multiple_of(block * STRETCH, STRETCH), STRETCH)
        doc_window = rows_of(doc_cols, block, STRETCH, PAD)
        same = same_documents(doc_window)
        raw = dot6(pre_ref[pl.ds(pl.multiple_of(block * STRETCH, STRETCH) + PAD, STRETCH), scal_cols], select)
        lane = iota((STRETCH, DK), 1)
        beta = (2.0 * jax.nn.sigmoid(raw)).astype(BF).astype(F32)
        decay = rate * softplus(raw + rates_ref[1:2, :])
        docs = doc_window[PAD:]
        fresh = (docs == doc_window[PAD - 1 : PAD]).astype(F32)
        aux = jnp.where(lane < 2 * heads, beta, jnp.where(lane < 3 * heads, decay, 0.0))
        aux = jnp.where(lane == 3 * heads, docs, jnp.where(lane == 3 * heads + 1, fresh, aux))
        aux_ref[rows, :] = aux
        for head in range(heads):
            cols = slice(head * DK, (head + 1) * DK)
            for kind in (1, 2, 0, 3, 4):
                first_col = (0, 2, 3, 4, 5)[kind] * half + head * DK
                window = pre_ref[
                    pl.ds(pl.multiple_of(block * STRETCH, STRETCH), STRETCH + PAD), first_col : first_col + DK
                ]
                value = conv_window(window, conv_ref[kind, :, cols], same)
                value = value * jax.nn.sigmoid(value)
                if kind < 3:
                    value = value * lax.rsqrt(jnp.sum(value * value, axis=-1, keepdims=True) + 1e-06)
                if kind == 0:
                    q_ref[rows, cols] = value * DK ** (-0.5)
                elif kind < 3:
                    k_ref[kind - 1, rows, cols] = value.astype(BF)
                else:
                    v_ref[kind - 3, rows, cols] = value.astype(BF)
        aux2, run2, aux_t, run_t = block_scalars(aux)
        mats = []
        for head in range(heads):
            cols = slice(head * DK, (head + 1) * DK)
            beta, run_col, run_row, doc_col, doc_row, carried, to_last = head_terms(
                aux, aux2, run2, aux_t, run_t, head, heads
            )
            decay = decay_matrix(run_col, run_row, doc_col, doc_row, p_row, p_col)
            keys = keys_of(rows, cols)
            gram = dot1(keys, keys, NT)
            mats.append(beta * jnp.where(p_row > p_col, decay * gram, 0.0))
            attn[block * heads + head] = decay[STRETCH:] * dot3(q_ref[rows, cols], keys, NT)
        return mats

    def prepare(turn, carry):
        mats = []
        for i in range(together):
            mats += prepare_block(turn * together + i)
        for i, inv in enumerate(inverse(mats, masks)):
            inv_ref[turn * together * heads + i] = inv
        run_slot(slots[: blocks // together], turn)
        return carry

    lax.fori_loop(0, blocks // together, prepare, 0)
    for head in range(heads):
        state_ref[head] = jnp.zeros((DK, DK), F32)

    def advance(block, carry):
        rows = pl.ds(pl.multiple_of(block * STRETCH, STRETCH), STRETCH)
        aux = aux_ref[rows, :]
        aux2, run2, aux_t, run_t = block_scalars(aux)
        for head in range(heads):
            cols = slice(head * DK, (head + 1) * DK)
            beta, run_col, run_row, doc_col, doc_row, carried, to_last = head_terms(
                aux, aux2, run2, aux_t, run_t, head, heads
            )
            keys = keys_of(rows, cols)
            values = jnp.concatenate([v_ref[0, rows, cols], v_ref[1, rows, cols]], axis=0).astype(F32)
            state = state_ref[block * heads + head]
            state_parts = split(state)
            target = beta * (values - carried * dot3(keys, state_parts))
            pseudo = dot3(inv_ref[block * heads + head], target)
            pseudo_ref[block * heads + head] = pseudo
            mixed = carried[STRETCH:] * dot3(q_ref[rows, cols], state_parts) + dot3(
                attn[block * heads + head], pseudo
            )
            state_ref[(block + 1) * heads + head] = carried[span - 1 : span] * state + dot3(
                keys, to_last * pseudo, TN
            )
            mixed_ref[rows, cols] = mixed
            scale = lax.rsqrt(jnp.mean(mixed * mixed, axis=-1, keepdims=True) + 1e-05)
            gate = pre_ref[
                pl.ds(pl.multiple_of(block * STRETCH, STRETCH) + PAD, STRETCH),
                half + head * DK : half + (head + 1) * DK,
            ]
            gated_ref[rows, cols] = (mixed * scale * mix_ref[...] * (gate * jax.nn.sigmoid(gate))).astype(BF)
        run_slot(slots[blocks // together :], block)
        return carry

    lax.fori_loop(0, blocks, advance, 0)
    for part in range(4):
        second.ready(part)
    for swap in swaps:
        swap.wait_send()
    for part in range(3):
        first.drain(part)
    for part in range(4):
        second.drain(part)
    keep_front.wait()


def front_call(line, x, docs, norm, wq, wg, wk, wv, scal, rest, rates, cq, ck, cv, mix):
    seq, half = x.shape[0], wq.shape[1]
    depth, tail = rest.shape
    heads, blocks = half // DK, seq // STRETCH
    units, span = heads * blocks, 2 * STRETCH
    width = 6 * half + DK
    shape = jax.ShapeDtypeStruct
    anywhere = pl.BlockSpec(memory_space=pl.ANY)
    dma = pltpu.SemaphoreType.DMA
    return pl.pallas_call(
        functools.partial(front_kernel, line, heads),
        out_shape=(
            shape((seq, half), BF),
            shape((seq, half), F32),
            shape((units, span, span), F32),
            shape((units + heads, DK, DK), F32),
            shape((units, span, DK), F32),
            shape((seq + PAD, width), F32),
            shape((seq, half), F32),
            shape((2, seq, half), BF),
            shape((2, seq, half), BF),
            shape((seq, DK), F32),
            shape((5, KW, half), F32),
            shape((4 * line, depth, width), BF),
            shape((4 * line, depth, tail), BF),
        ),
        in_specs=[VMEM] * 8 + [anywhere] + [VMEM] * 5,
        out_specs=(VMEM,) * 11 + (anywhere,) * 2,
        scratch_shapes=[
            pltpu.VMEM((4 * line, depth, width), BF),
            pltpu.VMEM(x.shape, BF),
            pltpu.VMEM((seq + PAD, DK), F32),
            pltpu.VMEM((units, STRETCH, span), F32),
            pltpu.VMEM((depth, DK), BF),
            dma((2,)),
            dma((5,)),
            dma((5,)),
        ]
        + gather_sems(line, 3)
        + gather_sems(line, 4),
        compiler_params=pltpu.CompilerParams(
            collective_id=0, has_side_effects=True, vmem_limit_bytes=56 << 20
        ),
        name="front",
    )(x, docs, norm, wq, wg, wk, wv, scal, rest, rates, cq, ck, cv, mix)


CHUNK = 128


def chunk_rows(index):
    return pl.ds(pl.multiple_of(index * CHUNK, CHUNK), CHUNK)


def flat(ref, start, width):
    return ref[:, :, start : start + width].reshape(-1, width)


def put_blocks(ref, index, cols, value):
    depth = ref.shape[3]
    count = DK // depth
    value = value.astype(BF)
    if count == 2:
        ref[index // 2, index % 2, :, :, cols] = value.reshape(2, depth, value.shape[-1])
    else:
        ref[pl.ds(index * (count // 4), count // 4), :, :, :, cols] = value.reshape(
            count // 4, 2, 2, depth, value.shape[-1]
        )


def ffn_kernel(
    line, gated_ref, x_ref, cot_ref, weight_ref, gain_ref, w_ref,
    middle_ref, back_ref, dgated_ref, part_ref, grad_ref, dgain_ref,
    attn_own, attn_in, in_own, in_in, normed, seed_low, hidden, gu_back, attn_back,
    a_send, a_recv, f_send, f_recv,
):
    place = Place(line)
    place.enter(plane=False)
    seq, width = x_ref.shape
    half = gated_ref.shape[1]
    ff = (w_ref.shape[-1] - half) // 3
    chunks = seq // CHUNK
    gate_up = (half, 2 * ff)
    down = (half + 2 * ff, ff)

    def attn_copy(index):
        rows = chunk_rows(index)
        return remote(attn_own.at[rows], attn_in.at[rows], a_send.at[index], a_recv.at[index], place.peer)

    def in_copy(index):
        rows = chunk_rows(index)
        return remote(in_own.at[rows], in_in.at[rows], f_send.at[index], f_recv.at[index], place.peer)

    def project(index, carry):
        rows = chunk_rows(index)
        attn_own[rows, :] = product(gated_ref[rows, :], flat(w_ref, 0, half), NT).astype(BF)
        attn_copy(index).start()
        return carry

    lax.fori_loop(0, chunks, project, 0)
    dgain_ref[...] = jnp.zeros_like(dgain_ref)

    def feed(index, carry):
        rows = chunk_rows(index)
        attn_copy(index).wait_recv()
        middle = x_ref[rows, :].astype(F32) + (attn_own[rows, :].astype(F32) + attn_in[rows, :].astype(F32))
        middle_ref[rows, :] = middle
        scale = lax.rsqrt(jnp.mean(middle * middle, axis=-1, keepdims=True) + 1e-06)
        low = (middle * scale * gain_ref[...]).astype(BF)
        normed[rows, :] = low
        both = product(low, flat(w_ref, *gate_up))
        gate_in, up_in = both[:, :ff], both[:, ff:]
        sigmoid = jax.nn.sigmoid(gate_in)
        silu = gate_in * sigmoid
        seed = (cot_ref[rows, :].astype(F32) * weight_ref[...]).astype(BF)
        seed_low[rows, :] = seed
        hidden_back = product(seed, flat(w_ref, *down))
        gate_back = (hidden_back * up_in * (sigmoid * (1.0 + gate_in * (1.0 - sigmoid)))).astype(BF)
        up_back = (hidden_back * silu).astype(BF)
        gu_back[rows, 0:ff] = gate_back
        gu_back[rows, ff : 2 * ff] = up_back
        in_own[rows, :] = product(gu_back[rows, :], flat(w_ref, *gate_up), NT).astype(BF)
        in_copy(index).start()
        low_hidden = (silu * up_in).astype(BF)
        hidden[rows, :] = low_hidden
        part_ref[rows, :] = product(low_hidden, flat(w_ref, *down), NT).astype(BF)
        return carry

    lax.fori_loop(0, chunks, feed, 0)

    def weigh(index, carry):
        cols = pl.ds(pl.multiple_of(index * DK, DK), DK)
        put_blocks(grad_ref, index, slice(half + 2 * ff, half + 3 * ff), product(seed_low[:, cols], hidden[...], TN))
        put_blocks(grad_ref, index, slice(half, half + 2 * ff), product(normed[:, cols], gu_back[...], TN))
        return carry

    lax.fori_loop(0, width // DK, weigh, 0)

    def finish(index, carry):
        rows = chunk_rows(index)
        in_copy(index).wait_recv()
        grad = in_own[rows, :].astype(F32) + in_in[rows, :].astype(F32)
        middle = middle_ref[rows, :]
        scale = lax.rsqrt(jnp.mean(middle * middle, axis=-1, keepdims=True) + 1e-06)
        unit = middle * scale
        dgain_ref[...] += jnp.sum(grad * unit, axis=0, keepdims=True)
        grad = grad * gain_ref[...]
        seed = cot_ref[rows, :].astype(F32) * weight_ref[...]
        total = seed + scale * (grad - unit * jnp.mean(unit * grad, axis=-1, keepdims=True))
        back_ref[rows, :] = total
        low = total.astype(BF)
        attn_back[rows, :] = low
        dgated_ref[rows, :] = product(low, flat(w_ref, 0, half))
        return carry

    lax.fori_loop(0, chunks, finish, 0)

    def weigh_out(index, carry):
        cols = pl.ds(pl.multiple_of(index * DK, DK), DK)
        put_blocks(grad_ref, index, slice(0, half), product(attn_back[:, cols], gated_ref[...], TN))
        return carry

    lax.fori_loop(0, width // DK, weigh_out, 0)

    def sent(index, carry):
        attn_copy(index).wait_send()
        in_copy(index).wait_send()
        return carry

    lax.fori_loop(0, chunks, sent, 0)


def ffn_call(line, gated, x, cot, weight, gain, w):
    seq, width = x.shape
    half = gated.shape[1]
    devices, depth, tail = w.shape
    ff = (tail - half) // 3
    shape = jax.ShapeDtypeStruct
    dma = pltpu.SemaphoreType.DMA
    chunks = seq // CHUNK
    low = pltpu.VMEM((seq, width), BF)
    return pl.pallas_call(
        functools.partial(ffn_kernel, line),
        out_shape=(
            shape((seq, width), F32),
            shape((seq, width), F32),
            shape((seq, half), F32),
            shape((seq, width), BF),
            shape((line, 2, 2, depth, tail), BF),
            shape((1, width), F32),
        ),
        in_specs=[VMEM] * 6,
        out_specs=(VMEM,) * 6,
        scratch_shapes=[low] * 6
        + [pltpu.VMEM((seq, ff), BF), pltpu.VMEM((seq, 2 * ff), BF), low]
        + [dma((chunks,))] * 4,
        compiler_params=pltpu.CompilerParams(
            collective_id=1, has_side_effects=True, vmem_limit_bytes=56 << 20
        ),
        name="feed_forward",
    )(gated, x, cot, weight, gain, w)


def scatter_sems(line, parts):
    dma = pltpu.SemaphoreType.DMA
    return [dma((2, parts))] * 4 + [dma((parts,))] * 2 + [dma((2, line, parts))] * 2


def scatter_scratch(line, depth, width, own):
    slots = [pltpu.VMEM((2, line, depth, width), BF), pltpu.VMEM((line, depth, width), BF),
             pltpu.VMEM((2, line, depth, width), BF)]
    return slots + ([pltpu.VMEM((2, line, depth, width), BF)] if own else [])


class Scatter:
    def __init__(self, place, grad, out, cuts, slots, sems, own=None):
        self.place, self.grad, self.out, self.cuts, self.own = place, grad, out, cuts, own
        self.mid, self.far, self.path = slots
        self.cs, self.cr, self.ls, self.lr, self.xs, self.xr, self.zs, self.zr = sems

    def cols(self, part):
        start, width = self.cuts[part]
        return pl.ds(start, width)

    def column(self, which):
        return 1 - self.place.x if which == 0 else self.place.x

    def sibling_copy(self, part, which):
        place, cols, x = self.place, self.cols(part), self.column(which)
        return remote(
            self.grad.at[:, x, 1 - place.c, :, cols], self.mid.at[which, :, :, cols],
            self.cs.at[which, part], self.cr.at[which, part], place.sibling,
        )

    def own_copy(self, part, which):
        cols, x = self.cols(part), self.column(which)
        return pltpu.make_async_copy(
            self.grad.at[:, x, self.place.c, :, cols], self.own.at[which, :, :, cols], self.ls.at[which, part]
        )

    def across_copy(self, part):
        cols = self.cols(part)
        return remote(
            self.mid.at[0, :, :, cols], self.far.at[:, :, cols], self.xs.at[part], self.xr.at[part], self.place.across
        )

    def line_copy(self, part, way, target):
        cols = self.cols(part)
        ref = self.path.at[way, target, :, cols]
        return remote(
            self.mid.at[1, target, :, cols], ref,
            self.zs.at[way, target, part], self.zr.at[way, target, part], self.place.ahead[way],
        )

    def pass_copy(self, part, way, target):
        cols = self.cols(part)
        ref = self.path.at[way, target, :, cols]
        return remote(
            ref, ref, self.zs.at[way, target, part], self.zr.at[way, target, part], self.place.ahead[way]
        )

    def begin(self, part):
        for which in (0, 1):
            if self.own is not None:
                self.own_copy(part, which).start()
            self.sibling_copy(part, which).start()

    def merge(self, part, which):
        self.sibling_copy(part, which).wait_recv()
        if self.own is not None:
            self.own_copy(part, which).wait()
        cols = self.cols(part)
        for target in range(self.place.line):
            if self.own is not None:
                mine = self.own[which, target, :, cols]
            else:
                mine = self.grad[target, self.column(which), self.place.c, :, cols]
            both = self.mid[which, target, :, cols].astype(F32) + mine.astype(F32)
            self.mid[which, target, :, cols] = both.astype(BF)
        if which == 0:
            self.across_copy(part).start()

    def join(self, part):
        self.across_copy(part).wait_recv()
        cols = self.cols(part)
        for target in range(self.place.line):
            both = self.mid[1, target, :, cols].astype(F32) + self.far[target, :, cols].astype(F32)
            self.mid[1, target, :, cols] = both.astype(BF)

    def relay(self, part, way, target):
        place, cols = self.place, self.cols(part)
        ahead = target > place.z if way == 0 else target < place.z
        first = place.z == 0 if way == 0 else place.z == place.line - 1

        def start():
            self.line_copy(part, way, target).start()

        def go_on():
            self.pass_copy(part, way, target).wait_recv()
            both = self.path[way, target, :, cols].astype(F32) + self.mid[1, target, :, cols].astype(F32)
            self.path[way, target, :, cols] = both.astype(BF)
            self.pass_copy(part, way, target).start()

        pl.when(ahead & first)(start)
        pl.when(ahead & jnp.logical_not(first))(go_on)

    def relays(self, part, distance):
        self.relay(part, 0, self.place.line - 1 - distance)
        self.relay(part, 1, distance)

    def end(self, part):
        place, cols = self.place, self.cols(part)
        start, width = self.cuts[part]
        z = place.z
        self.out[:, cols] = self.mid[1, z, :, cols].astype(F32)

        def take(way):
            self.pass_copy(part, way, z).wait_recv()
            self.out[:, cols] += self.path[way, z, :, cols].astype(F32)

        pl.when(z > 0)(functools.partial(take, 0))
        pl.when(z < place.line - 1)(functools.partial(take, 1))

    def drain(self, part):
        place = self.place
        for which in (0, 1):
            self.sibling_copy(part, which).wait_send()
        self.across_copy(part).wait_send()
        for target in range(place.line):
            for way in (0, 1):
                ahead = target > place.z if way == 0 else target < place.z
                pl.when(ahead)(lambda way=way, target=target: self.pass_copy(part, way, target).wait_send())

    def stages(self, part):
        line = self.place.line
        return [functools.partial(self.join, part)] + [
            functools.partial(self.relays, part, distance) for distance in range(line - 1)
        ]


def back_kernel(
    line, heads, q_ref, k_ref, v_ref, aux_ref, pre_ref, docs_ref, conv_ref, rates_ref, mix_ref, mixed_ref, inv_ref,
    state_ref, pseudo_ref, dgated_ref, middle_ref, part_ref, grad_ref,
    dpre_ref, dconv_ref, dscal_ref, dgain_ref, sum_ref, out_ref,
    dstate, doc_cols, dy_next, part_in, mid, far, path, own, o_send, o_recv, *sems,
):
    place = Place(line)
    side = place.side
    place.enter()
    seq, half = q_ref.shape
    blocks = seq // STRETCH
    span = 2 * STRETCH
    tail = sum_ref.shape[-1]
    ff = (tail - half) // 3
    cuts = [(half, ff), (half + ff, ff), (half + 2 * ff, ff), (0, half)]
    scatter = Scatter(place, grad_ref, sum_ref, cuts, (mid, far, path), sems, own)
    parts = range(len(cuts))
    for part in parts:
        scatter.begin(part)
    swap = remote(part_ref, part_in, o_send, o_recv, place.peer)
    swap.start()

    masks = block_masks()
    t_row, t_col, p_row, p_col = masks
    strict = p_row > p_col
    for head in range(heads):
        dstate[head] = jnp.zeros((DK, DK), F32)
    dgain_ref[...] = jnp.zeros_like(dgain_ref)
    dconv_ref[...] = jnp.zeros_like(dconv_ref)
    dscal_ref[...] = jnp.zeros_like(dscal_ref)
    dy_next[...] = jnp.zeros_like(dy_next)
    doc_cols[0:PAD, :] = jnp.full((PAD, DK), -1.0, F32)
    doc_cols[PAD + seq :, :] = jnp.full((PAD, DK), -1.0, F32)
    for i in range(seq // DK):
        lane_docs = docs_ref[:, i * DK : (i + 1) * DK].astype(F32)
        doc_cols[PAD + i * DK : PAD + (i + 1) * DK, :] = jnp.broadcast_to(lane_docs, (DK, DK)).T
    upper = (iota((STRETCH, STRETCH), 0) <= iota((STRETCH, STRETCH), 1)).astype(F32)
    lanes = iota((STRETCH, DK), 1)
    wide_rows = iota((span, DK), 0)
    select = scalar_select(side, heads)
    rate = -jnp.exp(rates_ref[0:1, :])
    scal_at = 6 * half
    scal_cols = slice(scal_at, scal_at + DK)

    work = [functools.partial(scatter.merge, part, which) for part in parts for which in (0, 1)]
    chain = [step for part in parts for step in scatter.stages(part) + [functools.partial(scatter.end, part)]]
    slots = deal(work, 2) + [[]] + deal(chain[: len(chain) * 2 // 3], blocks - 3)
    left = chain[len(chain) * 2 // 3 :]

    def back(step, carry):
        block = blocks - 1 - step
        top = pl.multiple_of(block * STRETCH, STRETCH)
        rows = pl.ds(top, STRETCH)
        aux = aux_ref[rows, :]
        aux2, run2, aux_t, run_t = block_scalars(aux)
        doc_window = doc_cols[pl.ds(top, STRETCH + 2 * PAD), :]
        same = same_documents(doc_window[: STRETCH + PAD])
        here = doc_window[PAD : PAD + STRETCH]
        same_next = [doc_window[PAD + o : PAD + o + STRETCH] == here for o in range(1, KW)]
        dbeta_all = jnp.zeros((STRETCH, DK), F32)
        drun_all = jnp.zeros((STRETCH, DK), F32)
        column_sums = jnp.zeros((span, DK), F32)

        def conv_back(kind, head, grad):
            first_col = (0, 2, 3, 4, 5)[kind] * half + head * DK
            cols = slice(head * DK, (head + 1) * DK)
            window = pre_ref[pl.ds(top, STRETCH + PAD), first_col : first_col + DK]
            kernel = conv_ref[kind, :, cols]
            shifted = [window[PAD:]] + [
                jnp.where(same[o - 1], window[PAD - o : PAD - o + STRETCH], 0.0) for o in range(1, KW)
            ]
            y = shifted[0] * kernel[0:1]
            for o in range(1, KW):
                y = y + shifted[o] * kernel[o : o + 1]
            sigmoid = jax.nn.sigmoid(y)
            act = y * sigmoid
            if kind < 3:
                scale = lax.rsqrt(jnp.sum(act * act, axis=-1, keepdims=True) + 1e-06)
                unit = act * scale
                if kind == 0:
                    grad = grad * DK ** (-0.5)
                grad = scale * (grad - unit * jnp.sum(unit * grad, axis=-1, keepdims=True))
            dy = grad * (sigmoid * (1.0 + y * (1.0 - sigmoid)))
            for o in range(KW):
                dconv_ref[kind, o : o + 1, cols] += jnp.sum(dy * shifted[o], axis=0, keepdims=True)
            at = slice(kind * half + head * DK, kind * half + (head + 1) * DK)
            longer = jnp.concatenate([dy, dy_next[:, at]], axis=0)
            dy_next[:, at] = dy[:PAD]
            dpre = dy * kernel[0:1]
            for o in range(1, KW):
                dpre = dpre + jnp.where(same_next[o - 1], longer[o : o + STRETCH], 0.0) * kernel[o : o + 1]
            dpre_ref[rows, first_col : first_col + DK] = dpre.astype(BF)

        for head in range(heads):
            cols = slice(head * DK, (head + 1) * DK)
            gate_cols = slice(half + head * DK, half + (head + 1) * DK)
            beta, run_col, run_row, doc_col, doc_row, carried, to_last = head_terms(
                aux, aux2, run2, aux_t, run_t, head, heads
            )
            decay = decay_matrix(run_col, run_row, doc_col, doc_row, p_row, p_col)
            keys = jnp.concatenate([k_ref[0, rows, cols], k_ref[1, rows, cols]], axis=0)
            queries = q_ref[rows, cols]
            mixed = mixed_ref[rows, cols]
            gate = pre_ref[pl.ds(top + PAD, STRETCH), gate_cols]
            sigmoid = jax.nn.sigmoid(gate)
            silu = gate * sigmoid
            scale = lax.rsqrt(jnp.mean(mixed * mixed, axis=-1, keepdims=True) + 1e-05)
            scaled = mixed * scale
            dgated = dgated_ref[rows, cols]
            part = dgated * scaled
            dpre_ref[rows, gate_cols] = (
                part * mix_ref[...] * (sigmoid * (1.0 + gate * (1.0 - sigmoid)))
            ).astype(BF)
            dgain_ref[...] += jnp.sum(part * silu, axis=0, keepdims=True)
            dscaled = dgated * mix_ref[...] * silu
            dout = scale * (dscaled - scaled * jnp.mean(dscaled * scaled, axis=-1, keepdims=True))

            index = block * heads + head
            state, pseudo = state_ref[index], pseudo_ref[index]
            dnext = dstate[head]
            dnext_parts, state_parts, pseudo_parts = split(dnext), split(state), split(pseudo)
            dout_parts, q_parts = split(dout), split(queries)
            gram = dot1(keys, keys, NT)
            core = jnp.where(strict, decay * gram, 0.0)
            amat = beta * core
            qdecay = decay[STRETCH:]
            attn = qdecay * dot3(q_parts, keys, NT)
            dattn = dot3(dout_parts, pseudo_parts, NT)
            dqk = split(qdecay * dattn)
            dpseudo = dot3(attn, dout_parts, TN) + to_last * dot3(keys, dnext_parts)
            dtarget = dot3(inv_ref[index], dpseudo, TN)
            dtarget_parts = split(dtarget)
            damat = jnp.where(strict, -dot3(dtarget_parts, pseudo_parts, NT), 0.0)
            e_a, e_m = damat * amat, dattn * attn
            dgram = split(beta * decay * damat)
            dbeta = jnp.sum(dtarget * pseudo, axis=-1, keepdims=True) / jnp.maximum(beta, 1e-30)
            dvalues = (beta * dtarget).astype(BF).astype(F32)
            dread = -(beta * carried) * dtarget
            dout_c = carried[STRETCH:] * dout
            dread_parts, dout_c_parts = split(dread), split(dout_c)
            last = carried[span - 1 : span]
            dstate[head] = last * dnext + dot3(keys, dread_parts, TN) + dot3(q_parts, dout_c_parts, TN)
            dq_state = dot3(dout_c_parts, state_parts, NT)
            dk_state = dot3(dread_parts, state_parts, NT)
            dk_last = dot3(to_last * pseudo, dnext_parts, NT)
            conv_back(0, head, dq_state + dot3(dqk, keys))
            dkeys = (
                dk_state + dk_last + dot3(dgram, keys) + dot3(dgram, keys, TN) + dot3(dqk, q_parts, TN)
            ).astype(BF).astype(F32)
            conv_back(1, head, dkeys[:STRETCH])
            conv_back(2, head, dkeys[STRETCH:])
            conv_back(3, head, dvalues[:STRETCH])
            conv_back(4, head, dvalues[STRETCH:])

            wide = keys.astype(F32)
            e_last = jnp.sum(wide * dk_last, axis=-1, keepdims=True)
            drun = jnp.sum(e_a, axis=-1, keepdims=True) - e_last + jnp.sum(wide * dk_state, axis=-1, keepdims=True)
            drun_q = jnp.sum(e_m, axis=-1, keepdims=True) + jnp.sum(queries * dq_state, axis=-1, keepdims=True)
            at_last = jnp.sum(e_last, axis=0, keepdims=True) + last * jnp.sum(
                jnp.sum(dnext * state, axis=-1, keepdims=True), axis=0, keepdims=True
            )
            drun = drun[:STRETCH] + drun[STRETCH:] + drun_q
            drun = drun + jnp.where(iota((STRETCH, 1), 0) == STRETCH - 1, at_last, 0.0)
            lane = 2 * heads + head
            drun_all = jnp.where(lanes == lane, drun, drun_all)
            dbeta_all = jnp.where(lanes == head, dbeta[:STRETCH], dbeta_all)
            dbeta_all = jnp.where(lanes == heads + head, dbeta[STRETCH:], dbeta_all)
            sums = jnp.sum(e_a, axis=0, keepdims=True) + jnp.sum(e_m, axis=0, keepdims=True)
            column_sums = jnp.where(wide_rows == lane, sums, column_sums)
        down = column_sums.T
        ddecay = dot6(upper, drun_all - down[:STRETCH] - down[STRETCH:])
        raw = dot6(pre_ref[pl.ds(top + PAD, STRETCH), scal_cols], select)
        sigmoid = jax.nn.sigmoid(raw)
        shifted = raw + rates_ref[1:2, :]
        draw_decay = ddecay * rate * jax.nn.sigmoid(shifted)
        is_decay = (lanes >= 2 * heads) & (lanes < 3 * heads)
        draw_decay = jnp.where(is_decay, draw_decay, 0.0)
        dscal_ref[0:1, :] += jnp.sum(
            jnp.where(is_decay, ddecay * rate * softplus(shifted), 0.0), axis=0, keepdims=True
        )
        dscal_ref[1:2, :] += jnp.sum(draw_decay, axis=0, keepdims=True)
        dbeta_low = dbeta_all.astype(BF).astype(F32)
        draw = jnp.where(lanes < 2 * heads, dbeta_low * 2.0 * sigmoid * (1.0 - sigmoid), draw_decay)
        dpre_ref[rows, scal_cols] = dot6(draw, select, NT).astype(BF)
        run_slot(slots, step)
        return carry

    lax.fori_loop(0, blocks, back, 0)
    swap.wait_recv()

    def outputs(block, carry):
        rows = pl.ds(pl.multiple_of(block * STRETCH, STRETCH), STRETCH)
        total = part_ref[rows, :].astype(F32) + part_in[rows, :].astype(F32)
        out_ref[rows, :] = (middle_ref[rows, :] + total).astype(BF)
        return carry

    lax.fori_loop(0, blocks, outputs, 0)
    for step in left:
        step()
    swap.wait_send()
    for part in parts:
        scatter.drain(part)


def back_call(line, q, k, v, aux, pre, docs, conv, rates, mix, mixed, inv, state, pseudo, dgated, middle, part, grad):
    seq, half = q.shape
    heads = half // DK
    depth, tail = grad.shape[3:]
    shape = jax.ShapeDtypeStruct
    dma = pltpu.SemaphoreType.DMA
    return pl.pallas_call(
        functools.partial(back_kernel, line, heads),
        out_shape=(
            shape((seq, pre.shape[1]), BF),
            shape(conv.shape, F32),
            shape((2, DK), F32),
            shape((1, DK), F32),
            shape((depth, tail), F32),
            shape(part.shape, BF),
        ),
        in_specs=[VMEM] * 16 + [pl.BlockSpec(memory_space=pl.ANY)],
        out_specs=(VMEM,) * 6,
        scratch_shapes=[
            pltpu.VMEM((heads, DK, DK), F32),
            pltpu.VMEM((seq + 2 * PAD, DK), F32),
            pltpu.VMEM((PAD, 5 * half), F32),
            pltpu.VMEM(part.shape, BF),
        ]
        + scatter_scratch(line, depth, tail, True)
        + [dma, dma]
        + scatter_sems(line, 4),
        compiler_params=pltpu.CompilerParams(
            collective_id=2, has_side_effects=True, vmem_limit_bytes=60 << 20
        ),
        name="mixer_backward",
    )(q, k, v, aux, pre, docs, conv, rates, mix, mixed, inv, state, pseudo, dgated, middle, part, grad)


def tail_kernel(
    line, heads, x_ref, norm_ref, dpre_ref, w_ref, back_ref, dconv_ref, dscal_ref, dmix_ref, dffn_ref,
    out_ref, gq_ref, gg_ref, gk_ref, gv_ref, gs_ref, gcq_ref, gck_ref, gcv_ref, gnorm_ref, gffn_ref, gtiny_ref,
    normed, nb_own, nb_in, grad, total, mid, far, path, small, small_in, small_line, small_sum, mix_in, scal_in,
    n_send, n_recv, h_send, h_recv, m_send, m_recv, l_send, l_recv, *sems,
):
    place = Place(line)
    side, me = place.side, place.dp
    place.enter(everyone=True)
    seq, width = x_ref.shape
    half = gq_ref.shape[1]
    chunks = seq // CHUNK
    scal_at = 6 * half
    mix_swap = remote(dmix_ref, mix_in, m_send.at[2], m_recv.at[2], place.peer)
    mix_swap.start()

    def normalise(index, carry):
        rows = chunk_rows(index)
        x = x_ref[rows, :].astype(F32)
        scale = lax.rsqrt(jnp.mean(x * x, axis=-1, keepdims=True) + 1e-06)
        normed[rows, :] = (x * scale * norm_ref[...]).astype(BF)
        return carry

    lax.fori_loop(0, chunks, normalise, 0)

    def weigh(index, carry):
        cols = pl.ds(pl.multiple_of(index * DK, DK), DK)
        put_blocks(grad, index, slice(0, scal_at + DK), product(normed[:, cols], dpre_ref[...], TN))
        return carry

    lax.fori_loop(0, width // DK, weigh, 0)
    cuts = [(2 * half, 2 * half), (4 * half, 2 * half + DK), (0, 2 * half)]
    scatter = Scatter(place, grad, total, cuts, (mid, far, path), sems)
    parts = range(len(cuts))
    for part in parts:
        scatter.begin(part)

    def nb_copy(index):
        rows = chunk_rows(index)
        return remote(nb_own.at[rows], nb_in.at[rows], n_send.at[index], n_recv.at[index], place.peer)

    merges = [functools.partial(scatter.merge, part, which) for part in parts for which in (0, 1)]
    merge_slots = deal(merges, chunks)

    def project(index, carry):
        rows = chunk_rows(index)
        nb_own[rows, :] = product(dpre_ref[rows, :], flat(w_ref, 0, scal_at + DK), NT).astype(BF)
        nb_copy(index).start()
        run_slot(merge_slots, index)
        return carry

    lax.fori_loop(0, chunks, project, 0)
    gnorm_ref[...] = jnp.zeros_like(gnorm_ref)

    def finish(index, carry):
        rows = chunk_rows(index)
        nb_copy(index).wait_recv()
        back = nb_own[rows, :].astype(F32) + nb_in[rows, :].astype(F32)
        x = x_ref[rows, :].astype(F32)
        scale = lax.rsqrt(jnp.mean(x * x, axis=-1, keepdims=True) + 1e-06)
        unit = x * scale
        gnorm_ref[...] += jnp.sum(back * unit, axis=0, keepdims=True)
        back = back * norm_ref[...]
        total_back = back_ref[rows, :] + scale * (back - unit * jnp.mean(unit * back, axis=-1, keepdims=True))
        out_ref[rows, :] = total_back.astype(BF)
        return carry

    small_swaps = [
        remote(small, small_in.at[0], m_send.at[0], m_recv.at[0], place.sibling),
        remote(small_sum, small_in.at[1], m_send.at[1], m_recv.at[1], place.across),
    ]

    def line_copy(target):
        device = (target * 4 + place.x * 2 + place.c, side)
        return remote(small_line.at[place.z], small_line.at[place.z], l_send.at[target], l_recv.at[place.z], device)

    def line_from(source):
        device = (source * 4 + place.x * 2 + place.c, side)
        return remote(small_line.at[source], small_line.at[source], l_send.at[source], l_recv.at[source], device)

    def collect():
        mix_swap.wait_recv()
        small[0:5] = dconv_ref[...]
        for i in range(2):
            small[5, i : i + 1, :] = gnorm_ref[:, i * half : (i + 1) * half]
            small[5, 2 + i : 3 + i, :] = dffn_ref[:, i * half : (i + 1) * half]
        small[6] = jnp.zeros((KW, half), F32)
        small[6, 0:1, 0:DK] = dmix_ref[...] + mix_in[...]
        small[6, 0:1, DK : 2 * DK] = dscal_ref[0:1, :]
        small[6, 0:1, 2 * DK : 3 * DK] = dscal_ref[1:2, :]
        small_swaps[0].start()

    def collect_across():
        small_swaps[0].wait_recv()
        small_sum[...] = small[...] + small_in[0]
        small_swaps[1].start()

    def collect_line():
        small_swaps[1].wait_recv()
        small_line[place.z] = small_sum[...] + small_in[1]
        for target in range(line):
            pl.when(target != place.z)(lambda target=target: line_copy(target).start())

    home = [
        remote(
            total.at[:, pl.ds(pl.multiple_of((base + 1 - side) * half, half), half)],
            ref.at[:, pl.ds(pl.multiple_of(side * half, half), half)],
            h_send.at[i], h_recv.at[i], place.peer,
        )
        for i, (base, ref) in enumerate(((2, gk_ref), (4, gv_ref)))
    ]
    scal_home = remote(total.at[:, scal_at : scal_at + DK], scal_in, h_send.at[2], h_recv.at[2], place.peer)
    own_half = pl.ds(pl.multiple_of(side * half, half), half)

    def at_home(i):
        base, ref = ((2, gk_ref), (4, gv_ref))[i]
        home[i].start()
        ref[:, own_half] = total[:, pl.ds(pl.multiple_of((base + side) * half, half), half)]

    def at_home_value():
        at_home(1)
        scal_home.start()

    chain = []
    for part in parts:
        chain += scatter.stages(part) + [functools.partial(scatter.end, part)]
        if part == 0:
            chain.append(functools.partial(at_home, 0))
        if part == 1:
            chain.append(at_home_value)
    mid_way = len(scatter.stages(0)) + 2
    slots = deal(chain[:mid_way], chunks)

    def finish_and(index, carry):
        finish(index, carry)
        run_slot(slots, index)
        return carry

    lax.fori_loop(0, chunks, finish_and, 0)
    rest = chain[mid_way:]
    extra = [collect, collect_across, collect_line]
    for i, step in enumerate(rest):
        if i % 2 == 0 and extra:
            extra.pop(0)()
        step()
    for step in extra:
        step()
    for source in range(line):
        pl.when(source != place.z)(lambda source=source: line_from(source).wait_recv())
    summed = small_line[0]
    for source in range(1, line):
        summed = summed + small_line[source]
    small_sum_out = summed
    gcq_ref[...] = small_sum_out[0]
    small_swaps[0].wait_send()
    small_swaps[1].wait_send()
    small[...] = small_sum_out
    conv_home = [
        remote(
            small.at[base + 1 - side], ref.at[:, own_half], h_send.at[i], h_recv.at[i], place.peer
        )
        for i, (base, ref) in ((3, (1, gck_ref)), (4, (3, gcv_ref)))
    ]
    for copy in conv_home:
        copy.start()
    gck_ref[:, own_half] = small[1 + side]
    gcv_ref[:, own_half] = small[3 + side]
    for i in range(2):
        gnorm_ref[:, i * half : (i + 1) * half] = small_sum_out[5, i : i + 1]
        gffn_ref[:, i * half : (i + 1) * half] = small_sum_out[5, 2 + i : 3 + i]
    gtiny_ref[...] = small_sum_out[6, 0:1, 0 : 3 * DK]
    gq_ref[...] = total[:, 0:half]
    gg_ref[...] = total[:, half : 2 * half]
    scal_home.wait_recv()
    lanes = iota(scal_in.shape, 1)
    ours = total[:, scal_at : scal_at + DK]
    theirs = pltpu.roll(scal_in[...], DK - 2 * heads, 1)
    gs_ref[...] = jnp.where(lanes < 2 * heads, ours + theirs, ours)
    for copy in home + conv_home:
        copy.wait_recv()
    for copy in home + conv_home + [scal_home, mix_swap]:
        copy.wait_send()
    for target in range(line):
        pl.when(target != place.z)(lambda target=target: line_copy(target).wait_send())

    def sent(index, carry):
        nb_copy(index).wait_send()
        return carry

    lax.fori_loop(0, chunks, sent, 0)
    for part in parts:
        scatter.drain(part)


def tail_call(line, heads, x, norm, dpre, w, back, dconv, dscal, dmix, dffn):
    seq, width = x.shape
    devices, depth, columns = w.shape
    half = dconv.shape[-1]
    shape = jax.ShapeDtypeStruct
    dma = pltpu.SemaphoreType.DMA
    chunks = seq // CHUNK
    tiny = (7, KW, half)
    return pl.pallas_call(
        functools.partial(tail_kernel, line, heads),
        out_shape=(
            shape((seq, width), BF),
            shape((depth, half), F32),
            shape((depth, half), F32),
            shape((depth, 2 * half), F32),
            shape((depth, 2 * half), F32),
            shape((depth, DK), F32),
            shape((KW, half), F32),
            shape((KW, 2 * half), F32),
            shape((KW, 2 * half), F32),
            shape((1, width), F32),
            shape((1, width), F32),
            shape((1, 3 * DK), F32),
        ),
        in_specs=[VMEM] * 9,
        out_specs=(VMEM,) * 12,
        scratch_shapes=[
            pltpu.VMEM((seq, width), BF),
            pltpu.VMEM((seq, width), BF),
            pltpu.VMEM((seq, width), BF),
            pltpu.VMEM((line, 2, 2, depth, columns), BF),
            pltpu.VMEM((depth, columns), F32),
        ]
        + scatter_scratch(line, depth, columns, False)
        + [
            pltpu.VMEM(tiny, F32),
            pltpu.VMEM((2,) + tiny, F32),
            pltpu.VMEM((line,) + tiny, F32),
            pltpu.VMEM(tiny, F32),
            pltpu.VMEM((1, DK), F32),
            pltpu.VMEM((depth, DK), F32),
        ]
        + [dma((chunks,)), dma((chunks,)), dma((5,)), dma((5,)), dma((3,)), dma((3,)), dma((line,)), dma((line,))]
        + scatter_sems(line, 3),
        compiler_params=pltpu.CompilerParams(
            collective_id=3, has_side_effects=True, vmem_limit_bytes=56 << 20
        ),
        name="tail",
    )(x, norm, dpre, w, back, dconv, dscal, dmix, dffn)


GROUPS = 8


def per_device(
    tokens,
    cotangent,
    domains,
    doc_ids,
    norm_gain,
    w_query,
    w_outgate,
    w_key,
    w_value,
    w_beta,
    w_alpha,
    decay_log,
    decay_bias,
    conv_query,
    conv_key,
    conv_value,
    mix_gain,
    w_out,
    ffn_gain,
    w_gate,
    w_up,
    w_down,
):
    row_total = domains.shape[0]
    group_ids = lax.broadcasted_iota(jnp.int32, (row_total, GROUPS), 1)
    member = (domains[:, None] == group_ids).astype(F32)
    group_sizes = jnp.sum(member, axis=0)
    row_sizes = jnp.sum(member * group_sizes[None, :], axis=1)
    row_weights = 2.0 / (1.0 + row_sizes * (GROUPS / row_total))
    own_row = (lax.broadcasted_iota(jnp.int32, (row_total,), 0) == lax.axis_index("dp")).astype(F32)
    weight_here = jnp.sum(own_row * row_weights)

    depth = w_query.shape[0]
    half = w_query.shape[1]
    heads = w_alpha.shape[1]

    rest = jnp.concatenate([w_out.T, w_gate, w_up, w_down.T], axis=1)
    scal = jnp.concatenate(
        [w_beta[0], jnp.zeros((depth, 2 * heads), BF), w_alpha, jnp.zeros((depth, DK - 5 * heads), BF)], axis=1
    )
    rates = jnp.pad(jnp.stack([decay_log, decay_bias]), ((0, 0), (2 * heads, DK - 3 * heads)))
    gain_row = mix_gain[None]
    (gated, mixed, inv, state, pseudo, pre, queries, keys, values, aux, conv, front_w, back_w) = front_call(
        lax.axis_size("dp") // 4, tokens[0], doc_ids, norm_gain[None], w_query, w_outgate, w_key[0], w_value[0],
        scal, rest, rates, conv_query, conv_key[0], conv_value[0], gain_row,
    )
    ff = w_gate.shape[1]
    weight_row = jnp.full((1, tokens.shape[2]), weight_here, F32)
    middle, middle_back, gated_back, ffn_part, grad_back, grad_ffn_gain = ffn_call(
        lax.axis_size("dp") // 4, gated, tokens[0], cotangent[0], weight_row, ffn_gain[None], back_w
    )
    dpre_low, dconv, dscal, dgain, sum_back, output = back_call(
        lax.axis_size("dp") // 4, queries, keys, values, aux, pre, doc_ids, conv, rates, gain_row, mixed, inv, state,
        pseudo, gated_back, middle, ffn_part, grad_back,
    )
    output = output[None]
    input_grad, g_query, g_outgate, g_key, g_value, g_scal, g_cq, g_ck, g_cv, g_norm, g_ffn, tiny = tail_call(
        lax.axis_size("dp") // 4, heads, tokens[0], norm_gain[None], dpre_low, front_w, middle_back, dconv, dscal,
        dgain, grad_ffn_gain,
    )
    here = slice(2 * heads, 3 * heads)
    return (
        output,
        input_grad[None],
        g_norm[0],
        g_query,
        g_outgate,
        g_key[None],
        g_value[None],
        g_scal[None, :, : 2 * heads],
        g_scal[:, 4 * heads : 5 * heads],
        tiny[0, DK : 2 * DK][here],
        tiny[0, 2 * DK :][here],
        g_cq,
        g_ck[None],
        g_cv[None],
        tiny[0, :DK],
        sum_back[:, :half].T,
        g_ffn[0],
        sum_back[:, half : half + ff],
        sum_back[:, half + ff : half + 2 * ff],
        sum_back[:, half + 2 * ff :].T,
    )


def solution(mesh):
    return jax.shard_map(
        per_device,
        mesh=mesh,
        in_specs=(
            P("dp", None, None),
            P("dp", None, None),
            P(),
            P("dp", None),
            P(),
            P("dp", "step"),
            P("dp", "step"),
            P("step", "dp", None),
            P("step", "dp", None),
            P("step", "dp", None),
            P("dp", "step"),
            P("step"),
            P("step"),
            P(None, "step"),
            P("step", None, None),
            P("step", None, None),
            P(),
            P("step", "dp"),
            P(),
            P("dp", "step"),
            P("dp", "step"),
            P("step", "dp"),
        ),
        out_specs=(
            P("dp", None, None),
            P("dp", None, None),
            P(),
            P("dp", "step"),
            P("dp", "step"),
            P("step", "dp", None),
            P("step", "dp", None),
            P("step", "dp", None),
            P("dp", "step"),
            P("step"),
            P("step"),
            P(None, "step"),
            P("step", None, None),
            P("step", None, None),
            P(),
            P("step", "dp"),
            P(),
            P("dp", "step"),
            P("dp", "step"),
            P("step", "dp"),
        ),
        check_vma=False,
    )
```

```python
import functools

import jax
import jax.numpy as jnp
from jax import lax
from jax.experimental import pallas as pl
from jax.experimental.pallas import tpu as pltpu
from jax.sharding import PartitionSpec as P

STRETCH = 64
DK = 128
F32 = jnp.float32
BF = jnp.bfloat16
NN = ((1,), (0,))
NT = ((1,), (1,))
TN = ((0,), (0,))


def split(a):
    if a.dtype == BF:
        return (a,)
    hi = a.astype(BF)
    return (hi, (a - hi.astype(F32)).astype(BF))


def dot1(a, b, dims=NN):
    return lax.dot_general(a.astype(BF), b.astype(BF), (dims, ((), ())), preferred_element_type=F32)


def dot3(a, b, dims=NN):
    a = a if isinstance(a, tuple) else split(a)
    b = b if isinstance(b, tuple) else split(b)
    one = lambda x, y: lax.dot_general(x, y, (dims, ((), ())), preferred_element_type=F32)
    out = one(a[0], b[0])
    if len(a) > 1:
        out = out + one(a[1], b[0])
    if len(b) > 1:
        out = out + one(a[0], b[1])
    return out


def dot6(a, b, dims=NN):
    return lax.dot_general(
        a, b, (dims, ((), ())), precision=lax.Precision.HIGHEST, preferred_element_type=F32
    )


def iota(shape, dim):
    return lax.broadcasted_iota(jnp.int32, shape, dim)


def product(first, second, dims=NN):
    return lax.dot_general(first, second, (dims, ((), ())), preferred_element_type=F32)


def block_masks():
    span = 2 * STRETCH
    row, col = iota((span, span), 0), iota((span, span), 1)
    t_row, t_col = row % STRETCH, col % STRETCH
    p_row, p_col = 2 * t_row + row // STRETCH, 2 * t_col + col // STRETCH
    return t_row, t_col, p_row, p_col


def twice(block):
    return jnp.concatenate([block, block], axis=0)


def block_scalars(aux):
    low = (iota((STRETCH, STRETCH), 0) >= iota((STRETCH, STRETCH), 1)).astype(F32)
    running = dot6(low, aux)
    aux2, run2 = twice(aux), twice(running)
    return aux2, run2, aux2.T, run2.T


def head_terms(aux, aux2, run2, aux_t, run_t, head, heads):
    beta = jnp.concatenate(
        [aux[:, head : head + 1], aux[:, heads + head : heads + head + 1]], axis=0
    )
    lane = 2 * heads + head
    run_col = run2[:, lane : lane + 1]
    run_row = run_t[lane : lane + 1, :]
    doc_lane = 3 * heads
    doc_col = aux2[:, doc_lane : doc_lane + 1]
    doc_row = aux_t[doc_lane : doc_lane + 1, :]
    fresh = aux2[:, doc_lane + 1 : doc_lane + 2]
    span = 2 * STRETCH
    carried = jnp.where(fresh > 0.5, jnp.exp(run_col), 0.0)
    last_run = run_col[span - 1 : span, :]
    to_last = jnp.where(doc_col == doc_col[span - 1 : span, :], jnp.exp(last_run - run_col), 0.0)
    return beta, run_col, run_row, doc_col, doc_row, carried, to_last


def decay_matrix(run_col, run_row, doc_col, doc_row, p_row, p_col):
    inside = (p_row >= p_col) & (doc_col == doc_row)
    return jnp.where(inside, jnp.exp(jnp.where(inside, run_col - run_row, 0.0)), 0.0)


def inverse(mats, masks):
    t_row, t_col, p_row, p_col = masks
    eye = (p_row == p_col).astype(F32)
    pair = (t_row == t_col) & (p_row > p_col)
    out = [eye - jnp.where(pair, a, 0.0) for a in mats]
    level = 1
    while (1 << level) <= STRETCH:
        merge = (
            ((t_row >> level) == (t_col >> level))
            & (((t_row >> (level - 1)) & 1) == 1)
            & (((t_col >> (level - 1)) & 1) == 0)
        )
        low = [x.astype(BF) for x in out]
        half = [dot1(x, jnp.where(merge, a, 0.0)) for x, a in zip(low, mats)]
        out = [o - dot1(h, x) for o, h, x in zip(out, half, low)]
        level += 1
    rest = [eye - x - dot3(a, x) for a, x in zip(mats, out)]
    return [x + dot1(x, r) for x, r in zip(out, rest)]


VMEM = pl.BlockSpec(memory_space=pltpu.VMEM)


MESH = pl.DeviceIdType.MESH


class Place:
    def __init__(self, line):
        self.line = line
        self.dp, self.side = lax.axis_index("dp"), lax.axis_index("step")
        self.z, self.x, self.c = self.dp // 4, (self.dp // 2) % 2, self.dp % 2
        self.sibling = (self.dp + 1 - 2 * self.c, self.side)
        self.across = (self.dp + 2 - 4 * self.x, self.side)
        self.ahead = (
            (lax.rem(self.dp + 4, 4 * line), self.side),
            (lax.rem(self.dp + 4 * line - 4, 4 * line), self.side),
        )
        self.peer = (self.dp, 1 - self.side)
        self.can_send = (self.z + 1 < line, self.z > 0)

    def reaches(self, way, far):
        return self.z - far >= 0 if way == 0 else self.z + far < self.line

    def behind(self, way, far):
        return self.dp - 4 * far if way == 0 else self.dp + 4 * far

    def enter(self, plane=True, peer=True, everyone=False):
        barrier = pltpu.get_barrier_semaphore()

        def greet(device):
            pl.semaphore_signal(barrier, inc=1, device_id=device, device_id_type=MESH)

        count = 0
        if peer:
            greet(self.peer)
            count = 1
        if plane:
            greet(self.sibling)
            greet(self.across)
            count = count + 2
        if everyone:
            for z in range(self.line):
                device = (z * 4 + self.x * 2 + self.c, self.side)
                pl.when(z != self.z)(functools.partial(greet, device))
            count = count + self.line - 1
        elif plane:
            for way in (0, 1):
                pl.when(self.can_send[way])(functools.partial(greet, self.ahead[way]))
            count = count + self.can_send[0].astype(jnp.int32) + self.can_send[1].astype(jnp.int32)
        pl.semaphore_wait(barrier, count)


def remote(src, dst, send_sem, recv_sem, device):
    return pltpu.make_async_remote_copy(
        src_ref=src, dst_ref=dst, send_sem=send_sem, recv_sem=recv_sem,
        device_id=device, device_id_type=MESH,
    )


def gather_sems(line, parts):
    dma = pltpu.SemaphoreType.DMA
    return [
        dma((2, line, parts)), dma((2, line, parts)),
        dma((2, line, parts)), dma((2, line, parts)),
        dma((2, 2, line, parts)), dma((2, 2, line, parts)),
    ]


class Gather:
    def __init__(self, place, buf, cuts, sems):
        self.place, self.buf, self.cuts = place, buf, cuts
        self.zs, self.zr, self.xs, self.xr, self.cs, self.cr = sems

    def block(self, index, part):
        start, width = self.cuts[part]
        return self.buf.at[index, :, pl.ds(start, width)]

    def line_copy(self, index, way, far, part):
        ref = self.block(index, part)
        return remote(ref, ref, self.zs.at[way, far, part], self.zr.at[way, far, part], self.place.ahead[way])

    def across_copy(self, index, way, far, part):
        ref = self.block(index, part)
        return remote(ref, ref, self.xs.at[way, far, part], self.xr.at[way, far, part], self.place.across)

    def sibling_copy(self, index, column, way, far, part):
        ref = self.block(index, part)
        return remote(
            ref, ref, self.cs.at[column, way, far, part], self.cr.at[column, way, far, part], self.place.sibling
        )

    def spread(self, index, way, far, part):
        place = self.place
        for to in (0, 1) if far == 0 else (way,):
            pl.when(place.can_send[to])(lambda to=to: self.line_copy(index, to, far + 1, part).start())
        self.across_copy(index, way, far, part).start()
        self.sibling_copy(index, 0, way, far, part).start()

    def ways(self, far):
        return (0,) if far == 0 else (0, 1)

    def each(self, far, act):
        if far == 0:
            act(0)
            return
        for way in (0, 1):
            pl.when(self.place.reaches(way, far))(functools.partial(act, way))

    def step(self, far, part):
        place = self.place
        if far == 0:
            self.spread(place.dp, 0, 0, part)
            return

        def from_line(way):
            index = place.behind(way, far)
            self.line_copy(index, way, far, part).wait_recv()
            self.spread(index, way, far, part)

        def from_across(way):
            index = place.behind(way, far - 1) + 2 - 4 * place.x
            self.across_copy(index, way, far - 1, part).wait_recv()
            self.sibling_copy(index, 1, way, far - 1, part).start()

        if far < place.line:
            self.each(far, from_line)
        self.each(far - 1, from_across)

    def steps(self):
        return [
            functools.partial(self.step, far, part)
            for far in range(self.place.line + 1)
            for part in range(len(self.cuts))
        ]

    def ready(self, part):
        place = self.place
        for far in range(place.line):
            for column in (0, 1):

                def from_sibling(way):
                    index = place.behind(way, far) + 1 - 2 * place.c + column * (2 - 4 * place.x)
                    self.sibling_copy(index, column, way, far, part).wait_recv()

                self.each(far, from_sibling)

    def drain(self, part):
        place = self.place
        for far in range(place.line):

            def sent(way):
                index = place.behind(way, far)
                for to in (0, 1) if far == 0 else (way,):
                    pl.when(place.can_send[to])(
                        lambda to=to: self.line_copy(index, to, far + 1, part).wait_send()
                    )
                self.across_copy(index, way, far, part).wait_send()
                self.sibling_copy(index, 0, way, far, part).wait_send()
                self.sibling_copy(index + 2 - 4 * place.x, 1, way, far, part).wait_send()

            self.each(far, sent)


def run_slot(slots, turn):
    for index, steps in enumerate(slots):
        if steps:

            def go(steps=steps):
                for step in steps:
                    step()

            pl.when(turn == index)(go)


def deal(steps, turns):
    return [steps[len(steps) * i // turns : len(steps) * (i + 1) // turns] for i in range(turns)]


def scatter_sems(line, parts):
    dma = pltpu.SemaphoreType.DMA
    return [dma((2, parts))] * 4 + [dma((parts,))] * 2 + [dma((2, line, parts))] * 2


def scatter_scratch(line, depth, width, own):
    slots = [pltpu.VMEM((2, line, depth, width), BF), pltpu.VMEM((line, depth, width), BF),
             pltpu.VMEM((2, line, depth, width), BF)]
    return slots + ([pltpu.VMEM((2, line, depth, width), BF)] if own else [])


class Scatter:
    def __init__(self, place, grad, out, cuts, slots, sems, own=None):
        self.place, self.grad, self.out, self.cuts, self.own = place, grad, out, cuts, own
        self.mid, self.far, self.path = slots
        self.cs, self.cr, self.ls, self.lr, self.xs, self.xr, self.zs, self.zr = sems

    def cols(self, part):
        start, width = self.cuts[part]
        return pl.ds(start, width)

    def column(self, which):
        return 1 - self.place.x if which == 0 else self.place.x

    def sibling_copy(self, part, which):
        place, cols, x = self.place, self.cols(part), self.column(which)
        return remote(
            self.grad.at[:, x, 1 - place.c, :, cols], self.mid.at[which, :, :, cols],
            self.cs.at[which, part], self.cr.at[which, part], place.sibling,
        )

    def own_copy(self, part, which):
        cols, x = self.cols(part), self.column(which)
        return pltpu.make_async_copy(
            self.grad.at[:, x, self.place.c, :, cols], self.own.at[which, :, :, cols], self.ls.at[which, part]
        )

    def across_copy(self, part):
        cols = self.cols(part)
        return remote(
            self.mid.at[0, :, :, cols], self.far.at[:, :, cols], self.xs.at[part], self.xr.at[part], self.place.across
        )

    def line_copy(self, part, way, target):
        cols = self.cols(part)
        ref = self.path.at[way, target, :, cols]
        return remote(
            self.mid.at[1, target, :, cols], ref,
            self.zs.at[way, target, part], self.zr.at[way, target, part], self.place.ahead[way],
        )

    def pass_copy(self, part, way, target):
        cols = self.cols(part)
        ref = self.path.at[way, target, :, cols]
        return remote(
            ref, ref, self.zs.at[way, target, part], self.zr.at[way, target, part], self.place.ahead[way]
        )

    def begin(self, part):
        for which in (0, 1):
            if self.own is not None:
                self.own_copy(part, which).start()
            self.sibling_copy(part, which).start()

    def merge(self, part, which):
        self.sibling_copy(part, which).wait_recv()
        if self.own is not None:
            self.own_copy(part, which).wait()
        cols = self.cols(part)
        for target in range(self.place.line):
            if self.own is not None:
                mine = self.own[which, target, :, cols]
            else:
                mine = self.grad[target, self.column(which), self.place.c, :, cols]
            both = self.mid[which, target, :, cols].astype(F32) + mine.astype(F32)
            self.mid[which, target, :, cols] = both.astype(BF)
        if which == 0:
            self.across_copy(part).start()

    def join(self, part):
        self.across_copy(part).wait_recv()
        cols = self.cols(part)
        for target in range(self.place.line):
            both = self.mid[1, target, :, cols].astype(F32) + self.far[target, :, cols].astype(F32)
            self.mid[1, target, :, cols] = both.astype(BF)

    def wave(self, part, turn):
        place, cols = self.place, self.cols(part)
        for way in (0, 1):
            hops = place.z if way == 0 else place.line - 1 - place.z
            target = place.line - 1 - turn + hops if way == 0 else turn - hops

            def start(way=way, target=target):
                self.line_copy(part, way, target).start()

            def go_on(way=way, target=target):
                self.pass_copy(part, way, target).wait_recv()
                both = self.path[way, target, :, cols].astype(F32) + self.mid[1, target, :, cols].astype(F32)
                self.path[way, target, :, cols] = both.astype(BF)
                self.pass_copy(part, way, target).start()

            pl.when(hops == 0)(start)
            pl.when((hops > 0) & (hops <= turn))(go_on)

    def end(self, part):
        place, cols = self.place, self.cols(part)
        start, width = self.cuts[part]
        z = place.z
        self.out[:, cols] = self.mid[1, z, :, cols].astype(F32)

        def take(way):
            self.pass_copy(part, way, z).wait_recv()
            self.out[:, cols] += self.path[way, z, :, cols].astype(F32)

        pl.when(z > 0)(functools.partial(take, 0))
        pl.when(z < place.line - 1)(functools.partial(take, 1))

    def drain_sibling(self, part):
        for which in (0, 1):
            self.sibling_copy(part, which).wait_send()

    def drain(self, part):
        place = self.place
        self.across_copy(part).wait_send()
        for target in range(place.line):
            for way in (0, 1):
                ahead = target > place.z if way == 0 else target < place.z
                pl.when(ahead)(lambda way=way, target=target: self.pass_copy(part, way, target).wait_send())

    def stages(self, part):
        waves = [functools.partial(self.wave, part, turn) for turn in range(self.place.line - 1)]
        return [functools.partial(self.join, part)] + waves + [functools.partial(self.end, part)]


KW = 4
PAD = 8


def conv_window(window, kernel, same):
    rows = window.shape[0] - PAD
    out = window[PAD:] * kernel[0:1]
    for offset in range(1, KW):
        out = out + jnp.where(same[offset - 1], window[PAD - offset : PAD - offset + rows], 0.0) * kernel[offset : offset + 1]
    return out


def same_documents(window):
    rows = window.shape[0] - PAD
    return [window[PAD:] == window[PAD - offset : PAD - offset + rows] for offset in range(1, KW)]


def rows_of(ref, block, count, extra=0):
    return ref[pl.ds(pl.multiple_of(block * STRETCH, STRETCH), count + extra), :]


def scalar_select(side, heads):
    src, dst = iota((DK, DK), 0), iota((DK, DK), 1)
    kind, head = dst // heads, dst % heads
    first = jnp.where(kind == side, 0, 2 * heads)
    source = jnp.where(kind < 2, first + side * heads + head, 4 * heads + head)
    return ((src == source) & (kind < 3)).astype(F32)


def softplus(values):
    return jnp.maximum(values, 0.0) + jnp.log1p(jnp.exp(-jnp.abs(values)))


def front_kernel(
    line, heads, x_ref, docs_ref, norm_ref, wq_ref, wg_ref, wk_ref, wv_ref, beta_ref, alpha_ref, wo_ref, gate_ref,
    up_ref, down_ref, log_ref, bias_ref, cq_ref, ck_ref, cv_ref, mix_ref,
    gated_ref, middle_ref, conv_ref, rates_ref,
    mixed_out, inv_out, state_out, pseudo_out, pre_out, q_out, k_out, v_out, aux_out, front_out, rest_out,
    mixed_ref, inv_ref, state_ref, pseudo_ref, pre_ref, q_ref, k_ref, v_ref, aux_ref,
    front, rest, wo, normed, doc_cols, attn, scal, scal_in, attn_own, attn_in,
    local_sem, y_send, y_recv, a_send, a_recv, *sems,
):
    place = Place(line)
    side = place.side
    seq = x_ref.shape[0]
    depth, half = wq_ref.shape
    span = 2 * STRETCH
    blocks = seq // STRETCH
    scal_at = 6 * half
    me = place.dp
    place.enter()

    own_cols = pl.ds(pl.multiple_of(side * half, half), half)
    other_cols = pl.ds(pl.multiple_of((1 - side) * half, half), half)

    def at(first):
        return pl.ds(pl.multiple_of((first + side) * half, half), half)

    swaps = [
        remote(wk_ref.at[:, other_cols], front.at[me, :, at(2)], y_send.at[0], y_recv.at[0], place.peer),
        remote(wv_ref.at[:, other_cols], front.at[me, :, at(4)], y_send.at[1], y_recv.at[1], place.peer),
        remote(scal, scal_in, y_send.at[2], y_recv.at[2], place.peer),
        remote(ck_ref.at[:, other_cols], conv_ref.at[1 + side], y_send.at[3], y_recv.at[3], place.peer),
        remote(cv_ref.at[:, other_cols], conv_ref.at[3 + side], y_send.at[4], y_recv.at[4], place.peer),
    ]
    scal[...] = jnp.zeros_like(scal)
    corner = (iota((depth, depth), 0) == iota((depth, depth), 1)).astype(BF)
    scal[:, 0 : 2 * heads] = product(corner, beta_ref[...], NT).astype(BF)
    scal[:, 4 * heads : 5 * heads] = product(corner, alpha_ref[...], NT).astype(BF)
    for swap in swaps:
        swap.start()
    ff = gate_ref.shape[1]
    rest[:, 0:half] = wo_ref[...]
    rest[:, half : half + ff] = gate_ref[...]
    rest[:, half + ff : half + 2 * ff] = up_ref[...]
    rest[:, half + 2 * ff : half + 3 * ff] = down_ref[...]
    own_rest = pltpu.make_async_copy(rest, rest_out.at[me], local_sem.at[0])
    own_rest.start()
    rates_ref[...] = jnp.zeros_like(rates_ref)
    rates_ref[0:1, 2 * heads : 3 * heads] = log_ref[...]
    rates_ref[1:2, 2 * heads : 3 * heads] = bias_ref[...]
    front[me, :, 0:half] = wq_ref[...]
    front[me, :, half : 2 * half] = wg_ref[...]
    front[me, :, at(2)] = wk_ref[:, own_cols]
    front[me, :, at(4)] = wv_ref[:, own_cols]
    conv_ref[0] = cq_ref[...]
    conv_ref[1 + side] = ck_ref[:, own_cols]
    conv_ref[3 + side] = cv_ref[:, own_cols]

    head_cuts = [(0, 2 * half), (2 * half, 2 * half), (4 * half, 2 * half + DK)]
    first = Gather(place, front, head_cuts, sems[:6])
    rest_cuts = [(0, half)] + [(half + i * ff, ff) for i in range(3)]
    second = Gather(place, rest_out, rest_cuts, sems[6:])

    first.step(0, 0)
    for swap in swaps:
        swap.wait_recv()
    lanes = iota((depth, DK), 1)
    theirs = pltpu.roll(scal_in[...].astype(F32), 2 * heads, 1)
    ours = scal[...].astype(F32)
    swapped = (lanes >= 2 * heads) & (lanes < 4 * heads)
    front[me, :, scal_at : scal_at + DK] = jnp.where(swapped, theirs, ours).astype(BF)
    for part in (1, 2):
        first.step(0, part)

    def normalise(block, carry):
        rows = pl.ds(pl.multiple_of(block * STRETCH, STRETCH), STRETCH)
        x = x_ref[rows, :].astype(F32)
        scale = lax.rsqrt(jnp.mean(x * x, axis=-1, keepdims=True) + 1e-06)
        normed[rows, :] = (x * scale * norm_ref[...]).astype(BF)
        return carry

    lax.fori_loop(0, blocks, normalise, 0)
    doc_cols[0:PAD, :] = jnp.full((PAD, DK), -1.0, F32)
    for i in range(seq // DK):
        lane_docs = docs_ref[:, i * DK : (i + 1) * DK].astype(F32)
        doc_cols[PAD + i * DK : PAD + (i + 1) * DK, :] = jnp.broadcast_to(lane_docs, (DK, DK)).T
    pre_ref[0:PAD, :] = jnp.zeros((PAD, pre_ref.shape[1]), F32)

    steps = first.steps()[3:]
    for step in steps:
        step()
    own_rest.wait()
    for part in range(4):
        second.step(0, part)
    tile = 2 * DK
    for part, (start, width) in enumerate(head_cuts):
        first.ready(part)

        def project(index, carry, start=start):
            cols = pl.ds(pl.multiple_of(start + index * tile, DK), tile)
            weights = front[:, :, cols].reshape(-1, tile)
            pre_ref[PAD:, cols] = jnp.dot(normed[...], weights, preferred_element_type=F32)
            return carry

        lax.fori_loop(0, 2 * half // tile, project, 0)
    scal_cols = slice(scal_at, scal_at + DK)
    pre_ref[PAD:, scal_cols] = jnp.dot(
        normed[...], front[:, :, scal_cols].reshape(-1, DK), preferred_element_type=F32
    )
    keep_front = pltpu.make_async_copy(front, front_out, local_sem.at[1])
    keep_front.start()

    def keep(index, src, dst):
        return pltpu.make_async_copy(src, dst, local_sem.at[index])

    keep_pre = keep(2, pre_ref, pre_out)
    keep_pre.start()
    early = [keep(3, inv_ref, inv_out), keep(4, q_ref, q_out), keep(5, k_ref, k_out), keep(6, v_ref, v_out)]
    early.append(keep(7, aux_ref, aux_out))
    late = [keep(8, mixed_ref, mixed_out), keep(9, state_ref, state_out), keep(10, pseudo_ref, pseudo_out)]
    keep_wo = keep(11, rest_out.at[:, :, pl.ds(0, half)], wo)

    select = scalar_select(side, heads)
    rate = -jnp.exp(rates_ref[0:1, :])
    masks = block_masks()
    t_row, t_col, p_row, p_col = masks
    together = 2
    turns = blocks // together
    slots = deal(second.steps()[4:], turns + blocks // 2) + [[]] * (blocks - blocks // 2)

    def keys_of(rows, cols):
        return jnp.concatenate([k_ref[0, rows, cols], k_ref[1, rows, cols]], axis=0)

    def prepare_block(block):
        rows = pl.ds(pl.multiple_of(block * STRETCH, STRETCH), STRETCH)
        doc_window = rows_of(doc_cols, block, STRETCH, PAD)
        same = same_documents(doc_window)
        raw = dot6(pre_ref[pl.ds(pl.multiple_of(block * STRETCH, STRETCH) + PAD, STRETCH), scal_cols], select)
        lane = iota((STRETCH, DK), 1)
        beta = (2.0 * jax.nn.sigmoid(raw)).astype(BF).astype(F32)
        decay = rate * softplus(raw + rates_ref[1:2, :])
        docs = doc_window[PAD:]
        fresh = (docs == doc_window[PAD - 1 : PAD]).astype(F32)
        aux = jnp.where(lane < 2 * heads, beta, jnp.where(lane < 3 * heads, decay, 0.0))
        aux = jnp.where(lane == 3 * heads, docs, jnp.where(lane == 3 * heads + 1, fresh, aux))
        aux_ref[rows, :] = aux
        for head in range(heads):
            cols = slice(head * DK, (head + 1) * DK)
            for kind in (1, 2, 0, 3, 4):
                first_col = (0, 2, 3, 4, 5)[kind] * half + head * DK
                window = pre_ref[
                    pl.ds(pl.multiple_of(block * STRETCH, STRETCH), STRETCH + PAD), first_col : first_col + DK
                ]
                value = conv_window(window, conv_ref[kind, :, cols], same)
                value = value * jax.nn.sigmoid(value)
                if kind < 3:
                    value = value * lax.rsqrt(jnp.sum(value * value, axis=-1, keepdims=True) + 1e-06)
                if kind == 0:
                    q_ref[rows, cols] = value * DK ** (-0.5)
                elif kind < 3:
                    k_ref[kind - 1, rows, cols] = value.astype(BF)
                else:
                    v_ref[kind - 3, rows, cols] = value.astype(BF)
        aux2, run2, aux_t, run_t = block_scalars(aux)
        mats = []
        for head in range(heads):
            cols = slice(head * DK, (head + 1) * DK)
            beta, run_col, run_row, doc_col, doc_row, carried, to_last = head_terms(
                aux, aux2, run2, aux_t, run_t, head, heads
            )
            decay = decay_matrix(run_col, run_row, doc_col, doc_row, p_row, p_col)
            keys = keys_of(rows, cols)
            gram = dot1(keys, keys, NT)
            mats.append(beta * jnp.where(p_row > p_col, decay * gram, 0.0))
            attn[block * heads + head] = decay[STRETCH:] * dot3(q_ref[rows, cols], keys, NT)
        return mats

    def prepare(turn, carry):
        mats = []
        for i in range(together):
            mats += prepare_block(turn * together + i)
        for i, inv in enumerate(inverse(mats, masks)):
            inv_ref[turn * together * heads + i] = inv
        run_slot(slots[:turns], turn)
        return carry

    lax.fori_loop(0, blocks // together, prepare, 0)
    for copy in early:
        copy.start()
    for head in range(heads):
        state_ref[head] = jnp.zeros((DK, DK), F32)

    def attn_copy(index):
        rows = chunk_rows(index)
        return remote(attn_own.at[rows], attn_in.at[rows], a_send.at[index], a_recv.at[index], place.peer)


    def advance(block, carry):
        rows = pl.ds(pl.multiple_of(block * STRETCH, STRETCH), STRETCH)
        aux = aux_ref[rows, :]
        aux2, run2, aux_t, run_t = block_scalars(aux)
        for head in range(heads):
            cols = slice(head * DK, (head + 1) * DK)
            beta, run_col, run_row, doc_col, doc_row, carried, to_last = head_terms(
                aux, aux2, run2, aux_t, run_t, head, heads
            )
            keys = keys_of(rows, cols)
            values = jnp.concatenate([v_ref[0, rows, cols], v_ref[1, rows, cols]], axis=0).astype(F32)
            state = state_ref[block * heads + head]
            state_parts = split(state)
            target = beta * (values - carried * dot3(keys, state_parts))
            pseudo = dot3(inv_ref[block * heads + head], target)
            pseudo_ref[block * heads + head] = pseudo
            mixed = carried[STRETCH:] * dot3(q_ref[rows, cols], state_parts) + dot3(
                attn[block * heads + head], pseudo
            )
            state_ref[(block + 1) * heads + head] = carried[span - 1 : span] * state + dot3(
                keys, to_last * pseudo, TN
            )
            mixed_ref[rows, cols] = mixed
            scale = lax.rsqrt(jnp.mean(mixed * mixed, axis=-1, keepdims=True) + 1e-05)
            gate = pre_ref[
                pl.ds(pl.multiple_of(block * STRETCH, STRETCH) + PAD, STRETCH),
                half + head * DK : half + (head + 1) * DK,
            ]
            gated_ref[rows, cols] = (mixed * scale * mix_ref[...] * (gate * jax.nn.sigmoid(gate))).astype(BF)
        run_slot(slots[turns:], block)
        per_pair = 2 * CHUNK // STRETCH

        def hand_over():
            pair = block // per_pair

            def complete():
                second.ready(0)
                keep_wo.start()
                keep_wo.wait()

            pl.when(pair == 0)(complete)
            rows = pair_rows(pair)
            attn_own[rows, :] = product(gated_ref[rows, :], wo[...].reshape(-1, half), NT).astype(BF)
            attn_copy(2 * pair).start()
            attn_copy(2 * pair + 1).start()

        pl.when(lax.rem(block, per_pair) == per_pair - 1)(hand_over)
        return carry

    lax.fori_loop(0, blocks, advance, 0)
    for copy in late:
        copy.start()

    def middle(index, carry):
        rows = chunk_rows(index)
        attn_copy(index).wait_recv()
        both = attn_own[rows, :].astype(F32) + attn_in[rows, :].astype(F32)
        middle_ref[rows, :] = x_ref[rows, :].astype(F32) + both
        return carry

    lax.fori_loop(0, seq // CHUNK, middle, 0)
    for part in (1, 2, 3):
        second.ready(part)

    def handed(index, carry):
        attn_copy(index).wait_send()
        return carry

    lax.fori_loop(0, seq // CHUNK, handed, 0)
    for swap in swaps:
        swap.wait_send()
    for part in range(3):
        first.drain(part)
    for part in range(4):
        second.drain(part)
    for copy in [keep_front, keep_pre] + early + late:
        copy.wait()


def front_call(line, x, docs, norm, wq, wg, wk, wv, beta, alpha, wo, gate, up, down, log, bias, cq, ck, cv, mix):
    seq, half = x.shape[0], wq.shape[1]
    depth, ff = gate.shape
    tail = half + 3 * ff
    heads, blocks = half // DK, seq // STRETCH
    units, span = heads * blocks, 2 * STRETCH
    width = 6 * half + DK
    shape = jax.ShapeDtypeStruct
    anywhere = pl.BlockSpec(memory_space=pl.ANY)
    dma = pltpu.SemaphoreType.DMA
    kept = (
        shape((seq, half), F32),
        shape((units, span, span), F32),
        shape((units + heads, DK, DK), F32),
        shape((units, span, DK), F32),
        shape((seq + PAD, width), F32),
        shape((seq, half), F32),
        shape((2, seq, half), BF),
        shape((2, seq, half), BF),
        shape((seq, DK), F32),
    )
    low = pltpu.VMEM(x.shape, BF)
    chunks = seq // CHUNK
    return pl.pallas_call(
        functools.partial(front_kernel, line, heads),
        out_shape=(
            shape((seq, half), BF),
            shape(x.shape, F32),
            shape((5, KW, half), F32),
            shape((2, DK), F32),
        )
        + kept
        + (
            shape((4 * line, depth, width), BF),
            shape((4 * line, depth, tail), BF),
        ),
        in_specs=[VMEM] * 19,
        out_specs=(VMEM,) * 4 + (anywhere,) * 11,
        scratch_shapes=[pltpu.VMEM(array.shape, array.dtype) for array in kept]
        + [
            pltpu.VMEM((4 * line, depth, width), BF),
            pltpu.VMEM((depth, tail), BF),
            pltpu.VMEM((4 * line, depth, half), BF),
            low,
            pltpu.VMEM((seq + PAD, DK), F32),
            pltpu.VMEM((units, STRETCH, span), F32),
            pltpu.VMEM((depth, DK), BF),
            pltpu.VMEM((depth, DK), BF),
            low,
            low,
            dma((12,)),
            dma((5,)),
            dma((5,)),
            dma((chunks,)),
            dma((chunks,)),
        ]
        + gather_sems(line, 3)
        + gather_sems(line, 4),
        compiler_params=pltpu.CompilerParams(
            collective_id=0, has_side_effects=True, vmem_limit_bytes=60 << 20
        ),
        name="front",
    )(x, docs, norm, wq, wg, wk, wv, beta, alpha, wo, gate, up, down, log, bias, cq, ck, cv, mix)


CHUNK = 128


def chunk_rows(index):
    return pl.ds(pl.multiple_of(index * CHUNK, CHUNK), CHUNK)


def pair_rows(index):
    return pl.ds(pl.multiple_of(index * 2 * CHUNK, 2 * CHUNK), 2 * CHUNK)


def flat(ref, start, width):
    return ref[:, :, :, :, start : start + width].reshape(-1, width)


def put_blocks(ref, index, cols, value):
    depth = ref.shape[3]
    count = DK // depth
    value = value.astype(BF)
    if count == 2:
        ref[index // 2, index % 2, :, :, cols] = value.reshape(2, depth, value.shape[-1])
    else:
        ref[pl.ds(index * (count // 4), count // 4), :, :, :, cols] = value.reshape(
            count // 4, 2, 2, depth, value.shape[-1]
        )


def rest_kernel(
    line, heads, gated_ref, x_ref, cot_ref, middle_ref, domains_ref, gain_ref, norm_ref, docs_ref, conv_ref, rates_ref, mix_ref,
    w_hbm, fw_hbm, pre_hbm, q_hbm, k_hbm, v_hbm, aux_hbm, mixed_hbm, inv_hbm, state_hbm, pseudo_hbm,
    out_ref, igrad_ref, sum_ref, gq_ref, gg_ref, gk_ref, gv_ref, gs_ref, gcq_ref, gck_ref, gcv_ref, gnorm_ref,
    gffn_ref, gtiny_ref,
    w_ref, fw_ref, attn_own, attn_in, in_own, in_in, normed, seed_low, work, back_ref, dgated_ref,
    dstate, doc_cols, dy_next, dconv_ref, dscal_ref, dgain_ref, total, mid, far, path,
    pre_s, q_s, k_s, v_s, aux_s, mixed_s, inv_s, state_s, pseudo_s,
    small, small_in, small_line, small_sum, mix_in, scal_in,
    load_sem, stream_sem, f_send, f_recv, o_send, o_recv, n_send, n_recv, h_send, h_recv,
    m_send, m_recv, l_send, l_recv, free_sem, *sems,
):
    place = Place(line)
    side, me = place.side, place.dp
    seq, width = x_ref.shape
    half = gated_ref.shape[1]
    tail = sum_ref.shape[-1]
    ff = (tail - half) // 3
    chunks = seq // CHUNK
    blocks = seq // STRETCH
    span = 2 * STRETCH
    gate_up = (half, 2 * ff)
    down = (half + 2 * ff, ff)
    scal_at = 6 * half
    front_width = scal_at + DK

    def load(index, start, count):
        cols = pl.ds(start, count)
        return pltpu.make_async_copy(w_hbm.at[:, :, :, :, cols], w_ref.at[:, :, :, :, cols], load_sem.at[index])

    loads = [load(0, 0, half), load(1, *gate_up), load(2, *down)]
    load_front = pltpu.make_async_copy(fw_hbm, fw_ref, load_sem.at[3])
    for copy in loads:
        copy.start()
    place.enter(everyone=True)

    def streams(block, slot):
        units = pl.ds(block * heads, heads)
        rows = pl.ds(pl.multiple_of(block * STRETCH, STRETCH), STRETCH)
        pairs = [
            (pre_hbm.at[pl.ds(pl.multiple_of(block * STRETCH, STRETCH), STRETCH + PAD)], pre_s),
            (q_hbm.at[rows], q_s),
            (k_hbm.at[:, rows], k_s),
            (v_hbm.at[:, rows], v_s),
            (aux_hbm.at[rows], aux_s),
            (mixed_hbm.at[rows], mixed_s),
            (inv_hbm.at[units], inv_s),
            (state_hbm.at[units], state_s),
            (pseudo_hbm.at[units], pseudo_s),
        ]
        return [
            pltpu.make_async_copy(src, dst.at[slot], stream_sem.at[slot, i]) for i, (src, dst) in enumerate(pairs)
        ]

    domains = domains_ref[...]
    rows_all = domains.shape[1]
    places = iota(domains.shape, 1)
    mine = jnp.sum(jnp.where(places == me, domains, 0), axis=1, keepdims=True)
    count = jnp.sum((domains == mine).astype(F32), axis=1, keepdims=True)
    row_weight = 2.0 / (1.0 + count * (GROUPS / rows_all))

    def in_copy(index):
        rows = chunk_rows(index)
        return remote(in_own.at[rows], in_in.at[rows], f_send.at[index], f_recv.at[index], place.peer)

    gffn_ref[...] = jnp.zeros_like(gffn_ref)
    for copy in loads:
        copy.wait()

    def feed(index, carry):
        rows = chunk_rows(index)
        middle = middle_ref[rows, :]
        scale = lax.rsqrt(jnp.mean(middle * middle, axis=-1, keepdims=True) + 1e-06)
        low = (middle * scale * gain_ref[...]).astype(BF)
        normed[rows, :] = low
        both = product(low, flat(w_ref, *gate_up))
        gate_in, up_in = both[:, :ff], both[:, ff:]
        sigmoid = jax.nn.sigmoid(gate_in)
        silu = gate_in * sigmoid
        seed = (cot_ref[rows, :].astype(F32) * row_weight).astype(BF)
        seed_low[rows, :] = seed
        hidden_back = product(seed, flat(w_ref, *down))
        gate_back = (hidden_back * up_in * (sigmoid * (1.0 + gate_in * (1.0 - sigmoid)))).astype(BF)
        up_back = (hidden_back * silu).astype(BF)
        work[rows, 0:ff] = gate_back
        work[rows, ff : 2 * ff] = up_back
        low_hidden = (silu * up_in).astype(BF)
        work[rows, 2 * ff : 3 * ff] = low_hidden
        return carry

    def feed_pair(index, carry):
        lax.fori_loop(2 * index, 2 * index + 2, feed, 0)
        rows = pair_rows(index)
        in_own[rows, :] = product(work[rows, 0 : 2 * ff], flat(w_ref, *gate_up), NT).astype(BF)
        in_copy(2 * index).start()
        in_copy(2 * index + 1).start()
        attn_own[rows, :] = product(work[rows, 2 * ff : 3 * ff], flat(w_ref, *down), NT).astype(BF)
        return carry

    lax.fori_loop(0, chunks // 2, feed_pair, 0)

    def weigh(index, carry):
        cols = pl.ds(pl.multiple_of(index * DK, DK), DK)
        put_blocks(w_ref, index, slice(half + 2 * ff, half + 3 * ff), product(seed_low[:, cols], work[:, 2 * ff : 3 * ff], TN))
        put_blocks(w_ref, index, slice(half, half + 2 * ff), product(normed[:, cols], work[:, 0 : 2 * ff], TN))
        return carry

    lax.fori_loop(0, width // DK, weigh, 0)
    cuts = [(half, ff), (half + ff, ff), (half + 2 * ff, ff), (0, half)]
    scatter = Scatter(place, w_ref, sum_ref, cuts, (mid, far, path), sems[:8])
    parts = range(len(cuts))
    for part in parts[:-1]:
        scatter.begin(part)
    scatter.merge(0, 0)
    scatter.merge(0, 1)
    merges = [functools.partial(scatter.merge, part, which) for part in (1, 2) for which in (0, 1)]
    merge_slots = deal(merges, chunks - 1)


    def finish(index, carry):
        rows = chunk_rows(index)
        in_copy(index).wait_recv()
        grad = in_own[rows, :].astype(F32) + in_in[rows, :].astype(F32)
        middle = middle_ref[rows, :]
        scale = lax.rsqrt(jnp.mean(middle * middle, axis=-1, keepdims=True) + 1e-06)
        unit = middle * scale
        gffn_ref[...] += jnp.sum(grad * unit, axis=0, keepdims=True)
        grad = grad * gain_ref[...]
        seed = cot_ref[rows, :].astype(F32) * row_weight
        total = seed + scale * (grad - unit * jnp.mean(unit * grad, axis=-1, keepdims=True))
        back_ref[rows, :] = total
        low = total.astype(BF)
        seed_low[rows, :] = low
        dgated_ref[rows, :] = product(low, flat(w_ref, 0, half))
        run_slot(merge_slots, index)
        return carry

    lax.fori_loop(0, chunks, finish, 0)

    def weigh_out(index, carry):
        cols = pl.ds(pl.multiple_of(index * DK, DK), DK)
        put_blocks(w_ref, index, slice(0, half), product(seed_low[:, cols], gated_ref[...], TN))
        return carry

    lax.fori_loop(0, width // DK, weigh_out, 0)
    scatter.begin(parts[-1])
    swap = remote(attn_own, attn_in, o_send, o_recv, place.peer)
    swap.start()
    for copy in streams(blocks - 1, (blocks - 1) % 2):
        copy.start()
    load_front.start()

    masks = block_masks()
    t_row, t_col, p_row, p_col = masks
    strict = p_row > p_col
    for head in range(heads):
        dstate[head] = jnp.zeros((DK, DK), F32)
    dgain_ref[...] = jnp.zeros_like(dgain_ref)
    dconv_ref[...] = jnp.zeros_like(dconv_ref)
    dscal_ref[...] = jnp.zeros_like(dscal_ref)
    dy_next[...] = jnp.zeros_like(dy_next)
    doc_cols[0:PAD, :] = jnp.full((PAD, DK), -1.0, F32)
    doc_cols[PAD + seq :, :] = jnp.full((PAD, DK), -1.0, F32)
    for i in range(seq // DK):
        lane_docs = docs_ref[:, i * DK : (i + 1) * DK].astype(F32)
        doc_cols[PAD + i * DK : PAD + (i + 1) * DK, :] = jnp.broadcast_to(lane_docs, (DK, DK)).T
    upper = (iota((STRETCH, STRETCH), 0) <= iota((STRETCH, STRETCH), 1)).astype(F32)
    lanes = iota((STRETCH, DK), 1)
    wide_rows = iota((span, DK), 0)
    select = scalar_select(side, heads)
    rate = -jnp.exp(rates_ref[0:1, :])
    scal_at = 6 * half
    scal_cols = slice(scal_at, scal_at + DK)

    chains = [scatter.stages(part) for part in parts]
    slots = [[] for _ in range(blocks)]
    left = []
    slots[0] += [functools.partial(scatter.merge, parts[-1], which) for which in (0, 1)]
    for part, turn in ((0, 2), (1, 5)):
        for step in chains[part]:
            (slots[turn] if turn < blocks else left).append(step)
            turn += step is not chains[part][0]

    def back(step, carry):
        block = blocks - 1 - step
        top = pl.multiple_of(block * STRETCH, STRETCH)
        rows = pl.ds(top, STRETCH)
        slot = lax.rem(block, 2)
        for copy in streams(block, slot):
            copy.wait()

        def fetch():
            for copy in streams(block - 1, 1 - slot):
                copy.start()

        pl.when(block > 0)(fetch)
        aux = aux_s[slot]
        aux2, run2, aux_t, run_t = block_scalars(aux)
        doc_window = doc_cols[pl.ds(top, STRETCH + 2 * PAD), :]
        same = same_documents(doc_window[: STRETCH + PAD])
        here = doc_window[PAD : PAD + STRETCH]
        same_next = [doc_window[PAD + o : PAD + o + STRETCH] == here for o in range(1, KW)]
        dbeta_all = jnp.zeros((STRETCH, DK), F32)
        drun_all = jnp.zeros((STRETCH, DK), F32)
        column_sums = jnp.zeros((span, DK), F32)

        def conv_back(kind, head, grad):
            first_col = (0, 2, 3, 4, 5)[kind] * half + head * DK
            cols = slice(head * DK, (head + 1) * DK)
            window = pre_s[slot, :, first_col : first_col + DK]
            kernel = conv_ref[kind, :, cols]
            shifted = [window[PAD:]] + [
                jnp.where(same[o - 1], window[PAD - o : PAD - o + STRETCH], 0.0) for o in range(1, KW)
            ]
            y = shifted[0] * kernel[0:1]
            for o in range(1, KW):
                y = y + shifted[o] * kernel[o : o + 1]
            sigmoid = jax.nn.sigmoid(y)
            act = y * sigmoid
            if kind < 3:
                scale = lax.rsqrt(jnp.sum(act * act, axis=-1, keepdims=True) + 1e-06)
                unit = act * scale
                if kind == 0:
                    grad = grad * DK ** (-0.5)
                grad = scale * (grad - unit * jnp.sum(unit * grad, axis=-1, keepdims=True))
            dy = grad * (sigmoid * (1.0 + y * (1.0 - sigmoid)))
            for o in range(KW):
                dconv_ref[kind, o : o + 1, cols] += jnp.sum(dy * shifted[o], axis=0, keepdims=True)
            at = slice(kind * half + head * DK, kind * half + (head + 1) * DK)
            longer = jnp.concatenate([dy, dy_next[:, at]], axis=0)
            dy_next[:, at] = dy[:PAD]
            dpre = dy * kernel[0:1]
            for o in range(1, KW):
                dpre = dpre + jnp.where(same_next[o - 1], longer[o : o + STRETCH], 0.0) * kernel[o : o + 1]
            work[rows, first_col : first_col + DK] = dpre.astype(BF)

        for head in range(heads):
            cols = slice(head * DK, (head + 1) * DK)
            gate_cols = slice(half + head * DK, half + (head + 1) * DK)
            beta, run_col, run_row, doc_col, doc_row, carried, to_last = head_terms(
                aux, aux2, run2, aux_t, run_t, head, heads
            )
            decay = decay_matrix(run_col, run_row, doc_col, doc_row, p_row, p_col)
            keys = jnp.concatenate([k_s[slot, 0, :, cols], k_s[slot, 1, :, cols]], axis=0)
            queries = q_s[slot, :, cols]
            mixed = mixed_s[slot, :, cols]
            gate = pre_s[slot, PAD:, gate_cols]
            sigmoid = jax.nn.sigmoid(gate)
            silu = gate * sigmoid
            scale = lax.rsqrt(jnp.mean(mixed * mixed, axis=-1, keepdims=True) + 1e-05)
            scaled = mixed * scale
            dgated = dgated_ref[rows, cols]
            part = dgated * scaled
            work[rows, gate_cols] = (
                part * mix_ref[...] * (sigmoid * (1.0 + gate * (1.0 - sigmoid)))
            ).astype(BF)
            dgain_ref[...] += jnp.sum(part * silu, axis=0, keepdims=True)
            dscaled = dgated * mix_ref[...] * silu
            dout = scale * (dscaled - scaled * jnp.mean(dscaled * scaled, axis=-1, keepdims=True))

            state, pseudo = state_s[slot, head], pseudo_s[slot, head]
            dnext = dstate[head]
            dnext_parts, state_parts, pseudo_parts = split(dnext), split(state), split(pseudo)
            dout_parts, q_parts = split(dout), split(queries)
            gram = dot1(keys, keys, NT)
            core = jnp.where(strict, decay * gram, 0.0)
            amat = beta * core
            qdecay = decay[STRETCH:]
            attn = qdecay * dot3(q_parts, keys, NT)
            dattn = dot3(dout_parts, pseudo_parts, NT)
            dqk = split(qdecay * dattn)
            dpseudo = dot3(attn, dout_parts, TN) + to_last * dot3(keys, dnext_parts)
            dtarget = dot3(inv_s[slot, head], dpseudo, TN)
            dtarget_parts = split(dtarget)
            damat = jnp.where(strict, -dot3(dtarget_parts, pseudo_parts, NT), 0.0)
            e_a, e_m = damat * amat, dattn * attn
            dgram = split(beta * decay * damat)
            dbeta = jnp.sum(dtarget * pseudo, axis=-1, keepdims=True) / jnp.maximum(beta, 1e-30)
            dvalues = (beta * dtarget).astype(BF).astype(F32)
            dread = -(beta * carried) * dtarget
            dout_c = carried[STRETCH:] * dout
            dread_parts, dout_c_parts = split(dread), split(dout_c)
            last = carried[span - 1 : span]
            dstate[head] = last * dnext + dot3(keys, dread_parts, TN) + dot3(q_parts, dout_c_parts, TN)
            dq_state = dot3(dout_c_parts, state_parts, NT)
            dk_state = dot3(dread_parts, state_parts, NT)
            dk_last = dot3(to_last * pseudo, dnext_parts, NT)
            conv_back(0, head, dq_state + dot3(dqk, keys))
            dkeys = (
                dk_state + dk_last + dot3(dgram, keys) + dot3(dgram, keys, TN) + dot3(dqk, q_parts, TN)
            ).astype(BF).astype(F32)
            conv_back(1, head, dkeys[:STRETCH])
            conv_back(2, head, dkeys[STRETCH:])
            conv_back(3, head, dvalues[:STRETCH])
            conv_back(4, head, dvalues[STRETCH:])

            wide = keys.astype(F32)
            e_last = jnp.sum(wide * dk_last, axis=-1, keepdims=True)
            drun = jnp.sum(e_a, axis=-1, keepdims=True) - e_last + jnp.sum(wide * dk_state, axis=-1, keepdims=True)
            drun_q = jnp.sum(e_m, axis=-1, keepdims=True) + jnp.sum(queries * dq_state, axis=-1, keepdims=True)
            at_last = jnp.sum(e_last, axis=0, keepdims=True) + last * jnp.sum(
                jnp.sum(dnext * state, axis=-1, keepdims=True), axis=0, keepdims=True
            )
            drun = drun[:STRETCH] + drun[STRETCH:] + drun_q
            drun = drun + jnp.where(iota((STRETCH, 1), 0) == STRETCH - 1, at_last, 0.0)
            lane = 2 * heads + head
            drun_all = jnp.where(lanes == lane, drun, drun_all)
            dbeta_all = jnp.where(lanes == head, dbeta[:STRETCH], dbeta_all)
            dbeta_all = jnp.where(lanes == heads + head, dbeta[STRETCH:], dbeta_all)
            sums = jnp.sum(e_a, axis=0, keepdims=True) + jnp.sum(e_m, axis=0, keepdims=True)
            column_sums = jnp.where(wide_rows == lane, sums, column_sums)
        down = column_sums.T
        ddecay = dot6(upper, drun_all - down[:STRETCH] - down[STRETCH:])
        raw = dot6(pre_s[slot, PAD:, scal_cols], select)
        sigmoid = jax.nn.sigmoid(raw)
        shifted = raw + rates_ref[1:2, :]
        draw_decay = ddecay * rate * jax.nn.sigmoid(shifted)
        is_decay = (lanes >= 2 * heads) & (lanes < 3 * heads)
        draw_decay = jnp.where(is_decay, draw_decay, 0.0)
        dscal_ref[0:1, :] += jnp.sum(
            jnp.where(is_decay, ddecay * rate * softplus(shifted), 0.0), axis=0, keepdims=True
        )
        dscal_ref[1:2, :] += jnp.sum(draw_decay, axis=0, keepdims=True)
        dbeta_low = dbeta_all.astype(BF).astype(F32)
        draw = jnp.where(lanes < 2 * heads, dbeta_low * 2.0 * sigmoid * (1.0 - sigmoid), draw_decay)
        work[rows, scal_cols] = dot6(draw, select, NT).astype(BF)
        run_slot(slots, step)
        return carry

    lax.fori_loop(0, blocks, back, 0)
    mix_swap = remote(dgain_ref, mix_in, m_send.at[2], m_recv.at[2], place.peer)
    mix_swap.start()

    def normalise(index, carry):
        rows = chunk_rows(index)
        x = x_ref[rows, :].astype(F32)
        scale = lax.rsqrt(jnp.mean(x * x, axis=-1, keepdims=True) + 1e-06)
        normed[rows, :] = (x * scale * norm_ref[...]).astype(BF)
        return carry

    lax.fori_loop(0, chunks, normalise, 0)

    def in_sent(index, carry):
        in_copy(index).wait_send()
        return carry

    lax.fori_loop(0, chunks, in_sent, 0)

    def weigh_front(index, carry):
        cols = pl.ds(pl.multiple_of(index * DK, DK), DK)
        put_blocks(w_ref, index, slice(0, front_width), product(normed[:, cols], work[:, 0:front_width], TN))
        return carry

    for part in parts:
        scatter.drain_sibling(part)
    for step in left:
        step()
    lax.fori_loop(0, width // DK, weigh_front, 0)

    def release(stage):
        for part in ((0, 1), (2, 3))[stage]:
            scatter.drain(part)
        sem = free_sem.at[stage]
        for device in (place.sibling, place.across):
            pl.semaphore_signal(sem, inc=1, device_id=device, device_id_type=MESH)
        for way in (0, 1):
            pl.when(place.can_send[way])(
                lambda way=way: pl.semaphore_signal(sem, inc=1, device_id=place.ahead[way], device_id_type=MESH)
            )

    def await_release(stage):
        senders = 2 + place.can_send[0].astype(jnp.int32) + place.can_send[1].astype(jnp.int32)
        pl.semaphore_wait(free_sem.at[stage], senders)

    cuts = [(2 * half, 2 * half), (4 * half, 2 * half + DK), (0, half), (half, half)]
    later = Scatter(place, w_ref, total, cuts, (mid, far, path), sems[8:])
    chains[2][0]()
    chains[2][1]()
    release(0)
    await_release(0)
    later.begin(0)
    later.begin(1)
    load_front.wait()

    def outputs(index, carry):
        rows = chunk_rows(index)
        both = attn_own[rows, :].astype(F32) + attn_in[rows, :].astype(F32)
        out_ref[rows, :] = (middle_ref[rows, :] + both).astype(BF)
        return carry

    def nb_copy(index):
        rows = chunk_rows(index)
        return remote(in_own.at[rows], in_in.at[rows], n_send.at[index], n_recv.at[index], place.peer)

    def project_back(index):
        rows = pair_rows(index)
        in_own[rows, :] = product(work[rows, 0:front_width], flat(fw_ref, 0, front_width), NT).astype(BF)
        nb_copy(2 * index).start()
        nb_copy(2 * index + 1).start()

    swap.wait_recv()
    project_back(0)
    later.merge(0, 0)
    later.merge(0, 1)
    for step in chains[2][2:3]:
        step()
    for index in range(1, chunks // 2):
        project_back(index)
    later.merge(1, 0)
    later.merge(1, 1)
    for step in chains[2][3:-1] + chains[3][:2]:
        step()
    lax.fori_loop(0, chunks, outputs, 0)
    chains[2][-1]()
    for step in chains[3][2:]:
        step()
    release(1)
    await_release(1)
    later.begin(2)
    later.begin(3)
    gnorm_ref[...] = jnp.zeros_like(gnorm_ref)

    def finish_back(index, carry):
        rows = chunk_rows(index)
        nb_copy(index).wait_recv()
        back = in_own[rows, :].astype(F32) + in_in[rows, :].astype(F32)
        x = x_ref[rows, :].astype(F32)
        scale = lax.rsqrt(jnp.mean(x * x, axis=-1, keepdims=True) + 1e-06)
        unit = x * scale
        gnorm_ref[...] += jnp.sum(back * unit, axis=0, keepdims=True)
        back = back * norm_ref[...]
        total_back = back_ref[rows, :] + scale * (back - unit * jnp.mean(unit * back, axis=-1, keepdims=True))
        igrad_ref[rows, :] = total_back.astype(BF)
        return carry

    small_swaps = [
        remote(small, small_in.at[0], m_send.at[0], m_recv.at[0], place.sibling),
        remote(small_sum, small_in.at[1], m_send.at[1], m_recv.at[1], place.across),
    ]

    def line_copy(target):
        device = (target * 4 + place.x * 2 + place.c, side)
        return remote(small_line.at[place.z], small_line.at[place.z], l_send.at[target], l_recv.at[place.z], device)

    def line_from(source):
        device = (source * 4 + place.x * 2 + place.c, side)
        return remote(small_line.at[source], small_line.at[source], l_send.at[source], l_recv.at[source], device)

    def collect():
        mix_swap.wait_recv()
        small[0:5] = dconv_ref[...]
        for i in range(2):
            small[5, i : i + 1, :] = gnorm_ref[:, i * half : (i + 1) * half]
            small[5, 2 + i : 3 + i, :] = gffn_ref[:, i * half : (i + 1) * half]
        small[6] = jnp.zeros((KW, half), F32)
        small[6, 0:1, 0:DK] = dgain_ref[...] + mix_in[...]
        small[6, 0:1, DK : 2 * DK] = dscal_ref[0:1, :]
        small[6, 0:1, 2 * DK : 3 * DK] = dscal_ref[1:2, :]
        small_swaps[0].start()

    def collect_across():
        small_swaps[0].wait_recv()
        small_sum[...] = small[...] + small_in[0]
        small_swaps[1].start()

    def collect_line():
        small_swaps[1].wait_recv()
        small_line[place.z] = small_sum[...] + small_in[1]
        for target in range(line):
            pl.when(target != place.z)(lambda target=target: line_copy(target).start())

    home = [
        remote(
            total.at[:, pl.ds(pl.multiple_of((base + 1 - side) * half, half), half)],
            ref.at[:, pl.ds(pl.multiple_of(side * half, half), half)],
            h_send.at[i], h_recv.at[i], place.peer,
        )
        for i, (base, ref) in enumerate(((2, gk_ref), (4, gv_ref)))
    ]
    scal_home = remote(total.at[:, scal_at : scal_at + DK], scal_in, h_send.at[2], h_recv.at[2], place.peer)
    own_half = pl.ds(pl.multiple_of(side * half, half), half)

    def at_home(i):
        base, ref = ((2, gk_ref), (4, gv_ref))[i]
        home[i].start()
        ref[:, own_half] = total[:, pl.ds(pl.multiple_of((base + side) * half, half), half)]

    def at_home_value():
        at_home(1)
        scal_home.start()

    after = [later.stages(part) for part in range(4)]
    homes = [functools.partial(at_home, 0), at_home_value]
    merge = functools.partial
    slots = [
        [merge(later.merge, 2, 0), merge(later.merge, 2, 1)],
        [merge(later.merge, 3, 0), merge(later.merge, 3, 1)],
        after[0][:2],
        after[0][2:3],
    ]

    def finish_and(index, carry):
        finish_back(index, carry)
        run_slot(slots, index)
        return carry

    lax.fori_loop(0, chunks, finish_and, 0)
    rest = after[0][3:-1] + after[1][:2] + after[0][-1:] + homes[:1] + after[1][2:-1] + after[2][:2] + after[1][-1:]
    rest += homes[1:] + after[3][:2]
    for pair in zip(after[2][2:], after[3][2:]):
        rest += pair
    extra = [collect, collect_across, collect_line]
    for i, step in enumerate(rest):
        if i % 2 == 0 and extra:
            extra.pop(0)()
        step()
    for step in extra:
        step()
    for source in range(line):
        pl.when(source != place.z)(lambda source=source: line_from(source).wait_recv())
    summed = small_line[0]
    for source in range(1, line):
        summed = summed + small_line[source]
    small_sum_out = summed
    gcq_ref[...] = small_sum_out[0]
    small_swaps[0].wait_send()
    small_swaps[1].wait_send()
    small[...] = small_sum_out
    conv_home = [
        remote(
            small.at[base + 1 - side], ref.at[:, own_half], h_send.at[i], h_recv.at[i], place.peer
        )
        for i, (base, ref) in ((3, (1, gck_ref)), (4, (3, gcv_ref)))
    ]
    for copy in conv_home:
        copy.start()
    gck_ref[:, own_half] = small[1 + side]
    gcv_ref[:, own_half] = small[3 + side]
    for i in range(2):
        gnorm_ref[:, i * half : (i + 1) * half] = small_sum_out[5, i : i + 1]
        gffn_ref[:, i * half : (i + 1) * half] = small_sum_out[5, 2 + i : 3 + i]
    gtiny_ref[...] = small_sum_out[6, 0:1, 0 : 3 * DK]
    gq_ref[...] = total[:, 0:half]
    gg_ref[...] = total[:, half : 2 * half]
    scal_home.wait_recv()
    lanes = iota(scal_in.shape, 1)
    ours = total[:, scal_at : scal_at + DK]
    theirs = pltpu.roll(scal_in[...], DK - 2 * heads, 1)
    gs_ref[...] = jnp.where(lanes < 2 * heads, ours + theirs, ours)
    for copy in home + conv_home:
        copy.wait_recv()
    for copy in home + conv_home + [scal_home, mix_swap]:
        copy.wait_send()
    for target in range(line):
        pl.when(target != place.z)(lambda target=target: line_copy(target).wait_send())

    def sent(index, carry):
        nb_copy(index).wait_send()
        return carry

    lax.fori_loop(0, chunks, sent, 0)
    for part in range(4):
        later.drain_sibling(part)
        later.drain(part)
    swap.wait_send()


def rest_call(line, gated, x, cot, middle, domains, gain, norm, docs, conv, rates, mix, w, fw, pre, q, k, v, aux, mixed, inv, state, pseudo):
    seq, width = x.shape
    half = gated.shape[1]
    heads = half // DK
    depth, tail = w.shape[3:]
    columns = fw.shape[-1]
    ff = (tail - half) // 3
    shape = jax.ShapeDtypeStruct
    dma = pltpu.SemaphoreType.DMA
    chunks = seq // CHUNK
    span = 2 * STRETCH
    tiny = (7, KW, half)
    low = pltpu.VMEM((seq, width), BF)
    wide = pltpu.VMEM((seq, width), F32)
    return pl.pallas_call(
        functools.partial(rest_kernel, line, heads),
        out_shape=(
            shape((seq, width), BF),
            shape((seq, width), BF),
            shape((depth, tail), F32),
            shape((depth, half), F32),
            shape((depth, half), F32),
            shape((depth, 2 * half), F32),
            shape((depth, 2 * half), F32),
            shape((depth, DK), F32),
            shape((KW, half), F32),
            shape((KW, 2 * half), F32),
            shape((KW, 2 * half), F32),
            shape((1, width), F32),
            shape((1, width), F32),
            shape((1, 3 * DK), F32),
        ),
        in_specs=[VMEM] * 11 + [pl.BlockSpec(memory_space=pl.ANY)] * 11,
        out_specs=(VMEM,) * 14,
        scratch_shapes=[
            pltpu.VMEM(w.shape, BF),
            pltpu.VMEM(fw.shape, BF),
        ]
        + [low] * 6
        + [pltpu.VMEM((seq, 3 * ff), BF), wide, pltpu.VMEM((seq, half), F32)]
        + [
            pltpu.VMEM((heads, DK, DK), F32),
            pltpu.VMEM((seq + 2 * PAD, DK), F32),
            pltpu.VMEM((PAD, 5 * half), F32),
            pltpu.VMEM((5, KW, half), F32),
            pltpu.VMEM((2, DK), F32),
            pltpu.VMEM((1, DK), F32),
            pltpu.VMEM((depth, columns), F32),
        ]
        + scatter_scratch(line, depth, tail, False)
        + [
            pltpu.VMEM((2, STRETCH + PAD, columns), F32),
            pltpu.VMEM((2, STRETCH, half), F32),
            pltpu.VMEM((2, 2, STRETCH, half), BF),
            pltpu.VMEM((2, 2, STRETCH, half), BF),
            pltpu.VMEM((2, STRETCH, DK), F32),
            pltpu.VMEM((2, STRETCH, half), F32),
            pltpu.VMEM((2, heads, span, span), F32),
            pltpu.VMEM((2, heads, DK, DK), F32),
            pltpu.VMEM((2, heads, span, DK), F32),
        ]
        + [
            pltpu.VMEM(tiny, F32),
            pltpu.VMEM((2,) + tiny, F32),
            pltpu.VMEM((line,) + tiny, F32),
            pltpu.VMEM(tiny, F32),
            pltpu.VMEM((1, DK), F32),
            pltpu.VMEM((depth, DK), F32),
        ]
        + [dma((4,)), dma((2, 9))]
        + [dma((chunks,))] * 2
        + [dma, dma]
        + [dma((chunks,)), dma((chunks,)), dma((5,)), dma((5,)), dma((3,)), dma((3,)), dma((line,)), dma((line,))]
        + [pltpu.SemaphoreType.REGULAR((2,))]
        + scatter_sems(line, 4)
        + scatter_sems(line, 4),
        compiler_params=pltpu.CompilerParams(
            collective_id=1, has_side_effects=True, vmem_limit_bytes=63 << 20
        ),
        name="rest",
    )(gated, x, cot, middle, domains, gain, norm, docs, conv, rates, mix, w, fw, pre, q, k, v, aux, mixed, inv, state, pseudo)


def deliver_kernel(heads, *refs):
    count = (len(refs) - 21) // 2
    sources, outs, held, sems = refs[:count], refs[count : count + 20], refs[count + 20 : -1], refs[-1]
    copies = [pltpu.make_async_copy(src, dst, sems.at[i]) for i, (src, dst) in enumerate(zip(sources, held))]
    for copy in copies:
        copy.start()
    (
        out_ref, igrad_ref, sum_ref, gq_ref, gg_ref, gk_ref, gv_ref, gs_ref, gcq_ref, gck_ref, gcv_ref, gnorm_ref,
        gffn_ref, gtiny_ref,
    ) = held
    (
        output, input_grad, norm, query, outgate, key, value, beta, alpha, log, bias, c_query, c_key, c_value, mix,
        w_out, ffn, gate, up, down,
    ) = outs
    for copy in copies:
        copy.wait()
    output[0] = out_ref[...]
    input_grad[0] = igrad_ref[...]
    norm[...] = gnorm_ref[...]
    ffn[...] = gffn_ref[...]
    query[...] = gq_ref[...]
    outgate[...] = gg_ref[...]
    key[0] = gk_ref[...]
    value[0] = gv_ref[...]
    depth, half = query.shape
    ff = gate.shape[1]
    corner = (iota((depth, depth), 0) == iota((depth, depth), 1)).astype(F32)
    turned = dot6(gs_ref[...], corner, TN)
    beta[...] = turned[0 : 2 * heads]
    alpha[...] = turned[4 * heads : 5 * heads]
    here = slice(2 * heads, 3 * heads)
    log[...] = gtiny_ref[:, DK : 2 * DK][:, here]
    bias[...] = gtiny_ref[:, 2 * DK :][:, here]
    mix[...] = gtiny_ref[:, 0:DK]
    c_query[...] = gcq_ref[...]
    c_key[0] = gck_ref[...]
    c_value[0] = gcv_ref[...]
    w_out[...] = sum_ref[:, 0:half]
    gate[...] = sum_ref[:, half : half + ff]
    up[...] = sum_ref[:, half + ff : half + 2 * ff]
    down[...] = sum_ref[:, half + 2 * ff :]


def deliver_call(heads, *parts):
    seq, width = parts[0].shape
    depth, tail = parts[2].shape
    half = parts[3].shape[1]
    ff = (tail - half) // 3
    shape = lambda *dims: jax.ShapeDtypeStruct(dims, F32)
    low = jax.ShapeDtypeStruct((1, seq, width), BF)
    return pl.pallas_call(
        functools.partial(deliver_kernel, heads),
        out_shape=(
            low, low, shape(1, width), shape(depth, half), shape(depth, half), shape(1, depth, 2 * half),
            shape(1, depth, 2 * half), shape(2 * heads, depth), shape(heads, depth), shape(1, heads),
            shape(1, heads), shape(KW, half), shape(1, KW, 2 * half), shape(1, KW, 2 * half), shape(1, DK),
            shape(depth, half), shape(1, width), shape(depth, ff), shape(depth, ff), shape(depth, ff),
        ),
        in_specs=[pl.BlockSpec(memory_space=pl.ANY)] * 14,
        out_specs=(VMEM,) * 20,
        scratch_shapes=[pltpu.VMEM(part.shape, part.dtype) for part in parts]
        + [pltpu.SemaphoreType.DMA((len(parts),))],
        compiler_params=pltpu.CompilerParams(vmem_limit_bytes=63 << 20),
        name="deliver",
    )(*parts)


GROUPS = 8


def per_device(
    tokens,
    cotangent,
    domains,
    doc_ids,
    norm_gain,
    w_query,
    w_outgate,
    w_key,
    w_value,
    w_beta,
    w_alpha,
    decay_log,
    decay_bias,
    conv_query,
    conv_key,
    conv_value,
    mix_gain,
    w_out,
    ffn_gain,
    w_gate,
    w_up,
    w_down,
):
    line = lax.axis_size("dp") // 4
    by_place = lambda array: array.reshape((line, 2, 2) + array.shape[1:])
    gain_row = mix_gain[None]
    (
        gated, middle, conv, rates, mixed, inv, state, pseudo, pre, queries, keys, values, aux, front_w, back_w
    ) = front_call(
        line, tokens[0], doc_ids, norm_gain[None], w_query, w_outgate, w_key[0], w_value[0], w_beta[0].T, w_alpha.T,
        w_out.T, w_gate, w_up, w_down.T, decay_log[None], decay_bias[None], conv_query, conv_key[0], conv_value[0],
        gain_row,
    )
    parts = rest_call(
        line, gated, tokens[0], cotangent[0], middle, domains[None], ffn_gain[None], norm_gain[None], doc_ids, conv,
        rates, gain_row, by_place(back_w), by_place(front_w), pre, queries, keys, values, aux, mixed, inv, state,
        pseudo,
    )
    results = list(deliver_call(w_alpha.shape[1], *parts))
    for index in (2, 9, 10, 14, 16):
        results[index] = results[index][0]
    for index in (8, 15, 19):
        results[index] = results[index].T
    results[7] = results[7].T[None]
    return tuple(results)


def solution(mesh):
    return jax.shard_map(
        per_device,
        mesh=mesh,
        in_specs=(
            P("dp", None, None),
            P("dp", None, None),
            P(),
            P("dp", None),
            P(),
            P("dp", "step"),
            P("dp", "step"),
            P("step", "dp", None),
            P("step", "dp", None),
            P("step", "dp", None),
            P("dp", "step"),
            P("step"),
            P("step"),
            P(None, "step"),
            P("step", None, None),
            P("step", None, None),
            P(),
            P("step", "dp"),
            P(),
            P("dp", "step"),
            P("dp", "step"),
            P("step", "dp"),
        ),
        out_specs=(
            P("dp", None, None),
            P("dp", None, None),
            P(),
            P("dp", "step"),
            P("dp", "step"),
            P("step", "dp", None),
            P("step", "dp", None),
            P("step", "dp", None),
            P("dp", "step"),
            P("step"),
            P("step"),
            P(None, "step"),
            P("step", None, None),
            P("step", None, None),
            P(),
            P("step", "dp"),
            P(),
            P("dp", "step"),
            P("dp", "step"),
            P("step", "dp"),
        ),
        check_vma=False,
    )
```

```python
import functools
import itertools

import jax
import jax.numpy as jnp
from jax import lax
from jax.experimental import pallas as pl
from jax.experimental.pallas import tpu as pltpu
from jax.sharding import PartitionSpec as P

STRETCH = 64
DK = 128
F32 = jnp.float32
BF = jnp.bfloat16
NN = ((1,), (0,))
NT = ((1,), (1,))
TN = ((0,), (0,))


def split(a):
    if a.dtype == BF:
        return (a,)
    hi = a.astype(BF)
    return (hi, (a - hi.astype(F32)).astype(BF))


def dot1(a, b, dims=NN):
    return lax.dot_general(a.astype(BF), b.astype(BF), (dims, ((), ())), preferred_element_type=F32)


def dot3(a, b, dims=NN):
    a = a if isinstance(a, tuple) else split(a)
    b = b if isinstance(b, tuple) else split(b)
    one = lambda x, y: lax.dot_general(x, y, (dims, ((), ())), preferred_element_type=F32)
    out = one(a[0], b[0])
    if len(a) > 1:
        out = out + one(a[1], b[0])
    if len(b) > 1:
        out = out + one(a[0], b[1])
    return out


def dot6(a, b, dims=NN):
    return lax.dot_general(
        a, b, (dims, ((), ())), precision=lax.Precision.HIGHEST, preferred_element_type=F32
    )


def iota(shape, dim):
    return lax.broadcasted_iota(jnp.int32, shape, dim)


def product(first, second, dims=NN):
    return lax.dot_general(first, second, (dims, ((), ())), preferred_element_type=F32)


def block_masks():
    span = 2 * STRETCH
    row, col = iota((span, span), 0), iota((span, span), 1)
    t_row, t_col = row % STRETCH, col % STRETCH
    p_row, p_col = 2 * t_row + row // STRETCH, 2 * t_col + col // STRETCH
    return t_row, t_col, p_row, p_col


def twice(block):
    return jnp.concatenate([block, block], axis=0)


def block_scalars(aux):
    low = (iota((STRETCH, STRETCH), 0) >= iota((STRETCH, STRETCH), 1)).astype(F32)
    running = dot6(low, aux)
    aux2, run2 = twice(aux), twice(running)
    return aux2, run2, aux2.T, run2.T


def head_terms(aux, aux2, run2, aux_t, run_t, head, heads):
    beta = jnp.concatenate(
        [aux[:, head : head + 1], aux[:, heads + head : heads + head + 1]], axis=0
    )
    lane = 2 * heads + head
    run_col = run2[:, lane : lane + 1]
    run_row = run_t[lane : lane + 1, :]
    doc_lane = 3 * heads
    doc_col = aux2[:, doc_lane : doc_lane + 1]
    doc_row = aux_t[doc_lane : doc_lane + 1, :]
    fresh = aux2[:, doc_lane + 1 : doc_lane + 2]
    span = 2 * STRETCH
    carried = jnp.where(fresh > 0.5, jnp.exp(run_col), 0.0)
    last_run = run_col[span - 1 : span, :]
    to_last = jnp.where(doc_col == doc_col[span - 1 : span, :], jnp.exp(last_run - run_col), 0.0)
    return beta, run_col, run_row, doc_col, doc_row, carried, to_last


def decay_matrix(run_col, run_row, doc_col, doc_row, p_row, p_col):
    inside = (p_row >= p_col) & (doc_col == doc_row)
    return jnp.where(inside, jnp.exp(jnp.where(inside, run_col - run_row, 0.0)), 0.0)


def inverse(mats, masks):
    t_row, t_col, p_row, p_col = masks
    eye = (p_row == p_col).astype(F32)
    pair = (t_row == t_col) & (p_row > p_col)
    out = [eye - jnp.where(pair, a, 0.0) for a in mats]
    level = 1
    while (1 << level) <= STRETCH:
        merge = (
            ((t_row >> level) == (t_col >> level))
            & (((t_row >> (level - 1)) & 1) == 1)
            & (((t_col >> (level - 1)) & 1) == 0)
        )
        low = [x.astype(BF) for x in out]
        half = [dot1(x, jnp.where(merge, a, 0.0)) for x, a in zip(low, mats)]
        out = [o - dot1(h, x) for o, h, x in zip(out, half, low)]
        level += 1
    rest = [eye - x - dot3(a, x) for a, x in zip(mats, out)]
    return [x + dot1(x, r) for x, r in zip(out, rest)]


VMEM = pl.BlockSpec(memory_space=pltpu.VMEM)


MESH = pl.DeviceIdType.MESH


class Place:
    def __init__(self, line):
        self.line = line
        self.dp, self.side = lax.axis_index("dp"), lax.axis_index("step")
        self.z, self.x, self.c = self.dp // 4, (self.dp // 2) % 2, self.dp % 2
        self.sibling = (self.dp + 1 - 2 * self.c, self.side)
        self.across = (self.dp + 2 - 4 * self.x, self.side)
        self.ahead = (
            (lax.rem(self.dp + 4, 4 * line), self.side),
            (lax.rem(self.dp + 4 * line - 4, 4 * line), self.side),
        )
        self.peer = (self.dp, 1 - self.side)
        self.can_send = (self.z + 1 < line, self.z > 0)

    def reaches(self, way, far):
        return self.z - far >= 0 if way == 0 else self.z + far < self.line

    def behind(self, way, far):
        return self.dp - 4 * far if way == 0 else self.dp + 4 * far

    def enter(self, plane=True, peer=True, everyone=False):
        barrier = pltpu.get_barrier_semaphore()

        def greet(device):
            pl.semaphore_signal(barrier, inc=1, device_id=device, device_id_type=MESH)

        count = 0
        if peer:
            greet(self.peer)
            count = 1
        if plane:
            greet(self.sibling)
            greet(self.across)
            count = count + 2
        if everyone:
            for z in range(self.line):
                device = (z * 4 + self.x * 2 + self.c, self.side)
                pl.when(z != self.z)(functools.partial(greet, device))
            count = count + self.line - 1
        elif plane:
            for way in (0, 1):
                pl.when(self.can_send[way])(functools.partial(greet, self.ahead[way]))
            count = count + self.can_send[0].astype(jnp.int32) + self.can_send[1].astype(jnp.int32)
        pl.semaphore_wait(barrier, count)


def remote(src, dst, send_sem, recv_sem, device):
    return pltpu.make_async_remote_copy(
        src_ref=src, dst_ref=dst, send_sem=send_sem, recv_sem=recv_sem,
        device_id=device, device_id_type=MESH,
    )


def gather_sems(line, parts):
    dma = pltpu.SemaphoreType.DMA
    return [
        dma((2, line, parts)), dma((2, line, parts)),
        dma((2, line, parts)), dma((2, line, parts)),
        dma((2, 2, line, parts)), dma((2, 2, line, parts)),
    ]


class Gather:
    def __init__(self, place, buf, cuts, sems):
        self.place, self.buf, self.cuts = place, buf, cuts
        self.zs, self.zr, self.xs, self.xr, self.cs, self.cr = sems

    def block(self, index, part):
        start, width = self.cuts[part]
        return self.buf.at[index, :, pl.ds(start, width)]

    def line_copy(self, index, way, far, part):
        ref = self.block(index, part)
        return remote(ref, ref, self.zs.at[way, far, part], self.zr.at[way, far, part], self.place.ahead[way])

    def across_copy(self, index, way, far, part):
        ref = self.block(index, part)
        return remote(ref, ref, self.xs.at[way, far, part], self.xr.at[way, far, part], self.place.across)

    def sibling_copy(self, index, column, way, far, part):
        ref = self.block(index, part)
        return remote(
            ref, ref, self.cs.at[column, way, far, part], self.cr.at[column, way, far, part], self.place.sibling
        )

    def spread(self, index, way, far, part):
        place = self.place
        for to in (0, 1) if far == 0 else (way,):
            pl.when(place.can_send[to])(lambda to=to: self.line_copy(index, to, far + 1, part).start())
        self.across_copy(index, way, far, part).start()
        self.sibling_copy(index, 0, way, far, part).start()

    def ways(self, far):
        return (0,) if far == 0 else (0, 1)

    def each(self, far, act):
        if far == 0:
            act(0)
            return
        for way in (0, 1):
            pl.when(self.place.reaches(way, far))(functools.partial(act, way))

    def step(self, far, part):
        place = self.place
        if far == 0:
            self.spread(place.dp, 0, 0, part)
            return

        def from_line(way):
            index = place.behind(way, far)
            self.line_copy(index, way, far, part).wait_recv()
            self.spread(index, way, far, part)

        def from_across(way):
            index = place.behind(way, far - 1) + 2 - 4 * place.x
            self.across_copy(index, way, far - 1, part).wait_recv()
            self.sibling_copy(index, 1, way, far - 1, part).start()

        if far < place.line:
            self.each(far, from_line)
        self.each(far - 1, from_across)

    def steps(self):
        return [
            functools.partial(self.step, far, part)
            for far in range(self.place.line + 1)
            for part in range(len(self.cuts))
        ]

    def ready(self, part):
        place = self.place
        for far in range(place.line):
            for column in (0, 1):

                def from_sibling(way):
                    index = place.behind(way, far) + 1 - 2 * place.c + column * (2 - 4 * place.x)
                    self.sibling_copy(index, column, way, far, part).wait_recv()

                self.each(far, from_sibling)

    def drain(self, part):
        place = self.place
        for far in range(place.line):

            def sent(way):
                index = place.behind(way, far)
                for to in (0, 1) if far == 0 else (way,):
                    pl.when(place.can_send[to])(
                        lambda to=to: self.line_copy(index, to, far + 1, part).wait_send()
                    )
                self.across_copy(index, way, far, part).wait_send()
                self.sibling_copy(index, 0, way, far, part).wait_send()
                self.sibling_copy(index + 2 - 4 * place.x, 1, way, far, part).wait_send()

            self.each(far, sent)


def run_slot(slots, turn):
    for index, steps in enumerate(slots):
        if steps:

            def go(steps=steps):
                for step in steps:
                    step()

            pl.when(turn == index)(go)


def deal(steps, turns):
    return [steps[len(steps) * i // turns : len(steps) * (i + 1) // turns] for i in range(turns)]


def scatter_sems(line, parts):
    dma = pltpu.SemaphoreType.DMA
    return [dma((2, parts))] * 4 + [dma((parts,))] * 2 + [dma((2, line, parts))] * 2


def scatter_scratch(line, depth, width, own):
    slots = [pltpu.VMEM((2, line, depth, width), BF), pltpu.VMEM((line, depth, width), BF),
             pltpu.VMEM((2, line, depth, width), BF)]
    return slots + ([pltpu.VMEM((2, line, depth, width), BF)] if own else [])


class Scatter:
    def __init__(self, place, grad, out, cuts, slots, sems, own=None):
        self.place, self.grad, self.out, self.cuts, self.own = place, grad, out, cuts, own
        self.mid, self.far, self.path = slots
        self.cs, self.cr, self.ls, self.lr, self.xs, self.xr, self.zs, self.zr = sems

    def cols(self, part):
        start, width = self.cuts[part]
        return pl.ds(start, width)

    def column(self, which):
        return 1 - self.place.x if which == 0 else self.place.x

    def sibling_copy(self, part, which):
        place, cols, x = self.place, self.cols(part), self.column(which)
        return remote(
            self.grad.at[:, x, 1 - place.c, :, cols], self.mid.at[which, :, :, cols],
            self.cs.at[which, part], self.cr.at[which, part], place.sibling,
        )

    def own_copy(self, part, which):
        cols, x = self.cols(part), self.column(which)
        return pltpu.make_async_copy(
            self.grad.at[:, x, self.place.c, :, cols], self.own.at[which, :, :, cols], self.ls.at[which, part]
        )

    def across_copy(self, part):
        cols = self.cols(part)
        return remote(
            self.mid.at[0, :, :, cols], self.far.at[:, :, cols], self.xs.at[part], self.xr.at[part], self.place.across
        )

    def line_copy(self, part, way, target):
        cols = self.cols(part)
        ref = self.path.at[way, target, :, cols]
        return remote(
            self.mid.at[1, target, :, cols], ref,
            self.zs.at[way, target, part], self.zr.at[way, target, part], self.place.ahead[way],
        )

    def pass_copy(self, part, way, target):
        cols = self.cols(part)
        ref = self.path.at[way, target, :, cols]
        return remote(
            ref, ref, self.zs.at[way, target, part], self.zr.at[way, target, part], self.place.ahead[way]
        )

    def begin(self, part):
        for which in (0, 1):
            if self.own is not None:
                self.own_copy(part, which).start()
            self.sibling_copy(part, which).start()

    def merge(self, part, which):
        self.sibling_copy(part, which).wait_recv()
        if self.own is not None:
            self.own_copy(part, which).wait()
        cols = self.cols(part)
        for target in range(self.place.line):
            if self.own is not None:
                mine = self.own[which, target, :, cols]
            else:
                mine = self.grad[target, self.column(which), self.place.c, :, cols]
            both = self.mid[which, target, :, cols].astype(F32) + mine.astype(F32)
            self.mid[which, target, :, cols] = both.astype(BF)
        if which == 0:
            self.across_copy(part).start()

    def join(self, part):
        self.across_copy(part).wait_recv()
        cols = self.cols(part)
        for target in range(self.place.line):
            both = self.mid[1, target, :, cols].astype(F32) + self.far[target, :, cols].astype(F32)
            self.mid[1, target, :, cols] = both.astype(BF)

    def wave(self, part, turn):
        place, cols = self.place, self.cols(part)
        for way in (0, 1):
            hops = place.z if way == 0 else place.line - 1 - place.z
            target = place.line - 1 - turn + hops if way == 0 else turn - hops

            def start(way=way, target=target):
                self.line_copy(part, way, target).start()

            def go_on(way=way, target=target):
                self.pass_copy(part, way, target).wait_recv()
                both = self.path[way, target, :, cols].astype(F32) + self.mid[1, target, :, cols].astype(F32)
                self.path[way, target, :, cols] = both.astype(BF)
                self.pass_copy(part, way, target).start()

            pl.when(hops == 0)(start)
            pl.when((hops > 0) & (hops <= turn))(go_on)

    def end(self, part):
        place, cols = self.place, self.cols(part)
        start, width = self.cuts[part]
        z = place.z
        self.out[:, cols] = self.mid[1, z, :, cols].astype(F32)

        def take(way):
            self.pass_copy(part, way, z).wait_recv()
            self.out[:, cols] += self.path[way, z, :, cols].astype(F32)

        pl.when(z > 0)(functools.partial(take, 0))
        pl.when(z < place.line - 1)(functools.partial(take, 1))

    def drain_sibling(self, part):
        for which in (0, 1):
            self.sibling_copy(part, which).wait_send()

    def drain(self, part):
        place = self.place
        self.across_copy(part).wait_send()
        for target in range(place.line):
            for way in (0, 1):
                ahead = target > place.z if way == 0 else target < place.z
                pl.when(ahead)(lambda way=way, target=target: self.pass_copy(part, way, target).wait_send())

    def stages(self, part):
        waves = [functools.partial(self.wave, part, turn) for turn in range(self.place.line - 1)]
        return [functools.partial(self.join, part)] + waves + [functools.partial(self.end, part)]


KW = 4
PAD = 8


def conv_window(window, kernel, same):
    rows = window.shape[0] - PAD
    out = window[PAD:] * kernel[0:1]
    for offset in range(1, KW):
        out = out + jnp.where(same[offset - 1], window[PAD - offset : PAD - offset + rows], 0.0) * kernel[offset : offset + 1]
    return out


def same_documents(window):
    rows = window.shape[0] - PAD
    return [window[PAD:] == window[PAD - offset : PAD - offset + rows] for offset in range(1, KW)]


def rows_of(ref, block, count, extra=0):
    return ref[pl.ds(pl.multiple_of(block * STRETCH, STRETCH), count + extra), :]


def scalar_select(side, heads):
    src, dst = iota((DK, DK), 0), iota((DK, DK), 1)
    kind, head = dst // heads, dst % heads
    first = jnp.where(kind == side, 0, 2 * heads)
    source = jnp.where(kind < 2, first + side * heads + head, 4 * heads + head)
    return ((src == source) & (kind < 3)).astype(F32)


def softplus(values):
    return jnp.maximum(values, 0.0) + jnp.log1p(jnp.exp(-jnp.abs(values)))


def front_kernel(
    line, heads, x_ref, docs_ref, norm_ref, wq_ref, wg_ref, wk_ref, wv_ref, beta_ref, alpha_ref, wo_ref, gate_ref,
    up_ref, down_ref, log_ref, bias_ref, cq_ref, ck_ref, cv_ref, mix_ref,
    gated_ref, middle_ref, conv_ref, rates_ref,
    mixed_out, inv_out, state_out, pseudo_out, pre_out, q_out, k_out, v_out, aux_out, front_out, rest_out,
    mixed_ref, inv_ref, state_ref, pseudo_ref, pre_ref, q_ref, k_ref, v_ref, aux_ref,
    front, rest, wo, normed, doc_cols, attn, scal, scal_in, attn_own, attn_in,
    local_sem, y_send, y_recv, a_send, a_recv, *sems,
):
    place = Place(line)
    side = place.side
    seq = x_ref.shape[0]
    depth, half = wq_ref.shape
    span = 2 * STRETCH
    blocks = seq // STRETCH
    scal_at = 6 * half
    me = place.dp
    place.enter()

    own_cols = pl.ds(pl.multiple_of(side * half, half), half)
    other_cols = pl.ds(pl.multiple_of((1 - side) * half, half), half)

    def at(first):
        return pl.ds(pl.multiple_of((first + side) * half, half), half)

    swaps = [
        remote(wk_ref.at[:, other_cols], front.at[me, :, at(2)], y_send.at[0], y_recv.at[0], place.peer),
        remote(wv_ref.at[:, other_cols], front.at[me, :, at(4)], y_send.at[1], y_recv.at[1], place.peer),
        remote(scal, scal_in, y_send.at[2], y_recv.at[2], place.peer),
        remote(ck_ref.at[:, other_cols], conv_ref.at[1 + side], y_send.at[3], y_recv.at[3], place.peer),
        remote(cv_ref.at[:, other_cols], conv_ref.at[3 + side], y_send.at[4], y_recv.at[4], place.peer),
    ]
    scal[...] = jnp.zeros_like(scal)
    corner = (iota((depth, depth), 0) == iota((depth, depth), 1)).astype(BF)
    scal[:, 0 : 2 * heads] = product(corner, beta_ref[...], NT).astype(BF)
    scal[:, 4 * heads : 5 * heads] = product(corner, alpha_ref[...], NT).astype(BF)
    for swap in swaps:
        swap.start()
    ff = gate_ref.shape[1]
    rest[:, 0:half] = wo_ref[...]
    rest[:, half : half + ff] = gate_ref[...]
    rest[:, half + ff : half + 2 * ff] = up_ref[...]
    rest[:, half + 2 * ff : half + 3 * ff] = down_ref[...]
    own_rest = pltpu.make_async_copy(rest, rest_out.at[me], local_sem.at[0])
    own_rest.start()
    rates_ref[...] = jnp.zeros_like(rates_ref)
    rates_ref[0:1, 2 * heads : 3 * heads] = log_ref[...]
    rates_ref[1:2, 2 * heads : 3 * heads] = bias_ref[...]
    front[me, :, 0:half] = wq_ref[...]
    front[me, :, half : 2 * half] = wg_ref[...]
    front[me, :, at(2)] = wk_ref[:, own_cols]
    front[me, :, at(4)] = wv_ref[:, own_cols]
    conv_ref[0] = cq_ref[...]
    conv_ref[1 + side] = ck_ref[:, own_cols]
    conv_ref[3 + side] = cv_ref[:, own_cols]

    head_cuts = [(0, 2 * half), (2 * half, 2 * half), (4 * half, 2 * half + DK)]
    first = Gather(place, front, head_cuts, sems[:6])
    rest_cuts = [(0, half)] + [(half + i * ff, ff) for i in range(3)]
    second = Gather(place, rest_out, rest_cuts, sems[6:])

    first.step(0, 0)
    for swap in swaps:
        swap.wait_recv()
    lanes = iota((depth, DK), 1)
    theirs = pltpu.roll(scal_in[...].astype(F32), 2 * heads, 1)
    ours = scal[...].astype(F32)
    swapped = (lanes >= 2 * heads) & (lanes < 4 * heads)
    front[me, :, scal_at : scal_at + DK] = jnp.where(swapped, theirs, ours).astype(BF)
    for part in (1, 2):
        first.step(0, part)

    def normalise(block, carry):
        rows = pl.ds(pl.multiple_of(block * STRETCH, STRETCH), STRETCH)
        x = x_ref[rows, :].astype(F32)
        scale = lax.rsqrt(jnp.mean(x * x, axis=-1, keepdims=True) + 1e-06)
        normed[rows, :] = (x * scale * norm_ref[...]).astype(BF)
        return carry

    lax.fori_loop(0, blocks, normalise, 0)
    doc_cols[0:PAD, :] = jnp.full((PAD, DK), -1.0, F32)
    for i in range(seq // DK):
        lane_docs = docs_ref[:, i * DK : (i + 1) * DK].astype(F32)
        doc_cols[PAD + i * DK : PAD + (i + 1) * DK, :] = jnp.broadcast_to(lane_docs, (DK, DK)).T
    pre_ref[0:PAD, :] = jnp.zeros((PAD, pre_ref.shape[1]), F32)

    own_rest.wait()
    second.step(0, 0)
    for far in range(1, line + 1):
        if far == line:
            for part in (1, 2, 3):
                second.step(0, part)
        for part in range(3):
            first.step(far, part)
        second.step(far, 0)
    tile = 2 * DK
    for part, (start, width) in enumerate(head_cuts):
        first.ready(part)

        def project(index, carry, start=start):
            cols = pl.ds(pl.multiple_of(start + index * tile, DK), tile)
            weights = front[:, :, cols].reshape(-1, tile)
            pre_ref[PAD:, cols] = jnp.dot(normed[...], weights, preferred_element_type=F32)
            return carry

        lax.fori_loop(0, 2 * half // tile, project, 0)
    scal_cols = slice(scal_at, scal_at + DK)
    pre_ref[PAD:, scal_cols] = jnp.dot(
        normed[...], front[:, :, scal_cols].reshape(-1, DK), preferred_element_type=F32
    )
    keep_front = pltpu.make_async_copy(front, front_out, local_sem.at[1])
    keep_front.start()
    second.ready(0)

    def keep(index, src, dst):
        return pltpu.make_async_copy(src, dst, local_sem.at[index])

    keep_pre = keep(2, pre_ref, pre_out)
    keep_pre.start()
    early = [keep(3, inv_ref, inv_out), keep(4, q_ref, q_out), keep(5, k_ref, k_out), keep(6, v_ref, v_out)]
    early.append(keep(7, aux_ref, aux_out))
    late = [keep(8, mixed_ref, mixed_out), keep(9, state_ref, state_out), keep(10, pseudo_ref, pseudo_out)]
    keep_wo = keep(11, rest_out.at[:, :, pl.ds(0, half)], wo)
    keep_wo.start()

    select = scalar_select(side, heads)
    rate = -jnp.exp(rates_ref[0:1, :])
    masks = block_masks()
    t_row, t_col, p_row, p_col = masks
    together = 2
    turns = blocks // together
    later = [functools.partial(second.step, far, part) for far in range(1, line + 1) for part in (1, 2, 3)]
    slots = deal(later[:3], turns) + [[]] * blocks

    def keys_of(rows, cols):
        return jnp.concatenate([k_ref[0, rows, cols], k_ref[1, rows, cols]], axis=0)

    def prepare_block(block):
        rows = pl.ds(pl.multiple_of(block * STRETCH, STRETCH), STRETCH)
        doc_window = rows_of(doc_cols, block, STRETCH, PAD)
        same = same_documents(doc_window)
        raw = dot6(pre_ref[pl.ds(pl.multiple_of(block * STRETCH, STRETCH) + PAD, STRETCH), scal_cols], select)
        lane = iota((STRETCH, DK), 1)
        beta = (2.0 * jax.nn.sigmoid(raw)).astype(BF).astype(F32)
        decay = rate * softplus(raw + rates_ref[1:2, :])
        docs = doc_window[PAD:]
        fresh = (docs == doc_window[PAD - 1 : PAD]).astype(F32)
        aux = jnp.where(lane < 2 * heads, beta, jnp.where(lane < 3 * heads, decay, 0.0))
        aux = jnp.where(lane == 3 * heads, docs, jnp.where(lane == 3 * heads + 1, fresh, aux))
        aux_ref[rows, :] = aux
        for head in range(heads):
            cols = slice(head * DK, (head + 1) * DK)
            for kind in (1, 2, 0, 3, 4):
                first_col = (0, 2, 3, 4, 5)[kind] * half + head * DK
                window = pre_ref[
                    pl.ds(pl.multiple_of(block * STRETCH, STRETCH), STRETCH + PAD), first_col : first_col + DK
                ]
                value = conv_window(window, conv_ref[kind, :, cols], same)
                value = value * jax.nn.sigmoid(value)
                if kind < 3:
                    value = value * lax.rsqrt(jnp.sum(value * value, axis=-1, keepdims=True) + 1e-06)
                if kind == 0:
                    q_ref[rows, cols] = value * DK ** (-0.5)
                elif kind < 3:
                    k_ref[kind - 1, rows, cols] = value.astype(BF)
                else:
                    v_ref[kind - 3, rows, cols] = value.astype(BF)
        aux2, run2, aux_t, run_t = block_scalars(aux)
        mats = []
        for head in range(heads):
            cols = slice(head * DK, (head + 1) * DK)
            beta, run_col, run_row, doc_col, doc_row, carried, to_last = head_terms(
                aux, aux2, run2, aux_t, run_t, head, heads
            )
            decay = decay_matrix(run_col, run_row, doc_col, doc_row, p_row, p_col)
            keys = keys_of(rows, cols)
            gram = dot1(keys, keys, NT)
            mats.append(beta * jnp.where(p_row > p_col, decay * gram, 0.0))
            attn[block * heads + head] = decay[STRETCH:] * dot3(q_ref[rows, cols], keys, NT)
        return mats

    def prepare(turn, carry):
        mats = []
        for i in range(together):
            mats += prepare_block(turn * together + i)
        for i, inv in enumerate(inverse(mats, masks)):
            inv_ref[turn * together * heads + i] = inv
        run_slot(slots[:turns], turn)
        return carry

    lax.fori_loop(0, blocks // together, prepare, 0)
    for copy in early:
        copy.start()
    keep_wo.wait()
    for head in range(heads):
        state_ref[head] = jnp.zeros((DK, DK), F32)

    def attn_copy(index):
        rows = chunk_rows(index)
        return remote(attn_own.at[rows], attn_in.at[rows], a_send.at[index], a_recv.at[index], place.peer)


    def advance(block, carry):
        rows = pl.ds(pl.multiple_of(block * STRETCH, STRETCH), STRETCH)
        aux = aux_ref[rows, :]
        aux2, run2, aux_t, run_t = block_scalars(aux)
        def of_head(head):
            cols = slice(head * DK, (head + 1) * DK)
            beta, run_col, run_row, doc_col, doc_row, carried, to_last = head_terms(
                aux, aux2, run2, aux_t, run_t, head, heads
            )
            keys = keys_of(rows, cols)
            values = jnp.concatenate([v_ref[0, rows, cols], v_ref[1, rows, cols]], axis=0).astype(F32)
            state = state_ref[block * heads + head]
            state_parts = split(state)
            yield
            target = beta * (values - carried * dot3(keys, state_parts))
            yield
            pseudo = dot3(inv_ref[block * heads + head], target)
            pseudo_ref[block * heads + head] = pseudo
            yield
            mixed = carried[STRETCH:] * dot3(q_ref[rows, cols], state_parts) + dot3(
                attn[block * heads + head], pseudo
            )
            yield
            state_ref[(block + 1) * heads + head] = carried[span - 1 : span] * state + dot3(
                keys, to_last * pseudo, TN
            )
            yield
            mixed_ref[rows, cols] = mixed
            scale = lax.rsqrt(jnp.mean(mixed * mixed, axis=-1, keepdims=True) + 1e-05)
            gate = pre_ref[
                pl.ds(pl.multiple_of(block * STRETCH, STRETCH) + PAD, STRETCH),
                half + head * DK : half + (head + 1) * DK,
            ]
            gated_ref[rows, cols] = (mixed * scale * mix_ref[...] * (gate * jax.nn.sigmoid(gate))).astype(BF)
        for _ in itertools.zip_longest(*[of_head(head) for head in range(heads)]):
            pass
        run_slot(slots[turns:], block)
        per_chunk = CHUNK // STRETCH

        def hand_over():
            chunk = block // per_chunk
            rows = chunk_rows(chunk)
            attn_own[rows, :] = product(gated_ref[rows, :], wo[...].reshape(-1, half), NT).astype(BF)
            attn_copy(chunk).start()

        pl.when(lax.rem(block, per_chunk) == per_chunk - 1)(hand_over)
        return carry

    lax.fori_loop(0, blocks, advance, 0)
    for copy in late:
        copy.start()
    for step in later[3:]:
        step()

    def middle(index, carry):
        rows = chunk_rows(index)
        attn_copy(index).wait_recv()
        both = attn_own[rows, :].astype(F32) + attn_in[rows, :].astype(F32)
        middle_ref[rows, :] = x_ref[rows, :].astype(F32) + both
        return carry

    lax.fori_loop(0, seq // CHUNK, middle, 0)
    for part in (1, 2, 3):
        second.ready(part)

    def handed(index, carry):
        attn_copy(index).wait_send()
        return carry

    lax.fori_loop(0, seq // CHUNK, handed, 0)
    for swap in swaps:
        swap.wait_send()
    for part in range(3):
        first.drain(part)
    for part in range(4):
        second.drain(part)
    for copy in [keep_front, keep_pre] + early + late:
        copy.wait()


def front_call(line, x, docs, norm, wq, wg, wk, wv, beta, alpha, wo, gate, up, down, log, bias, cq, ck, cv, mix):
    seq, half = x.shape[0], wq.shape[1]
    depth, ff = gate.shape
    tail = half + 3 * ff
    heads, blocks = half // DK, seq // STRETCH
    units, span = heads * blocks, 2 * STRETCH
    width = 6 * half + DK
    shape = jax.ShapeDtypeStruct
    anywhere = pl.BlockSpec(memory_space=pl.ANY)
    dma = pltpu.SemaphoreType.DMA
    kept = (
        shape((seq, half), F32),
        shape((units, span, span), F32),
        shape((units + heads, DK, DK), F32),
        shape((units, span, DK), F32),
        shape((seq + PAD, width), F32),
        shape((seq, half), F32),
        shape((2, seq, half), BF),
        shape((2, seq, half), BF),
        shape((seq, DK), F32),
    )
    low = pltpu.VMEM(x.shape, BF)
    chunks = seq // CHUNK
    return pl.pallas_call(
        functools.partial(front_kernel, line, heads),
        out_shape=(
            shape((seq, half), BF),
            shape(x.shape, F32),
            shape((5, KW, half), F32),
            shape((2, DK), F32),
        )
        + kept
        + (
            shape((4 * line, depth, width), BF),
            shape((4 * line, depth, tail), BF),
        ),
        in_specs=[VMEM] * 19,
        out_specs=(VMEM,) * 4 + (anywhere,) * 11,
        scratch_shapes=[pltpu.VMEM(array.shape, array.dtype) for array in kept]
        + [
            pltpu.VMEM((4 * line, depth, width), BF),
            pltpu.VMEM((depth, tail), BF),
            pltpu.VMEM((4 * line, depth, half), BF),
            low,
            pltpu.VMEM((seq + PAD, DK), F32),
            pltpu.VMEM((units, STRETCH, span), F32),
            pltpu.VMEM((depth, DK), BF),
            pltpu.VMEM((depth, DK), BF),
            low,
            low,
            dma((12,)),
            dma((5,)),
            dma((5,)),
            dma((chunks,)),
            dma((chunks,)),
        ]
        + gather_sems(line, 3)
        + gather_sems(line, 4),
        compiler_params=pltpu.CompilerParams(
            collective_id=0, has_side_effects=True, vmem_limit_bytes=60 << 20
        ),
        name="front",
    )(x, docs, norm, wq, wg, wk, wv, beta, alpha, wo, gate, up, down, log, bias, cq, ck, cv, mix)


CHUNK = 128


def chunk_rows(index):
    return pl.ds(pl.multiple_of(index * CHUNK, CHUNK), CHUNK)


def pair_rows(index):
    return pl.ds(pl.multiple_of(index * 2 * CHUNK, 2 * CHUNK), 2 * CHUNK)


def flat(ref, start, width):
    return ref[:, :, :, :, start : start + width].reshape(-1, width)


def put_blocks(ref, index, cols, value):
    depth = ref.shape[3]
    count = DK // depth
    value = value.astype(BF)
    if count == 2:
        ref[index // 2, index % 2, :, :, cols] = value.reshape(2, depth, value.shape[-1])
    else:
        ref[pl.ds(index * (count // 4), count // 4), :, :, :, cols] = value.reshape(
            count // 4, 2, 2, depth, value.shape[-1]
        )


def rest_kernel(
    line, heads, gated_ref, x_ref, cot_ref, middle_ref, domains_ref, gain_ref, norm_ref, docs_ref, conv_ref, rates_ref, mix_ref,
    w_hbm, fw_hbm, pre_hbm, q_hbm, k_hbm, v_hbm, aux_hbm, mixed_hbm, inv_hbm, state_hbm, pseudo_hbm,
    out_ref, igrad_ref, sum_ref, gq_ref, gg_ref, gk_ref, gv_ref, gs_ref, gcq_ref, gck_ref, gcv_ref, gnorm_ref,
    gffn_ref, gtiny_ref,
    w_ref, fw_ref, attn_own, attn_in, in_own, in_in, normed, seed_low, work, back_ref, dgated_ref,
    dstate, doc_cols, dy_next, dconv_ref, dscal_ref, dgain_ref, total, mid, far, path,
    pre_s, q_s, k_s, v_s, aux_s, mixed_s, inv_s, state_s, pseudo_s,
    small, small_in, small_line, small_sum, mix_in, scal_in,
    load_sem, stream_sem, f_send, f_recv, o_send, o_recv, n_send, n_recv, h_send, h_recv,
    m_send, m_recv, l_send, l_recv, free_sem, *sems,
):
    place = Place(line)
    side, me = place.side, place.dp
    seq, width = x_ref.shape
    half = gated_ref.shape[1]
    tail = sum_ref.shape[-1]
    ff = (tail - half) // 3
    chunks = seq // CHUNK
    blocks = seq // STRETCH
    span = 2 * STRETCH
    gate_up = (half, 2 * ff)
    down = (half + 2 * ff, ff)
    scal_at = 6 * half
    front_width = scal_at + DK

    def load(index, start, count):
        cols = pl.ds(start, count)
        return pltpu.make_async_copy(w_hbm.at[:, :, :, :, cols], w_ref.at[:, :, :, :, cols], load_sem.at[index])

    loads = [load(0, 0, half), load(1, *gate_up), load(2, *down)]
    load_front = pltpu.make_async_copy(fw_hbm, fw_ref, load_sem.at[3])
    for copy in loads:
        copy.start()
    place.enter(everyone=True)

    def streams(block, slot):
        units = pl.ds(block * heads, heads)
        rows = pl.ds(pl.multiple_of(block * STRETCH, STRETCH), STRETCH)
        pairs = [
            (pre_hbm.at[pl.ds(pl.multiple_of(block * STRETCH, STRETCH), STRETCH + PAD)], pre_s),
            (q_hbm.at[rows], q_s),
            (k_hbm.at[:, rows], k_s),
            (v_hbm.at[:, rows], v_s),
            (aux_hbm.at[rows], aux_s),
            (mixed_hbm.at[rows], mixed_s),
            (inv_hbm.at[units], inv_s),
            (state_hbm.at[units], state_s),
            (pseudo_hbm.at[units], pseudo_s),
        ]
        return [
            pltpu.make_async_copy(src, dst.at[slot], stream_sem.at[slot, i]) for i, (src, dst) in enumerate(pairs)
        ]

    domains = domains_ref[...]
    rows_all = domains.shape[1]
    places = iota(domains.shape, 1)
    mine = jnp.sum(jnp.where(places == me, domains, 0), axis=1, keepdims=True)
    count = jnp.sum((domains == mine).astype(F32), axis=1, keepdims=True)
    row_weight = 2.0 / (1.0 + count * (GROUPS / rows_all))

    def in_copy(index):
        rows = chunk_rows(index)
        return remote(in_own.at[rows], in_in.at[rows], f_send.at[index], f_recv.at[index], place.peer)

    gffn_ref[...] = jnp.zeros_like(gffn_ref)
    for copy in loads:
        copy.wait()

    def feed(index, carry):
        rows = chunk_rows(index)
        middle = middle_ref[rows, :]
        scale = lax.rsqrt(jnp.mean(middle * middle, axis=-1, keepdims=True) + 1e-06)
        low = (middle * scale * gain_ref[...]).astype(BF)
        normed[rows, :] = low
        both = product(low, flat(w_ref, *gate_up))
        gate_in, up_in = both[:, :ff], both[:, ff:]
        sigmoid = jax.nn.sigmoid(gate_in)
        silu = gate_in * sigmoid
        seed = (cot_ref[rows, :].astype(F32) * row_weight).astype(BF)
        seed_low[rows, :] = seed
        hidden_back = product(seed, flat(w_ref, *down))
        gate_back = (hidden_back * up_in * (sigmoid * (1.0 + gate_in * (1.0 - sigmoid)))).astype(BF)
        up_back = (hidden_back * silu).astype(BF)
        work[rows, 0:ff] = gate_back
        work[rows, ff : 2 * ff] = up_back
        low_hidden = (silu * up_in).astype(BF)
        work[rows, 2 * ff : 3 * ff] = low_hidden
        return carry

    def feed_pair(step, carry):
        index = chunks // 2 - 1 - step
        lax.fori_loop(2 * index, 2 * index + 2, feed, 0)
        rows = pair_rows(index)
        in_own[rows, :] = product(work[rows, 0 : 2 * ff], flat(w_ref, *gate_up), NT).astype(BF)
        in_copy(2 * index).start()
        in_copy(2 * index + 1).start()
        attn_own[rows, :] = product(work[rows, 2 * ff : 3 * ff], flat(w_ref, *down), NT).astype(BF)
        return carry

    lax.fori_loop(0, chunks // 2, feed_pair, 0)

    def weigh(index, carry):
        cols = pl.ds(pl.multiple_of(index * DK, DK), DK)
        put_blocks(w_ref, index, slice(half + 2 * ff, half + 3 * ff), product(seed_low[:, cols], work[:, 2 * ff : 3 * ff], TN))
        put_blocks(w_ref, index, slice(half, half + 2 * ff), product(normed[:, cols], work[:, 0 : 2 * ff], TN))
        return carry

    lax.fori_loop(0, width // DK, weigh, 0)
    cuts = [(half, ff), (half + ff, ff), (half + 2 * ff, ff), (0, half)]
    scatter = Scatter(place, w_ref, sum_ref, cuts, (mid, far, path), sems[:8])
    parts = range(len(cuts))
    for part in parts[:-1]:
        scatter.begin(part)
    scatter.merge(0, 0)
    scatter.merge(0, 1)
    merges = [functools.partial(scatter.merge, part, which) for part in (1, 2) for which in (0, 1)]
    for step in merges:
        step()


    def finish(index, carry):
        rows = chunk_rows(index)
        in_copy(index).wait_recv()
        grad = in_own[rows, :].astype(F32) + in_in[rows, :].astype(F32)
        middle = middle_ref[rows, :]
        scale = lax.rsqrt(jnp.mean(middle * middle, axis=-1, keepdims=True) + 1e-06)
        unit = middle * scale
        gffn_ref[...] += jnp.sum(grad * unit, axis=0, keepdims=True)
        grad = grad * gain_ref[...]
        seed = cot_ref[rows, :].astype(F32) * row_weight
        total = seed + scale * (grad - unit * jnp.mean(unit * grad, axis=-1, keepdims=True))
        back_ref[rows, :] = total
        low = total.astype(BF)
        seed_low[rows, :] = low
        dgated_ref[rows, :] = product(low, flat(w_ref, 0, half))
        return carry

    half_way = chunks // 2
    lax.fori_loop(half_way, chunks, finish, 0)
    streams_first = streams(blocks - 1, (blocks - 1) % 2)
    for copy in streams_first:
        copy.start()

    def weigh_out(index, carry):
        cols = pl.ds(pl.multiple_of(index * DK, DK), DK)
        put_blocks(w_ref, index, slice(0, half), product(seed_low[:, cols], gated_ref[...], TN))
        return carry

    swap = remote(attn_own, attn_in, o_send, o_recv, place.peer)
    load_front.start()


    masks = block_masks()
    t_row, t_col, p_row, p_col = masks
    strict = p_row > p_col
    for head in range(heads):
        dstate[head] = jnp.zeros((DK, DK), F32)
    dgain_ref[...] = jnp.zeros_like(dgain_ref)
    dconv_ref[...] = jnp.zeros_like(dconv_ref)
    dscal_ref[...] = jnp.zeros_like(dscal_ref)
    dy_next[...] = jnp.zeros_like(dy_next)
    doc_cols[0:PAD, :] = jnp.full((PAD, DK), -1.0, F32)
    doc_cols[PAD + seq :, :] = jnp.full((PAD, DK), -1.0, F32)
    for i in range(seq // DK):
        lane_docs = docs_ref[:, i * DK : (i + 1) * DK].astype(F32)
        doc_cols[PAD + i * DK : PAD + (i + 1) * DK, :] = jnp.broadcast_to(lane_docs, (DK, DK)).T
    upper = (iota((STRETCH, STRETCH), 0) <= iota((STRETCH, STRETCH), 1)).astype(F32)
    lanes = iota((STRETCH, DK), 1)
    wide_rows = iota((span, DK), 0)
    select = scalar_select(side, heads)
    rate = -jnp.exp(rates_ref[0:1, :])
    scal_at = 6 * half
    scal_cols = slice(scal_at, scal_at + DK)

    chains = [scatter.stages(part) for part in parts]
    slots = [[] for _ in range(blocks)]
    left = []
    slots[blocks // 2] += [functools.partial(scatter.merge, parts[-1], which) for which in (0, 1)]
    for part, turn in ((0, 1), (1, 3), (2, 6)):
        for step in chains[part]:
            (slots[turn] if turn < blocks else left).append(step)
            turn += step is not chains[part][0]

    def back(step, carry):
        block = blocks - 1 - step
        top = pl.multiple_of(block * STRETCH, STRETCH)
        rows = pl.ds(top, STRETCH)
        slot = lax.rem(block, 2)
        for copy in streams(block, slot):
            copy.wait()

        def fetch():
            for copy in streams(block - 1, 1 - slot):
                copy.start()

        pl.when(block > 0)(fetch)
        aux = aux_s[slot]
        aux2, run2, aux_t, run_t = block_scalars(aux)
        doc_window = doc_cols[pl.ds(top, STRETCH + 2 * PAD), :]
        same = same_documents(doc_window[: STRETCH + PAD])
        here = doc_window[PAD : PAD + STRETCH]
        same_next = [doc_window[PAD + o : PAD + o + STRETCH] == here for o in range(1, KW)]
        dbeta_all = jnp.zeros((STRETCH, DK), F32)
        drun_all = jnp.zeros((STRETCH, DK), F32)
        column_sums = jnp.zeros((span, DK), F32)

        def conv_back(kind, head, grad):
            first_col = (0, 2, 3, 4, 5)[kind] * half + head * DK
            cols = slice(head * DK, (head + 1) * DK)
            window = pre_s[slot, :, first_col : first_col + DK]
            kernel = conv_ref[kind, :, cols]
            shifted = [window[PAD:]] + [
                jnp.where(same[o - 1], window[PAD - o : PAD - o + STRETCH], 0.0) for o in range(1, KW)
            ]
            y = shifted[0] * kernel[0:1]
            for o in range(1, KW):
                y = y + shifted[o] * kernel[o : o + 1]
            sigmoid = jax.nn.sigmoid(y)
            act = y * sigmoid
            if kind < 3:
                scale = lax.rsqrt(jnp.sum(act * act, axis=-1, keepdims=True) + 1e-06)
                unit = act * scale
                if kind == 0:
                    grad = grad * DK ** (-0.5)
                grad = scale * (grad - unit * jnp.sum(unit * grad, axis=-1, keepdims=True))
            dy = grad * (sigmoid * (1.0 + y * (1.0 - sigmoid)))
            for o in range(KW):
                dconv_ref[kind, o : o + 1, cols] += jnp.sum(dy * shifted[o], axis=0, keepdims=True)
            at = slice(kind * half + head * DK, kind * half + (head + 1) * DK)
            longer = jnp.concatenate([dy, dy_next[:, at]], axis=0)
            dy_next[:, at] = dy[:PAD]
            dpre = dy * kernel[0:1]
            for o in range(1, KW):
                dpre = dpre + jnp.where(same_next[o - 1], longer[o : o + STRETCH], 0.0) * kernel[o : o + 1]
            work[rows, first_col : first_col + DK] = dpre.astype(BF)

        def of_head(head):
            nonlocal dbeta_all, drun_all, column_sums
            cols = slice(head * DK, (head + 1) * DK)
            gate_cols = slice(half + head * DK, half + (head + 1) * DK)
            beta, run_col, run_row, doc_col, doc_row, carried, to_last = head_terms(
                aux, aux2, run2, aux_t, run_t, head, heads
            )
            decay = decay_matrix(run_col, run_row, doc_col, doc_row, p_row, p_col)
            keys = jnp.concatenate([k_s[slot, 0, :, cols], k_s[slot, 1, :, cols]], axis=0)
            queries = q_s[slot, :, cols]
            mixed = mixed_s[slot, :, cols]
            gate = pre_s[slot, PAD:, gate_cols]
            sigmoid = jax.nn.sigmoid(gate)
            silu = gate * sigmoid
            scale = lax.rsqrt(jnp.mean(mixed * mixed, axis=-1, keepdims=True) + 1e-05)
            scaled = mixed * scale
            dgated = dgated_ref[rows, cols]
            part = dgated * scaled
            work[rows, gate_cols] = (
                part * mix_ref[...] * (sigmoid * (1.0 + gate * (1.0 - sigmoid)))
            ).astype(BF)
            dgain_ref[...] += jnp.sum(part * silu, axis=0, keepdims=True)
            dscaled = dgated * mix_ref[...] * silu
            dout = scale * (dscaled - scaled * jnp.mean(dscaled * scaled, axis=-1, keepdims=True))

            state, pseudo = state_s[slot, head], pseudo_s[slot, head]
            yield
            dnext = dstate[head]
            dnext_parts, state_parts, pseudo_parts = split(dnext), split(state), split(pseudo)
            dout_parts, q_parts = split(dout), split(queries)
            gram = dot1(keys, keys, NT)
            core = jnp.where(strict, decay * gram, 0.0)
            yield
            amat = beta * core
            qdecay = decay[STRETCH:]
            attn = qdecay * dot3(q_parts, keys, NT)
            yield
            dattn = dot3(dout_parts, pseudo_parts, NT)
            dqk = split(qdecay * dattn)
            yield
            dpseudo = dot3(attn, dout_parts, TN) + to_last * dot3(keys, dnext_parts)
            yield
            dtarget = dot3(inv_s[slot, head], dpseudo, TN)
            yield
            dtarget_parts = split(dtarget)
            damat = jnp.where(strict, -dot3(dtarget_parts, pseudo_parts, NT), 0.0)
            e_a, e_m = damat * amat, dattn * attn
            yield
            dgram = split(beta * decay * damat)
            dbeta = jnp.sum(dtarget * pseudo, axis=-1, keepdims=True) / jnp.maximum(beta, 1e-30)
            dvalues = (beta * dtarget).astype(BF).astype(F32)
            dread = -(beta * carried) * dtarget
            dout_c = carried[STRETCH:] * dout
            dread_parts, dout_c_parts = split(dread), split(dout_c)
            last = carried[span - 1 : span]
            yield
            dstate[head] = last * dnext + dot3(keys, dread_parts, TN) + dot3(q_parts, dout_c_parts, TN)
            yield
            dq_state = dot3(dout_c_parts, state_parts, NT)
            dk_state = dot3(dread_parts, state_parts, NT)
            yield
            dk_last = dot3(to_last * pseudo, dnext_parts, NT)
            yield
            conv_back(0, head, dq_state + dot3(dqk, keys))
            yield
            dkeys = (
                dk_state + dk_last + dot3(dgram, keys) + dot3(dgram, keys, TN) + dot3(dqk, q_parts, TN)
            ).astype(BF).astype(F32)
            yield
            conv_back(1, head, dkeys[:STRETCH])
            yield
            conv_back(2, head, dkeys[STRETCH:])
            yield
            conv_back(3, head, dvalues[:STRETCH])
            yield
            conv_back(4, head, dvalues[STRETCH:])

            yield
            wide = keys.astype(F32)
            e_last = jnp.sum(wide * dk_last, axis=-1, keepdims=True)
            drun = jnp.sum(e_a, axis=-1, keepdims=True) - e_last + jnp.sum(wide * dk_state, axis=-1, keepdims=True)
            drun_q = jnp.sum(e_m, axis=-1, keepdims=True) + jnp.sum(queries * dq_state, axis=-1, keepdims=True)
            at_last = jnp.sum(e_last, axis=0, keepdims=True) + last * jnp.sum(
                jnp.sum(dnext * state, axis=-1, keepdims=True), axis=0, keepdims=True
            )
            drun = drun[:STRETCH] + drun[STRETCH:] + drun_q
            drun = drun + jnp.where(iota((STRETCH, 1), 0) == STRETCH - 1, at_last, 0.0)
            lane = 2 * heads + head
            drun_all = jnp.where(lanes == lane, drun, drun_all)
            dbeta_all = jnp.where(lanes == head, dbeta[:STRETCH], dbeta_all)
            dbeta_all = jnp.where(lanes == heads + head, dbeta[STRETCH:], dbeta_all)
            sums = jnp.sum(e_a, axis=0, keepdims=True) + jnp.sum(e_m, axis=0, keepdims=True)
            column_sums = jnp.where(wide_rows == lane, sums, column_sums)
        for _ in itertools.zip_longest(*[of_head(head) for head in range(heads)]):
            pass
        down = column_sums.T
        ddecay = dot6(upper, drun_all - down[:STRETCH] - down[STRETCH:])
        raw = dot6(pre_s[slot, PAD:, scal_cols], select)
        sigmoid = jax.nn.sigmoid(raw)
        shifted = raw + rates_ref[1:2, :]
        draw_decay = ddecay * rate * jax.nn.sigmoid(shifted)
        is_decay = (lanes >= 2 * heads) & (lanes < 3 * heads)
        draw_decay = jnp.where(is_decay, draw_decay, 0.0)
        dscal_ref[0:1, :] += jnp.sum(
            jnp.where(is_decay, ddecay * rate * softplus(shifted), 0.0), axis=0, keepdims=True
        )
        dscal_ref[1:2, :] += jnp.sum(draw_decay, axis=0, keepdims=True)
        dbeta_low = dbeta_all.astype(BF).astype(F32)
        draw = jnp.where(lanes < 2 * heads, dbeta_low * 2.0 * sigmoid * (1.0 - sigmoid), draw_decay)
        work[rows, scal_cols] = dot6(draw, select, NT).astype(BF)
        run_slot(slots, step)
        return carry

    lax.fori_loop(0, blocks // 2, back, 0)
    lax.fori_loop(0, half_way, finish, 0)
    lax.fori_loop(0, width // DK, weigh_out, 0)
    scatter.begin(parts[-1])
    swap.start()
    lax.fori_loop(blocks // 2, blocks, back, 0)
    mix_swap = remote(dgain_ref, mix_in, m_send.at[2], m_recv.at[2], place.peer)
    mix_swap.start()

    def normalise(index, carry):
        rows = chunk_rows(index)
        x = x_ref[rows, :].astype(F32)
        scale = lax.rsqrt(jnp.mean(x * x, axis=-1, keepdims=True) + 1e-06)
        normed[rows, :] = (x * scale * norm_ref[...]).astype(BF)
        return carry

    lax.fori_loop(0, chunks, normalise, 0)

    def in_sent(index, carry):
        in_copy(index).wait_send()
        return carry

    lax.fori_loop(0, chunks, in_sent, 0)

    def weigh_front(index, carry):
        cols = pl.ds(pl.multiple_of(index * DK, DK), DK)
        put_blocks(w_ref, index, slice(0, front_width), product(normed[:, cols], work[:, 0:front_width], TN))
        return carry

    for part in parts:
        scatter.drain_sibling(part)
    lax.fori_loop(0, width // DK, weigh_front, 0)

    def release(stage):
        for part in ((0, 1), (2, 3))[stage]:
            scatter.drain(part)
        sem = free_sem.at[stage]
        for device in (place.sibling, place.across):
            pl.semaphore_signal(sem, inc=1, device_id=device, device_id_type=MESH)
        for way in (0, 1):
            pl.when(place.can_send[way])(
                lambda way=way: pl.semaphore_signal(sem, inc=1, device_id=place.ahead[way], device_id_type=MESH)
            )

    def await_release(stage):
        senders = 2 + place.can_send[0].astype(jnp.int32) + place.can_send[1].astype(jnp.int32)
        pl.semaphore_wait(free_sem.at[stage], senders)

    cuts = [(2 * half, 2 * half), (4 * half, 2 * half + DK), (0, half), (half, half)]
    later = Scatter(place, w_ref, total, cuts, (mid, far, path), sems[8:])
    release(0)
    await_release(0)
    later.begin(0)
    later.begin(1)
    load_front.wait()

    def outputs(index, carry):
        rows = chunk_rows(index)
        both = attn_own[rows, :].astype(F32) + attn_in[rows, :].astype(F32)
        out_ref[rows, :] = (middle_ref[rows, :] + both).astype(BF)
        return carry

    def nb_copy(index):
        rows = chunk_rows(index)
        return remote(in_own.at[rows], in_in.at[rows], n_send.at[index], n_recv.at[index], place.peer)

    def project_back(index):
        rows = pair_rows(index)
        in_own[rows, :] = product(work[rows, 0:front_width], flat(fw_ref, 0, front_width), NT).astype(BF)
        nb_copy(2 * index).start()
        nb_copy(2 * index + 1).start()

    swap.wait_recv()
    project_back(0)
    later.merge(0, 0)
    later.merge(0, 1)
    for step in left + chains[3][:2]:
        step()
    for index in range(1, chunks // 2):
        project_back(index)
    later.merge(1, 0)
    later.merge(1, 1)
    chains[3][2]()
    lax.fori_loop(0, chunks, outputs, 0)
    for step in chains[3][3:]:
        step()
    release(1)
    await_release(1)
    later.begin(2)
    later.begin(3)
    gnorm_ref[...] = jnp.zeros_like(gnorm_ref)

    def finish_back(index, carry):
        rows = chunk_rows(index)
        nb_copy(index).wait_recv()
        back = in_own[rows, :].astype(F32) + in_in[rows, :].astype(F32)
        x = x_ref[rows, :].astype(F32)
        scale = lax.rsqrt(jnp.mean(x * x, axis=-1, keepdims=True) + 1e-06)
        unit = x * scale
        gnorm_ref[...] += jnp.sum(back * unit, axis=0, keepdims=True)
        back = back * norm_ref[...]
        total_back = back_ref[rows, :] + scale * (back - unit * jnp.mean(unit * back, axis=-1, keepdims=True))
        igrad_ref[rows, :] = total_back.astype(BF)
        return carry

    small_swaps = [
        remote(small, small_in.at[0], m_send.at[0], m_recv.at[0], place.sibling),
        remote(small_sum, small_in.at[1], m_send.at[1], m_recv.at[1], place.across),
    ]

    def line_copy(target):
        device = (target * 4 + place.x * 2 + place.c, side)
        return remote(small_line.at[place.z], small_line.at[place.z], l_send.at[target], l_recv.at[place.z], device)

    def line_from(source):
        device = (source * 4 + place.x * 2 + place.c, side)
        return remote(small_line.at[source], small_line.at[source], l_send.at[source], l_recv.at[source], device)

    def collect():
        mix_swap.wait_recv()
        small[0:5] = dconv_ref[...]
        for i in range(2):
            small[5, i : i + 1, :] = gnorm_ref[:, i * half : (i + 1) * half]
            small[5, 2 + i : 3 + i, :] = gffn_ref[:, i * half : (i + 1) * half]
        small[6] = jnp.zeros((KW, half), F32)
        small[6, 0:1, 0:DK] = dgain_ref[...] + mix_in[...]
        small[6, 0:1, DK : 2 * DK] = dscal_ref[0:1, :]
        small[6, 0:1, 2 * DK : 3 * DK] = dscal_ref[1:2, :]
        small_swaps[0].start()

    def collect_across():
        small_swaps[0].wait_recv()
        small_sum[...] = small[...] + small_in[0]
        small_swaps[1].start()

    def collect_line():
        small_swaps[1].wait_recv()
        small_line[place.z] = small_sum[...] + small_in[1]
        for target in range(line):
            pl.when(target != place.z)(lambda target=target: line_copy(target).start())

    home = [
        remote(
            total.at[:, pl.ds(pl.multiple_of((base + 1 - side) * half, half), half)],
            ref.at[:, pl.ds(pl.multiple_of(side * half, half), half)],
            h_send.at[i], h_recv.at[i], place.peer,
        )
        for i, (base, ref) in enumerate(((2, gk_ref), (4, gv_ref)))
    ]
    scal_home = remote(total.at[:, scal_at : scal_at + DK], scal_in, h_send.at[2], h_recv.at[2], place.peer)
    own_half = pl.ds(pl.multiple_of(side * half, half), half)

    def at_home(i):
        base, ref = ((2, gk_ref), (4, gv_ref))[i]
        home[i].start()
        ref[:, own_half] = total[:, pl.ds(pl.multiple_of((base + side) * half, half), half)]

    def at_home_value():
        at_home(1)
        scal_home.start()

    after = [later.stages(part) for part in range(4)]
    homes = [functools.partial(at_home, 0), at_home_value]
    merge = functools.partial
    slots = [
        [merge(later.merge, 2, 0), merge(later.merge, 2, 1)],
        [merge(later.merge, 3, 0), merge(later.merge, 3, 1)],
        after[0][:2],
        after[0][2:3],
    ]

    def finish_and(index, carry):
        finish_back(index, carry)
        run_slot(slots, index)
        return carry

    lax.fori_loop(0, chunks, finish_and, 0)
    rest = after[0][3:-1] + after[1][:2] + after[0][-1:] + homes[:1] + after[1][2:-1] + after[2][:2] + after[1][-1:]
    rest += homes[1:] + after[3][:2]
    for pair in zip(after[2][2:], after[3][2:]):
        rest += pair
    extra = [collect, collect_across, collect_line]
    for i, step in enumerate(rest):
        if i % 2 == 0 and extra:
            extra.pop(0)()
        step()
    for step in extra:
        step()
    for source in range(line):
        pl.when(source != place.z)(lambda source=source: line_from(source).wait_recv())
    summed = small_line[0]
    for source in range(1, line):
        summed = summed + small_line[source]
    small_sum_out = summed
    gcq_ref[...] = small_sum_out[0]
    small_swaps[0].wait_send()
    small_swaps[1].wait_send()
    small[...] = small_sum_out
    conv_home = [
        remote(
            small.at[base + 1 - side], ref.at[:, own_half], h_send.at[i], h_recv.at[i], place.peer
        )
        for i, (base, ref) in ((3, (1, gck_ref)), (4, (3, gcv_ref)))
    ]
    for copy in conv_home:
        copy.start()
    gck_ref[:, own_half] = small[1 + side]
    gcv_ref[:, own_half] = small[3 + side]
    for i in range(2):
        gnorm_ref[:, i * half : (i + 1) * half] = small_sum_out[5, i : i + 1]
        gffn_ref[:, i * half : (i + 1) * half] = small_sum_out[5, 2 + i : 3 + i]
    gtiny_ref[...] = small_sum_out[6, 0:1, 0 : 3 * DK]
    gq_ref[...] = total[:, 0:half]
    gg_ref[...] = total[:, half : 2 * half]
    scal_home.wait_recv()
    lanes = iota(scal_in.shape, 1)
    ours = total[:, scal_at : scal_at + DK]
    theirs = pltpu.roll(scal_in[...], DK - 2 * heads, 1)
    gs_ref[...] = jnp.where(lanes < 2 * heads, ours + theirs, ours)
    for copy in home + conv_home:
        copy.wait_recv()
    for copy in home + conv_home + [scal_home, mix_swap]:
        copy.wait_send()
    for target in range(line):
        pl.when(target != place.z)(lambda target=target: line_copy(target).wait_send())

    def sent(index, carry):
        nb_copy(index).wait_send()
        return carry

    lax.fori_loop(0, chunks, sent, 0)
    for part in range(4):
        later.drain_sibling(part)
        later.drain(part)
    swap.wait_send()


def rest_call(line, gated, x, cot, middle, domains, gain, norm, docs, conv, rates, mix, w, fw, pre, q, k, v, aux, mixed, inv, state, pseudo):
    seq, width = x.shape
    half = gated.shape[1]
    heads = half // DK
    depth, tail = w.shape[3:]
    columns = fw.shape[-1]
    ff = (tail - half) // 3
    shape = jax.ShapeDtypeStruct
    dma = pltpu.SemaphoreType.DMA
    chunks = seq // CHUNK
    span = 2 * STRETCH
    tiny = (7, KW, half)
    low = pltpu.VMEM((seq, width), BF)
    wide = pltpu.VMEM((seq, width), F32)
    return pl.pallas_call(
        functools.partial(rest_kernel, line, heads),
        out_shape=(
            shape((seq, width), BF),
            shape((seq, width), BF),
            shape((depth, tail), F32),
            shape((depth, half), F32),
            shape((depth, half), F32),
            shape((depth, 2 * half), F32),
            shape((depth, 2 * half), F32),
            shape((depth, DK), F32),
            shape((KW, half), F32),
            shape((KW, 2 * half), F32),
            shape((KW, 2 * half), F32),
            shape((1, width), F32),
            shape((1, width), F32),
            shape((1, 3 * DK), F32),
        ),
        in_specs=[VMEM] * 11 + [pl.BlockSpec(memory_space=pl.ANY)] * 11,
        out_specs=(VMEM,) * 14,
        scratch_shapes=[
            pltpu.VMEM(w.shape, BF),
            pltpu.VMEM(fw.shape, BF),
        ]
        + [low] * 6
        + [pltpu.VMEM((seq, 3 * ff), BF), wide, pltpu.VMEM((seq, half), F32)]
        + [
            pltpu.VMEM((heads, DK, DK), F32),
            pltpu.VMEM((seq + 2 * PAD, DK), F32),
            pltpu.VMEM((PAD, 5 * half), F32),
            pltpu.VMEM((5, KW, half), F32),
            pltpu.VMEM((2, DK), F32),
            pltpu.VMEM((1, DK), F32),
            pltpu.VMEM((depth, columns), F32),
        ]
        + scatter_scratch(line, depth, tail, False)
        + [
            pltpu.VMEM((2, STRETCH + PAD, columns), F32),
            pltpu.VMEM((2, STRETCH, half), F32),
            pltpu.VMEM((2, 2, STRETCH, half), BF),
            pltpu.VMEM((2, 2, STRETCH, half), BF),
            pltpu.VMEM((2, STRETCH, DK), F32),
            pltpu.VMEM((2, STRETCH, half), F32),
            pltpu.VMEM((2, heads, span, span), F32),
            pltpu.VMEM((2, heads, DK, DK), F32),
            pltpu.VMEM((2, heads, span, DK), F32),
        ]
        + [
            pltpu.VMEM(tiny, F32),
            pltpu.VMEM((2,) + tiny, F32),
            pltpu.VMEM((line,) + tiny, F32),
            pltpu.VMEM(tiny, F32),
            pltpu.VMEM((1, DK), F32),
            pltpu.VMEM((depth, DK), F32),
        ]
        + [dma((4,)), dma((2, 9))]
        + [dma((chunks,))] * 2
        + [dma, dma]
        + [dma((chunks,)), dma((chunks,)), dma((5,)), dma((5,)), dma((3,)), dma((3,)), dma((line,)), dma((line,))]
        + [pltpu.SemaphoreType.REGULAR((2,))]
        + scatter_sems(line, 4)
        + scatter_sems(line, 4),
        compiler_params=pltpu.CompilerParams(
            collective_id=1, has_side_effects=True, vmem_limit_bytes=63 << 20
        ),
        name="rest",
    )(gated, x, cot, middle, domains, gain, norm, docs, conv, rates, mix, w, fw, pre, q, k, v, aux, mixed, inv, state, pseudo)


def deliver_kernel(heads, *refs):
    count = (len(refs) - 21) // 2
    sources, outs, held, sems = refs[:count], refs[count : count + 20], refs[count + 20 : -1], refs[-1]
    copies = [pltpu.make_async_copy(src, dst, sems.at[i]) for i, (src, dst) in enumerate(zip(sources, held))]
    for copy in copies:
        copy.start()
    (
        out_ref, igrad_ref, sum_ref, gq_ref, gg_ref, gk_ref, gv_ref, gs_ref, gcq_ref, gck_ref, gcv_ref, gnorm_ref,
        gffn_ref, gtiny_ref,
    ) = held
    (
        output, input_grad, norm, query, outgate, key, value, beta, alpha, log, bias, c_query, c_key, c_value, mix,
        w_out, ffn, gate, up, down,
    ) = outs
    for copy in copies:
        copy.wait()
    output[0] = out_ref[...]
    input_grad[0] = igrad_ref[...]
    norm[...] = gnorm_ref[...]
    ffn[...] = gffn_ref[...]
    query[...] = gq_ref[...]
    outgate[...] = gg_ref[...]
    key[0] = gk_ref[...]
    value[0] = gv_ref[...]
    depth, half = query.shape
    ff = gate.shape[1]
    corner = (iota((depth, depth), 0) == iota((depth, depth), 1)).astype(F32)
    turned = dot6(gs_ref[...], corner, TN)
    beta[...] = turned[0 : 2 * heads]
    alpha[...] = turned[4 * heads : 5 * heads]
    here = slice(2 * heads, 3 * heads)
    log[...] = gtiny_ref[:, DK : 2 * DK][:, here]
    bias[...] = gtiny_ref[:, 2 * DK :][:, here]
    mix[...] = gtiny_ref[:, 0:DK]
    c_query[...] = gcq_ref[...]
    c_key[0] = gck_ref[...]
    c_value[0] = gcv_ref[...]
    w_out[...] = sum_ref[:, 0:half]
    gate[...] = sum_ref[:, half : half + ff]
    up[...] = sum_ref[:, half + ff : half + 2 * ff]
    down[...] = sum_ref[:, half + 2 * ff :]


def deliver_call(heads, *parts):
    seq, width = parts[0].shape
    depth, tail = parts[2].shape
    half = parts[3].shape[1]
    ff = (tail - half) // 3
    shape = lambda *dims: jax.ShapeDtypeStruct(dims, F32)
    low = jax.ShapeDtypeStruct((1, seq, width), BF)
    return pl.pallas_call(
        functools.partial(deliver_kernel, heads),
        out_shape=(
            low, low, shape(1, width), shape(depth, half), shape(depth, half), shape(1, depth, 2 * half),
            shape(1, depth, 2 * half), shape(2 * heads, depth), shape(heads, depth), shape(1, heads),
            shape(1, heads), shape(KW, half), shape(1, KW, 2 * half), shape(1, KW, 2 * half), shape(1, DK),
            shape(depth, half), shape(1, width), shape(depth, ff), shape(depth, ff), shape(depth, ff),
        ),
        in_specs=[pl.BlockSpec(memory_space=pl.ANY)] * 14,
        out_specs=(VMEM,) * 20,
        scratch_shapes=[pltpu.VMEM(part.shape, part.dtype) for part in parts]
        + [pltpu.SemaphoreType.DMA((len(parts),))],
        compiler_params=pltpu.CompilerParams(vmem_limit_bytes=63 << 20),
        name="deliver",
    )(*parts)


GROUPS = 8


def per_device(
    tokens,
    cotangent,
    domains,
    doc_ids,
    norm_gain,
    w_query,
    w_outgate,
    w_key,
    w_value,
    w_beta,
    w_alpha,
    decay_log,
    decay_bias,
    conv_query,
    conv_key,
    conv_value,
    mix_gain,
    w_out,
    ffn_gain,
    w_gate,
    w_up,
    w_down,
):
    line = lax.axis_size("dp") // 4
    by_place = lambda array: array.reshape((line, 2, 2) + array.shape[1:])
    gain_row = mix_gain[None]
    (
        gated, middle, conv, rates, mixed, inv, state, pseudo, pre, queries, keys, values, aux, front_w, back_w
    ) = front_call(
        line, tokens[0], doc_ids, norm_gain[None], w_query, w_outgate, w_key[0], w_value[0], w_beta[0].T, w_alpha.T,
        w_out.T, w_gate, w_up, w_down.T, decay_log[None], decay_bias[None], conv_query, conv_key[0], conv_value[0],
        gain_row,
    )
    parts = rest_call(
        line, gated, tokens[0], cotangent[0], middle, domains[None], ffn_gain[None], norm_gain[None], doc_ids, conv,
        rates, gain_row, by_place(back_w), by_place(front_w), pre, queries, keys, values, aux, mixed, inv, state,
        pseudo,
    )
    results = list(deliver_call(w_alpha.shape[1], *parts))
    for index in (2, 9, 10, 14, 16):
        results[index] = results[index][0]
    for index in (8, 15, 19):
        results[index] = results[index].T
    results[7] = results[7].T[None]
    return tuple(results)


def solution(mesh):
    return jax.shard_map(
        per_device,
        mesh=mesh,
        in_specs=(
            P("dp", None, None),
            P("dp", None, None),
            P(),
            P("dp", None),
            P(),
            P("dp", "step"),
            P("dp", "step"),
            P("step", "dp", None),
            P("step", "dp", None),
            P("step", "dp", None),
            P("dp", "step"),
            P("step"),
            P("step"),
            P(None, "step"),
            P("step", None, None),
            P("step", None, None),
            P(),
            P("step", "dp"),
            P(),
            P("dp", "step"),
            P("dp", "step"),
            P("step", "dp"),
        ),
        out_specs=(
            P("dp", None, None),
            P("dp", None, None),
            P(),
            P("dp", "step"),
            P("dp", "step"),
            P("step", "dp", None),
            P("step", "dp", None),
            P("step", "dp", None),
            P("dp", "step"),
            P("step"),
            P("step"),
            P(None, "step"),
            P("step", None, None),
            P("step", None, None),
            P(),
            P("step", "dp"),
            P(),
            P("dp", "step"),
            P("dp", "step"),
            P("step", "dp"),
        ),
        check_vma=False,
    )
```

```python
import functools
import itertools

import jax
import jax.numpy as jnp
from jax import lax
from jax.experimental import pallas as pl
from jax.experimental.pallas import tpu as pltpu
from jax.sharding import PartitionSpec as P

STRETCH = 64
DK = 128
F32 = jnp.float32
BF = jnp.bfloat16
NN = ((1,), (0,))
NT = ((1,), (1,))
TN = ((0,), (0,))


def split(a):
    if a.dtype == BF:
        return (a,)
    hi = a.astype(BF)
    return (hi, (a - hi.astype(F32)).astype(BF))


def dot1(a, b, dims=NN):
    return lax.dot_general(a.astype(BF), b.astype(BF), (dims, ((), ())), preferred_element_type=F32)


def dot3(a, b, dims=NN):
    a = a if isinstance(a, tuple) else split(a)
    b = b if isinstance(b, tuple) else split(b)
    one = lambda x, y: lax.dot_general(x, y, (dims, ((), ())), preferred_element_type=F32)
    out = one(a[0], b[0])
    if len(a) > 1:
        out = out + one(a[1], b[0])
    if len(b) > 1:
        out = out + one(a[0], b[1])
    return out


def dot6(a, b, dims=NN):
    return lax.dot_general(
        a, b, (dims, ((), ())), precision=lax.Precision.HIGHEST, preferred_element_type=F32
    )


def iota(shape, dim):
    return lax.broadcasted_iota(jnp.int32, shape, dim)


def product(first, second, dims=NN):
    return lax.dot_general(first, second, (dims, ((), ())), preferred_element_type=F32)


def block_masks():
    span = 2 * STRETCH
    row, col = iota((span, span), 0), iota((span, span), 1)
    t_row, t_col = row % STRETCH, col % STRETCH
    p_row, p_col = 2 * t_row + row // STRETCH, 2 * t_col + col // STRETCH
    return t_row, t_col, p_row, p_col


def twice(block):
    return jnp.concatenate([block, block], axis=0)


def block_scalars(aux):
    low = (iota((STRETCH, STRETCH), 0) >= iota((STRETCH, STRETCH), 1)).astype(F32)
    running = dot6(low, aux)
    aux2, run2 = twice(aux), twice(running)
    return aux2, run2, aux2.T, run2.T


def head_terms(aux, aux2, run2, aux_t, run_t, head, heads):
    beta = jnp.concatenate(
        [aux[:, head : head + 1], aux[:, heads + head : heads + head + 1]], axis=0
    )
    lane = 2 * heads + head
    run_col = run2[:, lane : lane + 1]
    run_row = run_t[lane : lane + 1, :]
    doc_lane = 3 * heads
    doc_col = aux2[:, doc_lane : doc_lane + 1]
    doc_row = aux_t[doc_lane : doc_lane + 1, :]
    fresh = aux2[:, doc_lane + 1 : doc_lane + 2]
    span = 2 * STRETCH
    carried = jnp.where(fresh > 0.5, jnp.exp(run_col), 0.0)
    last_run = run_col[span - 1 : span, :]
    to_last = jnp.where(doc_col == doc_col[span - 1 : span, :], jnp.exp(last_run - run_col), 0.0)
    return beta, run_col, run_row, doc_col, doc_row, carried, to_last


def decay_matrix(run_col, run_row, doc_col, doc_row, p_row, p_col):
    inside = (p_row >= p_col) & (doc_col == doc_row)
    return jnp.where(inside, jnp.exp(jnp.where(inside, run_col - run_row, 0.0)), 0.0)


def inverse(mats, masks):
    t_row, t_col, p_row, p_col = masks
    eye = (p_row == p_col).astype(F32)
    pair = (t_row == t_col) & (p_row > p_col)
    out = [eye - jnp.where(pair, a, 0.0) for a in mats]
    level = 1
    while (1 << level) <= STRETCH:
        merge = (
            ((t_row >> level) == (t_col >> level))
            & (((t_row >> (level - 1)) & 1) == 1)
            & (((t_col >> (level - 1)) & 1) == 0)
        )
        low = [x.astype(BF) for x in out]
        half = [dot1(x, jnp.where(merge, a, 0.0)) for x, a in zip(low, mats)]
        out = [o - dot1(h, x) for o, h, x in zip(out, half, low)]
        level += 1
    rest = [eye - x - dot3(a, x) for a, x in zip(mats, out)]
    return [x + dot1(x, r) for x, r in zip(out, rest)]


VMEM = pl.BlockSpec(memory_space=pltpu.VMEM)


MESH = pl.DeviceIdType.MESH


class Place:
    def __init__(self, line):
        self.line = line
        self.dp, self.side = lax.axis_index("dp"), lax.axis_index("step")
        self.z, self.x, self.c = self.dp // 4, (self.dp // 2) % 2, self.dp % 2
        self.sibling = (self.dp + 1 - 2 * self.c, self.side)
        self.across = (self.dp + 2 - 4 * self.x, self.side)
        self.ahead = (
            (lax.rem(self.dp + 4, 4 * line), self.side),
            (lax.rem(self.dp + 4 * line - 4, 4 * line), self.side),
        )
        self.peer = (self.dp, 1 - self.side)
        self.can_send = (self.z + 1 < line, self.z > 0)

    def reaches(self, way, far):
        return self.z - far >= 0 if way == 0 else self.z + far < self.line

    def behind(self, way, far):
        return self.dp - 4 * far if way == 0 else self.dp + 4 * far

    def enter(self, plane=True, peer=True, everyone=False):
        barrier = pltpu.get_barrier_semaphore()

        def greet(device):
            pl.semaphore_signal(barrier, inc=1, device_id=device, device_id_type=MESH)

        count = 0
        if peer:
            greet(self.peer)
            count = 1
        if plane:
            greet(self.sibling)
            greet(self.across)
            count = count + 2
        if everyone:
            for z in range(self.line):
                device = (z * 4 + self.x * 2 + self.c, self.side)
                pl.when(z != self.z)(functools.partial(greet, device))
            count = count + self.line - 1
        elif plane:
            for way in (0, 1):
                pl.when(self.can_send[way])(functools.partial(greet, self.ahead[way]))
            count = count + self.can_send[0].astype(jnp.int32) + self.can_send[1].astype(jnp.int32)
        pl.semaphore_wait(barrier, count)


def remote(src, dst, send_sem, recv_sem, device):
    return pltpu.make_async_remote_copy(
        src_ref=src, dst_ref=dst, send_sem=send_sem, recv_sem=recv_sem,
        device_id=device, device_id_type=MESH,
    )


def gather_sems(line, parts):
    dma = pltpu.SemaphoreType.DMA
    return [
        dma((2, line, parts)), dma((2, line, parts)),
        dma((2, line, parts)), dma((2, line, parts)),
        dma((2, 2, line, parts)), dma((2, 2, line, parts)),
    ]


class Gather:
    def __init__(self, place, buf, cuts, sems):
        self.place, self.buf, self.cuts = place, buf, cuts
        self.zs, self.zr, self.xs, self.xr, self.cs, self.cr = sems

    def block(self, index, part):
        start, width = self.cuts[part]
        return self.buf.at[index, :, pl.ds(start, width)]

    def line_copy(self, index, way, far, part):
        ref = self.block(index, part)
        return remote(ref, ref, self.zs.at[way, far, part], self.zr.at[way, far, part], self.place.ahead[way])

    def across_copy(self, index, way, far, part):
        ref = self.block(index, part)
        return remote(ref, ref, self.xs.at[way, far, part], self.xr.at[way, far, part], self.place.across)

    def sibling_copy(self, index, column, way, far, part):
        ref = self.block(index, part)
        return remote(
            ref, ref, self.cs.at[column, way, far, part], self.cr.at[column, way, far, part], self.place.sibling
        )

    def spread(self, index, way, far, part):
        place = self.place
        for to in (0, 1) if far == 0 else (way,):
            pl.when(place.can_send[to])(lambda to=to: self.line_copy(index, to, far + 1, part).start())
        self.across_copy(index, way, far, part).start()
        self.sibling_copy(index, 0, way, far, part).start()

    def ways(self, far):
        return (0,) if far == 0 else (0, 1)

    def each(self, far, act):
        if far == 0:
            act(0)
            return
        for way in (0, 1):
            pl.when(self.place.reaches(way, far))(functools.partial(act, way))

    def step(self, far, part):
        place = self.place
        if far == 0:
            self.spread(place.dp, 0, 0, part)
            return

        def from_line(way):
            index = place.behind(way, far)
            self.line_copy(index, way, far, part).wait_recv()
            self.spread(index, way, far, part)

        def from_across(way):
            index = place.behind(way, far - 1) + 2 - 4 * place.x
            self.across_copy(index, way, far - 1, part).wait_recv()
            self.sibling_copy(index, 1, way, far - 1, part).start()

        if far < place.line:
            self.each(far, from_line)
        self.each(far - 1, from_across)

    def steps(self):
        return [
            functools.partial(self.step, far, part)
            for far in range(self.place.line + 1)
            for part in range(len(self.cuts))
        ]

    def ready(self, part):
        place = self.place
        for far in range(place.line):
            for column in (0, 1):

                def from_sibling(way):
                    index = place.behind(way, far) + 1 - 2 * place.c + column * (2 - 4 * place.x)
                    self.sibling_copy(index, column, way, far, part).wait_recv()

                self.each(far, from_sibling)

    def drain(self, part):
        place = self.place
        for far in range(place.line):

            def sent(way):
                index = place.behind(way, far)
                for to in (0, 1) if far == 0 else (way,):
                    pl.when(place.can_send[to])(
                        lambda to=to: self.line_copy(index, to, far + 1, part).wait_send()
                    )
                self.across_copy(index, way, far, part).wait_send()
                self.sibling_copy(index, 0, way, far, part).wait_send()
                self.sibling_copy(index + 2 - 4 * place.x, 1, way, far, part).wait_send()

            self.each(far, sent)


def run_slot(slots, turn):
    for index, steps in enumerate(slots):
        if steps:

            def go(steps=steps):
                for step in steps:
                    step()

            pl.when(turn == index)(go)


def deal(steps, turns):
    return [steps[len(steps) * i // turns : len(steps) * (i + 1) // turns] for i in range(turns)]


def scatter_sems(line, parts):
    dma = pltpu.SemaphoreType.DMA
    return [dma((2, parts))] * 4 + [dma((parts,))] * 2 + [dma((2, line, parts))] * 2


def scatter_scratch(line, depth, width, own):
    slots = [pltpu.VMEM((2, line, depth, width), BF), pltpu.VMEM((line, depth, width), BF),
             pltpu.VMEM((2, line, depth, width), BF)]
    return slots + ([pltpu.VMEM((2, line, depth, width), BF)] if own else [])


class Scatter:
    def __init__(self, place, grad, out, cuts, slots, sems, own=None):
        self.place, self.grad, self.out, self.cuts, self.own = place, grad, out, cuts, own
        self.mid, self.far, self.path = slots
        self.cs, self.cr, self.ls, self.lr, self.xs, self.xr, self.zs, self.zr = sems

    def cols(self, part):
        start, width = self.cuts[part]
        return pl.ds(start, width)

    def column(self, which):
        return 1 - self.place.x if which == 0 else self.place.x

    def sibling_copy(self, part, which):
        place, cols, x = self.place, self.cols(part), self.column(which)
        return remote(
            self.grad.at[:, x, 1 - place.c, :, cols], self.mid.at[which, :, :, cols],
            self.cs.at[which, part], self.cr.at[which, part], place.sibling,
        )

    def own_copy(self, part, which):
        cols, x = self.cols(part), self.column(which)
        return pltpu.make_async_copy(
            self.grad.at[:, x, self.place.c, :, cols], self.own.at[which, :, :, cols], self.ls.at[which, part]
        )

    def across_copy(self, part):
        cols = self.cols(part)
        return remote(
            self.mid.at[0, :, :, cols], self.far.at[:, :, cols], self.xs.at[part], self.xr.at[part], self.place.across
        )

    def line_copy(self, part, way, target):
        cols = self.cols(part)
        ref = self.path.at[way, target, :, cols]
        return remote(
            self.mid.at[1, target, :, cols], ref,
            self.zs.at[way, target, part], self.zr.at[way, target, part], self.place.ahead[way],
        )

    def pass_copy(self, part, way, target):
        cols = self.cols(part)
        ref = self.path.at[way, target, :, cols]
        return remote(
            ref, ref, self.zs.at[way, target, part], self.zr.at[way, target, part], self.place.ahead[way]
        )

    def begin(self, part):
        for which in (0, 1):
            if self.own is not None:
                self.own_copy(part, which).start()
            self.sibling_copy(part, which).start()

    def merge(self, part, which):
        self.sibling_copy(part, which).wait_recv()
        if self.own is not None:
            self.own_copy(part, which).wait()
        cols = self.cols(part)
        for target in range(self.place.line):
            if self.own is not None:
                mine = self.own[which, target, :, cols]
            else:
                mine = self.grad[target, self.column(which), self.place.c, :, cols]
            both = self.mid[which, target, :, cols].astype(F32) + mine.astype(F32)
            self.mid[which, target, :, cols] = both.astype(BF)
        if which == 0:
            self.across_copy(part).start()

    def join(self, part):
        self.across_copy(part).wait_recv()
        cols = self.cols(part)
        for target in range(self.place.line):
            both = self.mid[1, target, :, cols].astype(F32) + self.far[target, :, cols].astype(F32)
            self.mid[1, target, :, cols] = both.astype(BF)

    def wave(self, part, turn):
        place, cols = self.place, self.cols(part)
        for way in (0, 1):
            hops = place.z if way == 0 else place.line - 1 - place.z
            target = place.line - 1 - turn + hops if way == 0 else turn - hops

            def start(way=way, target=target):
                self.line_copy(part, way, target).start()

            def go_on(way=way, target=target):
                self.pass_copy(part, way, target).wait_recv()
                both = self.path[way, target, :, cols].astype(F32) + self.mid[1, target, :, cols].astype(F32)
                self.path[way, target, :, cols] = both.astype(BF)
                self.pass_copy(part, way, target).start()

            pl.when(hops == 0)(start)
            pl.when((hops > 0) & (hops <= turn))(go_on)

    def end(self, part):
        place, cols = self.place, self.cols(part)
        start, width = self.cuts[part]
        z = place.z
        self.out[:, cols] = self.mid[1, z, :, cols].astype(F32)

        def take(way):
            self.pass_copy(part, way, z).wait_recv()
            self.out[:, cols] += self.path[way, z, :, cols].astype(F32)

        pl.when(z > 0)(functools.partial(take, 0))
        pl.when(z < place.line - 1)(functools.partial(take, 1))

    def drain_sibling(self, part):
        for which in (0, 1):
            self.sibling_copy(part, which).wait_send()

    def drain(self, part):
        place = self.place
        self.across_copy(part).wait_send()
        for target in range(place.line):
            for way in (0, 1):
                ahead = target > place.z if way == 0 else target < place.z
                pl.when(ahead)(lambda way=way, target=target: self.pass_copy(part, way, target).wait_send())

    def stages(self, part):
        waves = [functools.partial(self.wave, part, turn) for turn in range(self.place.line - 1)]
        return [functools.partial(self.join, part)] + waves + [functools.partial(self.end, part)]


KW = 4
PAD = 8


def conv_window(window, kernel, same):
    rows = window.shape[0] - PAD
    out = window[PAD:] * kernel[0:1]
    for offset in range(1, KW):
        out = out + jnp.where(same[offset - 1], window[PAD - offset : PAD - offset + rows], 0.0) * kernel[offset : offset + 1]
    return out


def same_documents(window):
    rows = window.shape[0] - PAD
    return [window[PAD:] == window[PAD - offset : PAD - offset + rows] for offset in range(1, KW)]


def rows_of(ref, block, count, extra=0):
    return ref[pl.ds(pl.multiple_of(block * STRETCH, STRETCH), count + extra), :]


def scalar_select(side, heads):
    src, dst = iota((DK, DK), 0), iota((DK, DK), 1)
    kind, head = dst // heads, dst % heads
    first = jnp.where(kind == side, 0, 2 * heads)
    source = jnp.where(kind < 2, first + side * heads + head, 4 * heads + head)
    return ((src == source) & (kind < 3)).astype(F32)


def softplus(values):
    return jnp.maximum(values, 0.0) + jnp.log1p(jnp.exp(-jnp.abs(values)))


def front_kernel(
    line, heads, x_ref, docs_ref, norm_ref, wq_ref, wg_ref, wk_ref, wv_ref, beta_ref, alpha_ref, wo_ref, gate_ref,
    up_ref, down_ref, log_ref, bias_ref, cq_ref, ck_ref, cv_ref, mix_ref,
    gated_ref, middle_ref, conv_ref, rates_ref,
    mixed_out, inv_out, state_out, pseudo_out, pre_out, q_out, k_out, v_out, aux_out, front_out, rest_out,
    mixed_ref, inv_ref, state_ref, pseudo_ref, pre_ref, q_ref, k_ref, v_ref, aux_ref,
    front, rest, wo, normed, doc_cols, attn, scal, scal_in, attn_own, attn_in,
    local_sem, y_send, y_recv, a_send, a_recv, *sems,
):
    place = Place(line)
    side = place.side
    seq = x_ref.shape[0]
    depth, half = wq_ref.shape
    span = 2 * STRETCH
    blocks = seq // STRETCH
    scal_at = 6 * half
    me = place.dp
    place.enter()

    own_cols = pl.ds(pl.multiple_of(side * half, half), half)
    other_cols = pl.ds(pl.multiple_of((1 - side) * half, half), half)

    def at(first):
        return pl.ds(pl.multiple_of((first + side) * half, half), half)

    swaps = [
        remote(wk_ref.at[:, other_cols], front.at[me, :, at(2)], y_send.at[0], y_recv.at[0], place.peer),
        remote(wv_ref.at[:, other_cols], front.at[me, :, at(4)], y_send.at[1], y_recv.at[1], place.peer),
        remote(scal, scal_in, y_send.at[2], y_recv.at[2], place.peer),
        remote(ck_ref.at[:, other_cols], conv_ref.at[1 + side], y_send.at[3], y_recv.at[3], place.peer),
        remote(cv_ref.at[:, other_cols], conv_ref.at[3 + side], y_send.at[4], y_recv.at[4], place.peer),
    ]
    scal[...] = jnp.zeros_like(scal)
    corner = (iota((depth, depth), 0) == iota((depth, depth), 1)).astype(BF)
    scal[:, 0 : 2 * heads] = product(corner, beta_ref[...], NT).astype(BF)
    scal[:, 4 * heads : 5 * heads] = product(corner, alpha_ref[...], NT).astype(BF)
    for swap in swaps:
        swap.start()
    ff = gate_ref.shape[1]
    rest[:, 0:half] = wo_ref[...]
    rest[:, half : half + ff] = gate_ref[...]
    rest[:, half + ff : half + 2 * ff] = up_ref[...]
    rest[:, half + 2 * ff : half + 3 * ff] = down_ref[...]
    own_rest = pltpu.make_async_copy(rest, rest_out.at[me], local_sem.at[0])
    own_rest.start()
    rates_ref[...] = jnp.zeros_like(rates_ref)
    rates_ref[0:1, 2 * heads : 3 * heads] = log_ref[...]
    rates_ref[1:2, 2 * heads : 3 * heads] = bias_ref[...]
    front[me, :, 0:half] = wq_ref[...]
    front[me, :, half : 2 * half] = wg_ref[...]
    front[me, :, at(2)] = wk_ref[:, own_cols]
    front[me, :, at(4)] = wv_ref[:, own_cols]
    conv_ref[0] = cq_ref[...]
    conv_ref[1 + side] = ck_ref[:, own_cols]
    conv_ref[3 + side] = cv_ref[:, own_cols]

    head_cuts = [(0, 2 * half), (2 * half, 2 * half), (4 * half, 2 * half + DK)]
    first = Gather(place, front, head_cuts, sems[:6])
    rest_cuts = [(0, half)] + [(half + i * ff, ff) for i in range(3)]
    second = Gather(place, rest_out, rest_cuts, sems[6:])

    first.step(0, 0)
    for swap in swaps:
        swap.wait_recv()
    lanes = iota((depth, DK), 1)
    theirs = pltpu.roll(scal_in[...].astype(F32), 2 * heads, 1)
    ours = scal[...].astype(F32)
    swapped = (lanes >= 2 * heads) & (lanes < 4 * heads)
    front[me, :, scal_at : scal_at + DK] = jnp.where(swapped, theirs, ours).astype(BF)
    for part in (1, 2):
        first.step(0, part)

    def normalise(block, carry):
        rows = pl.ds(pl.multiple_of(block * STRETCH, STRETCH), STRETCH)
        x = x_ref[rows, :].astype(F32)
        scale = lax.rsqrt(jnp.mean(x * x, axis=-1, keepdims=True) + 1e-06)
        normed[rows, :] = (x * scale * norm_ref[...]).astype(BF)
        return carry

    lax.fori_loop(0, blocks, normalise, 0)
    doc_cols[0:PAD, :] = jnp.full((PAD, DK), -1.0, F32)
    for i in range(seq // DK):
        lane_docs = docs_ref[:, i * DK : (i + 1) * DK].astype(F32)
        doc_cols[PAD + i * DK : PAD + (i + 1) * DK, :] = jnp.broadcast_to(lane_docs, (DK, DK)).T
    pre_ref[0:PAD, :] = jnp.zeros((PAD, pre_ref.shape[1]), F32)

    own_rest.wait()
    second.step(0, 0)
    for far in range(1, line + 1):
        if far == line:
            for part in (1, 2, 3):
                second.step(0, part)
        for part in range(3):
            first.step(far, part)
        second.step(far, 0)
    tile = 2 * DK
    for part, (start, width) in enumerate(head_cuts):
        first.ready(part)

        def project(index, carry, start=start):
            cols = pl.ds(pl.multiple_of(start + index * tile, DK), tile)
            weights = front[:, :, cols].reshape(-1, tile)
            pre_ref[PAD:, cols] = jnp.dot(normed[...], weights, preferred_element_type=F32)
            return carry

        lax.fori_loop(0, 2 * half // tile, project, 0)
    scal_cols = slice(scal_at, scal_at + DK)
    pre_ref[PAD:, scal_cols] = jnp.dot(
        normed[...], front[:, :, scal_cols].reshape(-1, DK), preferred_element_type=F32
    )
    keep_front = pltpu.make_async_copy(front, front_out, local_sem.at[1])
    keep_front.start()
    second.ready(0)

    def keep(index, src, dst):
        return pltpu.make_async_copy(src, dst, local_sem.at[index])

    keep_pre = keep(2, pre_ref, pre_out)
    keep_pre.start()
    early = [keep(3, inv_ref, inv_out), keep(4, q_ref, q_out), keep(5, k_ref, k_out), keep(6, v_ref, v_out)]
    early.append(keep(7, aux_ref, aux_out))
    late = [keep(8, mixed_ref, mixed_out), keep(9, state_ref, state_out), keep(10, pseudo_ref, pseudo_out)]
    keep_wo = keep(11, rest_out.at[:, :, pl.ds(0, half)], wo)
    keep_wo.start()

    select = scalar_select(side, heads)
    rate = -jnp.exp(rates_ref[0:1, :])
    masks = block_masks()
    t_row, t_col, p_row, p_col = masks
    together = 2
    turns = blocks // together
    later = [functools.partial(second.step, far, part) for far in range(1, line + 1) for part in (1, 2, 3)]
    spread = len(later) // 2
    slots = deal(later[: spread // 2], turns) + deal(later[spread // 2 : spread], blocks)

    def keys_of(rows, cols):
        return jnp.concatenate([k_ref[0, rows, cols], k_ref[1, rows, cols]], axis=0)

    def prepare_block(block):
        rows = pl.ds(pl.multiple_of(block * STRETCH, STRETCH), STRETCH)
        doc_window = rows_of(doc_cols, block, STRETCH, PAD)
        same = same_documents(doc_window)
        raw = dot6(pre_ref[pl.ds(pl.multiple_of(block * STRETCH, STRETCH) + PAD, STRETCH), scal_cols], select)
        lane = iota((STRETCH, DK), 1)
        beta = (2.0 * jax.nn.sigmoid(raw)).astype(BF).astype(F32)
        decay = rate * softplus(raw + rates_ref[1:2, :])
        docs = doc_window[PAD:]
        fresh = (docs == doc_window[PAD - 1 : PAD]).astype(F32)
        aux = jnp.where(lane < 2 * heads, beta, jnp.where(lane < 3 * heads, decay, 0.0))
        aux = jnp.where(lane == 3 * heads, docs, jnp.where(lane == 3 * heads + 1, fresh, aux))
        aux_ref[rows, :] = aux
        for head in range(heads):
            cols = slice(head * DK, (head + 1) * DK)
            for kind in (1, 2, 0, 3, 4):
                first_col = (0, 2, 3, 4, 5)[kind] * half + head * DK
                window = pre_ref[
                    pl.ds(pl.multiple_of(block * STRETCH, STRETCH), STRETCH + PAD), first_col : first_col + DK
                ]
                value = conv_window(window, conv_ref[kind, :, cols], same)
                value = value * jax.nn.sigmoid(value)
                if kind < 3:
                    value = value * lax.rsqrt(jnp.sum(value * value, axis=-1, keepdims=True) + 1e-06)
                if kind == 0:
                    q_ref[rows, cols] = value * DK ** (-0.5)
                elif kind < 3:
                    k_ref[kind - 1, rows, cols] = value.astype(BF)
                else:
                    v_ref[kind - 3, rows, cols] = value.astype(BF)
        aux2, run2, aux_t, run_t = block_scalars(aux)
        mats = []
        for head in range(heads):
            cols = slice(head * DK, (head + 1) * DK)
            beta, run_col, run_row, doc_col, doc_row, carried, to_last = head_terms(
                aux, aux2, run2, aux_t, run_t, head, heads
            )
            decay = decay_matrix(run_col, run_row, doc_col, doc_row, p_row, p_col)
            keys = keys_of(rows, cols)
            gram = dot1(keys, keys, NT)
            mats.append(beta * jnp.where(p_row > p_col, decay * gram, 0.0))
            attn[block * heads + head] = decay[STRETCH:] * dot3(q_ref[rows, cols], keys, NT)
        return mats

    def prepare(turn, carry):
        mats = []
        for i in range(together):
            mats += prepare_block(turn * together + i)
        for i, inv in enumerate(inverse(mats, masks)):
            inv_ref[turn * together * heads + i] = inv
        run_slot(slots[:turns], turn)
        return carry

    lax.fori_loop(0, blocks // together, prepare, 0)
    for copy in early:
        copy.start()
    keep_wo.wait()
    for head in range(heads):
        state_ref[head] = jnp.zeros((DK, DK), F32)

    def attn_copy(index):
        rows = chunk_rows(index)
        return remote(attn_own.at[rows], attn_in.at[rows], a_send.at[index], a_recv.at[index], place.peer)


    def advance(block, carry):
        rows = pl.ds(pl.multiple_of(block * STRETCH, STRETCH), STRETCH)
        aux = aux_ref[rows, :]
        aux2, run2, aux_t, run_t = block_scalars(aux)
        def of_head(head):
            cols = slice(head * DK, (head + 1) * DK)
            beta, run_col, run_row, doc_col, doc_row, carried, to_last = head_terms(
                aux, aux2, run2, aux_t, run_t, head, heads
            )
            keys = keys_of(rows, cols)
            values = jnp.concatenate([v_ref[0, rows, cols], v_ref[1, rows, cols]], axis=0).astype(F32)
            state = state_ref[block * heads + head]
            state_parts = split(state)
            yield
            target = beta * (values - carried * dot3(keys, state_parts))
            yield
            pseudo = dot3(inv_ref[block * heads + head], target)
            pseudo_ref[block * heads + head] = pseudo
            yield
            mixed = carried[STRETCH:] * dot3(q_ref[rows, cols], state_parts) + dot3(
                attn[block * heads + head], pseudo
            )
            yield
            state_ref[(block + 1) * heads + head] = carried[span - 1 : span] * state + dot3(
                keys, to_last * pseudo, TN
            )
            yield
            mixed_ref[rows, cols] = mixed
            scale = lax.rsqrt(jnp.mean(mixed * mixed, axis=-1, keepdims=True) + 1e-05)
            gate = pre_ref[
                pl.ds(pl.multiple_of(block * STRETCH, STRETCH) + PAD, STRETCH),
                half + head * DK : half + (head + 1) * DK,
            ]
            gated_ref[rows, cols] = (mixed * scale * mix_ref[...] * (gate * jax.nn.sigmoid(gate))).astype(BF)
        for _ in itertools.zip_longest(*[of_head(head) for head in range(heads)]):
            pass
        run_slot(slots[turns:], block)
        per_chunk = CHUNK // STRETCH

        def hand_over():
            chunk = block // per_chunk
            rows = chunk_rows(chunk)
            attn_own[rows, :] = product(gated_ref[rows, :], wo[...].reshape(-1, half), NT).astype(BF)
            attn_copy(chunk).start()

        pl.when(lax.rem(block, per_chunk) == per_chunk - 1)(hand_over)
        return carry

    lax.fori_loop(0, blocks, advance, 0)
    for copy in late:
        copy.start()
    for step in later[spread:]:
        step()

    def middle(index, carry):
        rows = chunk_rows(index)
        attn_copy(index).wait_recv()
        both = attn_own[rows, :].astype(F32) + attn_in[rows, :].astype(F32)
        middle_ref[rows, :] = x_ref[rows, :].astype(F32) + both
        return carry

    lax.fori_loop(0, seq // CHUNK, middle, 0)
    for part in (1, 2, 3):
        second.ready(part)

    def handed(index, carry):
        attn_copy(index).wait_send()
        return carry

    lax.fori_loop(0, seq // CHUNK, handed, 0)
    for swap in swaps:
        swap.wait_send()
    for part in range(3):
        first.drain(part)
    for part in range(4):
        second.drain(part)
    for copy in [keep_front, keep_pre] + early + late:
        copy.wait()


def front_call(line, x, docs, norm, wq, wg, wk, wv, beta, alpha, wo, gate, up, down, log, bias, cq, ck, cv, mix):
    seq, half = x.shape[0], wq.shape[1]
    depth, ff = gate.shape
    tail = half + 3 * ff
    heads, blocks = half // DK, seq // STRETCH
    units, span = heads * blocks, 2 * STRETCH
    width = 6 * half + DK
    shape = jax.ShapeDtypeStruct
    anywhere = pl.BlockSpec(memory_space=pl.ANY)
    dma = pltpu.SemaphoreType.DMA
    kept = (
        shape((seq, half), F32),
        shape((units, span, span), F32),
        shape((units + heads, DK, DK), F32),
        shape((units, span, DK), F32),
        shape((seq + PAD, width), F32),
        shape((seq, half), F32),
        shape((2, seq, half), BF),
        shape((2, seq, half), BF),
        shape((seq, DK), F32),
    )
    low = pltpu.VMEM(x.shape, BF)
    chunks = seq // CHUNK
    return pl.pallas_call(
        functools.partial(front_kernel, line, heads),
        out_shape=(
            shape((seq, half), BF),
            shape(x.shape, F32),
            shape((5, KW, half), F32),
            shape((2, DK), F32),
        )
        + kept
        + (
            shape((4 * line, depth, width), BF),
            shape((4 * line, depth, tail), BF),
        ),
        in_specs=[VMEM] * 19,
        out_specs=(VMEM,) * 4 + (anywhere,) * 11,
        scratch_shapes=[pltpu.VMEM(array.shape, array.dtype) for array in kept]
        + [
            pltpu.VMEM((4 * line, depth, width), BF),
            pltpu.VMEM((depth, tail), BF),
            pltpu.VMEM((4 * line, depth, half), BF),
            low,
            pltpu.VMEM((seq + PAD, DK), F32),
            pltpu.VMEM((units, STRETCH, span), F32),
            pltpu.VMEM((depth, DK), BF),
            pltpu.VMEM((depth, DK), BF),
            low,
            low,
            dma((12,)),
            dma((5,)),
            dma((5,)),
            dma((chunks,)),
            dma((chunks,)),
        ]
        + gather_sems(line, 3)
        + gather_sems(line, 4),
        compiler_params=pltpu.CompilerParams(
            collective_id=0, has_side_effects=True, vmem_limit_bytes=60 << 20
        ),
        name="front",
    )(x, docs, norm, wq, wg, wk, wv, beta, alpha, wo, gate, up, down, log, bias, cq, ck, cv, mix)


CHUNK = 128


def chunk_rows(index):
    return pl.ds(pl.multiple_of(index * CHUNK, CHUNK), CHUNK)


def pair_rows(index):
    return pl.ds(pl.multiple_of(index * 2 * CHUNK, 2 * CHUNK), 2 * CHUNK)


def flat(ref, start, width):
    return ref[:, :, :, :, start : start + width].reshape(-1, width)


def put_blocks(ref, index, cols, value):
    depth = ref.shape[3]
    count = DK // depth
    value = value.astype(BF)
    if count == 2:
        ref[index // 2, index % 2, :, :, cols] = value.reshape(2, depth, value.shape[-1])
    else:
        ref[pl.ds(index * (count // 4), count // 4), :, :, :, cols] = value.reshape(
            count // 4, 2, 2, depth, value.shape[-1]
        )


def rest_kernel(
    line, heads, gated_ref, x_ref, cot_ref, middle_ref, domains_ref, gain_ref, norm_ref, docs_ref, conv_ref, rates_ref, mix_ref,
    w_hbm, fw_hbm, pre_hbm, q_hbm, k_hbm, v_hbm, aux_hbm, mixed_hbm, inv_hbm, state_hbm, pseudo_hbm,
    out_ref, igrad_ref, sum_ref, gq_ref, gg_ref, gk_ref, gv_ref, gs_ref, gcq_ref, gck_ref, gcv_ref, gnorm_ref,
    gffn_ref, gtiny_ref,
    w_ref, fw_ref, attn_own, attn_in, in_own, in_in, normed, seed_low, work, back_ref, dgated_ref,
    dstate, doc_cols, dy_next, dconv_ref, dscal_ref, dgain_ref, total, mid, far, path,
    pre_s, q_s, k_s, v_s, aux_s, mixed_s, inv_s, state_s, pseudo_s,
    small, small_in, small_line, small_sum, mix_in, scal_in,
    load_sem, stream_sem, f_send, f_recv, o_send, o_recv, n_send, n_recv, h_send, h_recv,
    m_send, m_recv, l_send, l_recv, free_sem, *sems,
):
    place = Place(line)
    side, me = place.side, place.dp
    seq, width = x_ref.shape
    half = gated_ref.shape[1]
    tail = sum_ref.shape[-1]
    ff = (tail - half) // 3
    chunks = seq // CHUNK
    blocks = seq // STRETCH
    span = 2 * STRETCH
    gate_up = (half, 2 * ff)
    down = (half + 2 * ff, ff)
    scal_at = 6 * half
    front_width = scal_at + DK

    def load(index, start, count):
        cols = pl.ds(start, count)
        return pltpu.make_async_copy(w_hbm.at[:, :, :, :, cols], w_ref.at[:, :, :, :, cols], load_sem.at[index])

    loads = [load(0, 0, half), load(1, *gate_up), load(2, *down)]
    load_front = pltpu.make_async_copy(fw_hbm, fw_ref, load_sem.at[3])
    for copy in loads:
        copy.start()
    place.enter(everyone=True)

    def streams(block, slot):
        units = pl.ds(block * heads, heads)
        rows = pl.ds(pl.multiple_of(block * STRETCH, STRETCH), STRETCH)
        pairs = [
            (pre_hbm.at[pl.ds(pl.multiple_of(block * STRETCH, STRETCH), STRETCH + PAD)], pre_s),
            (q_hbm.at[rows], q_s),
            (k_hbm.at[:, rows], k_s),
            (v_hbm.at[:, rows], v_s),
            (aux_hbm.at[rows], aux_s),
            (mixed_hbm.at[rows], mixed_s),
            (inv_hbm.at[units], inv_s),
            (state_hbm.at[units], state_s),
            (pseudo_hbm.at[units], pseudo_s),
        ]
        return [
            pltpu.make_async_copy(src, dst.at[slot], stream_sem.at[slot, i]) for i, (src, dst) in enumerate(pairs)
        ]

    domains = domains_ref[...]
    rows_all = domains.shape[1]
    places = iota(domains.shape, 1)
    mine = jnp.sum(jnp.where(places == me, domains, 0), axis=1, keepdims=True)
    count = jnp.sum((domains == mine).astype(F32), axis=1, keepdims=True)
    row_weight = 2.0 / (1.0 + count * (GROUPS / rows_all))

    def in_copy(index):
        rows = chunk_rows(index)
        return remote(in_own.at[rows], in_in.at[rows], f_send.at[index], f_recv.at[index], place.peer)

    gffn_ref[...] = jnp.zeros_like(gffn_ref)
    for copy in loads:
        copy.wait()

    def feed(index, carry):
        rows = chunk_rows(index)
        middle = middle_ref[rows, :]
        scale = lax.rsqrt(jnp.mean(middle * middle, axis=-1, keepdims=True) + 1e-06)
        low = (middle * scale * gain_ref[...]).astype(BF)
        normed[rows, :] = low
        both = product(low, flat(w_ref, *gate_up))
        gate_in, up_in = both[:, :ff], both[:, ff:]
        sigmoid = jax.nn.sigmoid(gate_in)
        silu = gate_in * sigmoid
        seed = (cot_ref[rows, :].astype(F32) * row_weight).astype(BF)
        seed_low[rows, :] = seed
        hidden_back = product(seed, flat(w_ref, *down))
        gate_back = (hidden_back * up_in * (sigmoid * (1.0 + gate_in * (1.0 - sigmoid)))).astype(BF)
        up_back = (hidden_back * silu).astype(BF)
        work[rows, 0:ff] = gate_back
        work[rows, ff : 2 * ff] = up_back
        low_hidden = (silu * up_in).astype(BF)
        work[rows, 2 * ff : 3 * ff] = low_hidden
        return carry

    def feed_pair(step, carry):
        index = chunks // 2 - 1 - step
        lax.fori_loop(2 * index, 2 * index + 2, feed, 0)
        rows = pair_rows(index)
        in_own[rows, :] = product(work[rows, 0 : 2 * ff], flat(w_ref, *gate_up), NT).astype(BF)
        in_copy(2 * index).start()
        in_copy(2 * index + 1).start()
        attn_own[rows, :] = product(work[rows, 2 * ff : 3 * ff], flat(w_ref, *down), NT).astype(BF)
        return carry

    lax.fori_loop(0, chunks // 2, feed_pair, 0)

    def weigh(index, carry):
        cols = pl.ds(pl.multiple_of(index * DK, DK), DK)
        put_blocks(w_ref, index, slice(half, half + 2 * ff), product(normed[:, cols], work[:, 0 : 2 * ff], TN))
        return carry

    def weigh_down(index, carry):
        cols = pl.ds(pl.multiple_of(index * DK, DK), DK)
        here = slice(half + 2 * ff, half + 3 * ff)
        put_blocks(w_ref, index, here, product(seed_low[:, cols], work[:, 2 * ff : 3 * ff], TN))
        return carry

    lax.fori_loop(0, width // DK, weigh, 0)
    cuts = [(half, ff), (half + ff, ff), (half + 2 * ff, ff), (0, half)]
    scatter = Scatter(place, w_ref, sum_ref, cuts, (mid, far, path), sems[:8])
    parts = range(len(cuts))
    scatter.begin(0)
    scatter.begin(1)
    lax.fori_loop(0, width // DK, weigh_down, 0)
    scatter.begin(2)
    scatter.merge(0, 0)
    scatter.merge(0, 1)
    merges = [functools.partial(scatter.merge, part, which) for part in (1, 2) for which in (0, 1)]
    for step in merges:
        step()


    def finish(index, carry):
        rows = chunk_rows(index)
        in_copy(index).wait_recv()
        grad = in_own[rows, :].astype(F32) + in_in[rows, :].astype(F32)
        middle = middle_ref[rows, :]
        scale = lax.rsqrt(jnp.mean(middle * middle, axis=-1, keepdims=True) + 1e-06)
        unit = middle * scale
        gffn_ref[...] += jnp.sum(grad * unit, axis=0, keepdims=True)
        grad = grad * gain_ref[...]
        seed = cot_ref[rows, :].astype(F32) * row_weight
        total = seed + scale * (grad - unit * jnp.mean(unit * grad, axis=-1, keepdims=True))
        back_ref[rows, :] = total
        low = total.astype(BF)
        seed_low[rows, :] = low
        dgated_ref[rows, :] = product(low, flat(w_ref, 0, half))
        return carry

    half_way = chunks // 2
    lax.fori_loop(half_way, chunks, finish, 0)
    streams_first = streams(blocks - 1, (blocks - 1) % 2)
    for copy in streams_first:
        copy.start()

    def weigh_out(index, carry):
        cols = pl.ds(pl.multiple_of(index * DK, DK), DK)
        put_blocks(w_ref, index, slice(0, half), product(seed_low[:, cols], gated_ref[...], TN))
        return carry

    swap = remote(attn_own, attn_in, o_send, o_recv, place.peer)
    load_front.start()


    masks = block_masks()
    t_row, t_col, p_row, p_col = masks
    strict = p_row > p_col
    for head in range(heads):
        dstate[head] = jnp.zeros((DK, DK), F32)
    dgain_ref[...] = jnp.zeros_like(dgain_ref)
    dconv_ref[...] = jnp.zeros_like(dconv_ref)
    dscal_ref[...] = jnp.zeros_like(dscal_ref)
    dy_next[...] = jnp.zeros_like(dy_next)
    doc_cols[0:PAD, :] = jnp.full((PAD, DK), -1.0, F32)
    doc_cols[PAD + seq :, :] = jnp.full((PAD, DK), -1.0, F32)
    for i in range(seq // DK):
        lane_docs = docs_ref[:, i * DK : (i + 1) * DK].astype(F32)
        doc_cols[PAD + i * DK : PAD + (i + 1) * DK, :] = jnp.broadcast_to(lane_docs, (DK, DK)).T
    upper = (iota((STRETCH, STRETCH), 0) <= iota((STRETCH, STRETCH), 1)).astype(F32)
    lanes = iota((STRETCH, DK), 1)
    wide_rows = iota((span, DK), 0)
    select = scalar_select(side, heads)
    rate = -jnp.exp(rates_ref[0:1, :])
    scal_at = 6 * half
    scal_cols = slice(scal_at, scal_at + DK)

    chains = [scatter.stages(part) for part in parts]
    slots = [[] for _ in range(blocks)]
    left, before = [], []
    slots[blocks // 2] += [functools.partial(scatter.merge, parts[-1], which) for which in (0, 1)]
    for part, turn in ((0, 1), (1, 4), (2, 6)):
        for step in chains[part]:
            (slots[turn] if turn < blocks else left if part == 2 else before).append(step)
            turn += step is not chains[part][0]

    def back(step, carry):
        block = blocks - 1 - step
        top = pl.multiple_of(block * STRETCH, STRETCH)
        rows = pl.ds(top, STRETCH)
        slot = lax.rem(block, 2)
        for copy in streams(block, slot):
            copy.wait()

        def fetch():
            for copy in streams(block - 1, 1 - slot):
                copy.start()

        pl.when(block > 0)(fetch)
        aux = aux_s[slot]
        aux2, run2, aux_t, run_t = block_scalars(aux)
        doc_window = doc_cols[pl.ds(top, STRETCH + 2 * PAD), :]
        same = same_documents(doc_window[: STRETCH + PAD])
        here = doc_window[PAD : PAD + STRETCH]
        same_next = [doc_window[PAD + o : PAD + o + STRETCH] == here for o in range(1, KW)]
        dbeta_all = jnp.zeros((STRETCH, DK), F32)
        drun_all = jnp.zeros((STRETCH, DK), F32)
        column_sums = jnp.zeros((span, DK), F32)

        def conv_back(kind, head, grad):
            first_col = (0, 2, 3, 4, 5)[kind] * half + head * DK
            cols = slice(head * DK, (head + 1) * DK)
            window = pre_s[slot, :, first_col : first_col + DK]
            kernel = conv_ref[kind, :, cols]
            shifted = [window[PAD:]] + [
                jnp.where(same[o - 1], window[PAD - o : PAD - o + STRETCH], 0.0) for o in range(1, KW)
            ]
            y = shifted[0] * kernel[0:1]
            for o in range(1, KW):
                y = y + shifted[o] * kernel[o : o + 1]
            sigmoid = jax.nn.sigmoid(y)
            act = y * sigmoid
            if kind < 3:
                scale = lax.rsqrt(jnp.sum(act * act, axis=-1, keepdims=True) + 1e-06)
                unit = act * scale
                if kind == 0:
                    grad = grad * DK ** (-0.5)
                grad = scale * (grad - unit * jnp.sum(unit * grad, axis=-1, keepdims=True))
            dy = grad * (sigmoid * (1.0 + y * (1.0 - sigmoid)))
            for o in range(KW):
                dconv_ref[kind, o : o + 1, cols] += jnp.sum(dy * shifted[o], axis=0, keepdims=True)
            at = slice(kind * half + head * DK, kind * half + (head + 1) * DK)
            longer = jnp.concatenate([dy, dy_next[:, at]], axis=0)
            dy_next[:, at] = dy[:PAD]
            dpre = dy * kernel[0:1]
            for o in range(1, KW):
                dpre = dpre + jnp.where(same_next[o - 1], longer[o : o + STRETCH], 0.0) * kernel[o : o + 1]
            work[rows, first_col : first_col + DK] = dpre.astype(BF)

        def of_head(head):
            nonlocal dbeta_all, drun_all, column_sums
            cols = slice(head * DK, (head + 1) * DK)
            gate_cols = slice(half + head * DK, half + (head + 1) * DK)
            beta, run_col, run_row, doc_col, doc_row, carried, to_last = head_terms(
                aux, aux2, run2, aux_t, run_t, head, heads
            )
            decay = decay_matrix(run_col, run_row, doc_col, doc_row, p_row, p_col)
            keys = jnp.concatenate([k_s[slot, 0, :, cols], k_s[slot, 1, :, cols]], axis=0)
            queries = q_s[slot, :, cols]
            mixed = mixed_s[slot, :, cols]
            gate = pre_s[slot, PAD:, gate_cols]
            sigmoid = jax.nn.sigmoid(gate)
            silu = gate * sigmoid
            scale = lax.rsqrt(jnp.mean(mixed * mixed, axis=-1, keepdims=True) + 1e-05)
            scaled = mixed * scale
            dgated = dgated_ref[rows, cols]
            part = dgated * scaled
            work[rows, gate_cols] = (
                part * mix_ref[...] * (sigmoid * (1.0 + gate * (1.0 - sigmoid)))
            ).astype(BF)
            dgain_ref[...] += jnp.sum(part * silu, axis=0, keepdims=True)
            dscaled = dgated * mix_ref[...] * silu
            dout = scale * (dscaled - scaled * jnp.mean(dscaled * scaled, axis=-1, keepdims=True))

            state, pseudo = state_s[slot, head], pseudo_s[slot, head]
            yield
            dnext = dstate[head]
            dnext_parts, state_parts, pseudo_parts = split(dnext), split(state), split(pseudo)
            dout_parts, q_parts = split(dout), split(queries)
            gram = dot1(keys, keys, NT)
            core = jnp.where(strict, decay * gram, 0.0)
            yield
            amat = beta * core
            qdecay = decay[STRETCH:]
            attn = qdecay * dot3(q_parts, keys, NT)
            yield
            dattn = dot3(dout_parts, pseudo_parts, NT)
            dqk = split(qdecay * dattn)
            yield
            dpseudo = dot3(attn, dout_parts, TN) + to_last * dot3(keys, dnext_parts)
            yield
            dtarget = dot3(inv_s[slot, head], dpseudo, TN)
            yield
            dtarget_parts = split(dtarget)
            damat = jnp.where(strict, -dot3(dtarget_parts, pseudo_parts, NT), 0.0)
            e_a, e_m = damat * amat, dattn * attn
            yield
            dgram = split(beta * decay * damat)
            dbeta = jnp.sum(dtarget * pseudo, axis=-1, keepdims=True) / jnp.maximum(beta, 1e-30)
            dvalues = (beta * dtarget).astype(BF).astype(F32)
            dread = -(beta * carried) * dtarget
            dout_c = carried[STRETCH:] * dout
            dread_parts, dout_c_parts = split(dread), split(dout_c)
            last = carried[span - 1 : span]
            yield
            dstate[head] = last * dnext + dot3(keys, dread_parts, TN) + dot3(q_parts, dout_c_parts, TN)
            yield
            dq_state = dot3(dout_c_parts, state_parts, NT)
            dk_state = dot3(dread_parts, state_parts, NT)
            yield
            dk_last = dot3(to_last * pseudo, dnext_parts, NT)
            yield
            conv_back(0, head, dq_state + dot3(dqk, keys))
            yield
            dkeys = (
                dk_state + dk_last + dot3(dgram, keys) + dot3(dgram, keys, TN) + dot3(dqk, q_parts, TN)
            ).astype(BF).astype(F32)
            yield
            conv_back(1, head, dkeys[:STRETCH])
            yield
            conv_back(2, head, dkeys[STRETCH:])
            yield
            conv_back(3, head, dvalues[:STRETCH])
            yield
            conv_back(4, head, dvalues[STRETCH:])

            yield
            wide = keys.astype(F32)
            e_last = jnp.sum(wide * dk_last, axis=-1, keepdims=True)
            drun = jnp.sum(e_a, axis=-1, keepdims=True) - e_last + jnp.sum(wide * dk_state, axis=-1, keepdims=True)
            drun_q = jnp.sum(e_m, axis=-1, keepdims=True) + jnp.sum(queries * dq_state, axis=-1, keepdims=True)
            at_last = jnp.sum(e_last, axis=0, keepdims=True) + last * jnp.sum(
                jnp.sum(dnext * state, axis=-1, keepdims=True), axis=0, keepdims=True
            )
            drun = drun[:STRETCH] + drun[STRETCH:] + drun_q
            drun = drun + jnp.where(iota((STRETCH, 1), 0) == STRETCH - 1, at_last, 0.0)
            lane = 2 * heads + head
            drun_all = jnp.where(lanes == lane, drun, drun_all)
            dbeta_all = jnp.where(lanes == head, dbeta[:STRETCH], dbeta_all)
            dbeta_all = jnp.where(lanes == heads + head, dbeta[STRETCH:], dbeta_all)
            sums = jnp.sum(e_a, axis=0, keepdims=True) + jnp.sum(e_m, axis=0, keepdims=True)
            column_sums = jnp.where(wide_rows == lane, sums, column_sums)
        for _ in itertools.zip_longest(*[of_head(head) for head in range(heads)]):
            pass
        down = column_sums.T
        ddecay = dot6(upper, drun_all - down[:STRETCH] - down[STRETCH:])
        raw = dot6(pre_s[slot, PAD:, scal_cols], select)
        sigmoid = jax.nn.sigmoid(raw)
        shifted = raw + rates_ref[1:2, :]
        draw_decay = ddecay * rate * jax.nn.sigmoid(shifted)
        is_decay = (lanes >= 2 * heads) & (lanes < 3 * heads)
        draw_decay = jnp.where(is_decay, draw_decay, 0.0)
        dscal_ref[0:1, :] += jnp.sum(
            jnp.where(is_decay, ddecay * rate * softplus(shifted), 0.0), axis=0, keepdims=True
        )
        dscal_ref[1:2, :] += jnp.sum(draw_decay, axis=0, keepdims=True)
        dbeta_low = dbeta_all.astype(BF).astype(F32)
        draw = jnp.where(lanes < 2 * heads, dbeta_low * 2.0 * sigmoid * (1.0 - sigmoid), draw_decay)
        work[rows, scal_cols] = dot6(draw, select, NT).astype(BF)
        run_slot(slots, step)
        return carry

    lax.fori_loop(0, blocks // 2, back, 0)
    lax.fori_loop(0, half_way, finish, 0)
    lax.fori_loop(0, width // DK, weigh_out, 0)
    scatter.begin(parts[-1])
    swap.start()
    lax.fori_loop(blocks // 2, blocks, back, 0)
    mix_swap = remote(dgain_ref, mix_in, m_send.at[2], m_recv.at[2], place.peer)
    mix_swap.start()

    def normalise(index, carry):
        rows = chunk_rows(index)
        x = x_ref[rows, :].astype(F32)
        scale = lax.rsqrt(jnp.mean(x * x, axis=-1, keepdims=True) + 1e-06)
        normed[rows, :] = (x * scale * norm_ref[...]).astype(BF)
        return carry

    lax.fori_loop(0, chunks, normalise, 0)

    def in_sent(index, carry):
        in_copy(index).wait_send()
        return carry

    lax.fori_loop(0, chunks, in_sent, 0)

    def weigh_front(start, count):
        def one(index, carry):
            cols = pl.ds(pl.multiple_of(index * DK, DK), DK)
            here = slice(start, start + count)
            put_blocks(w_ref, index, here, product(normed[:, cols], work[:, here], TN))
            return carry

        lax.fori_loop(0, width // DK, one, 0)

    for part in parts:
        scatter.drain_sibling(part)
    weigh_front(2 * half, 2 * half)

    def release(stage):
        for part in ((0, 1), (2, 3))[stage]:
            scatter.drain(part)
        sem = free_sem.at[stage]
        for device in (place.sibling, place.across):
            pl.semaphore_signal(sem, inc=1, device_id=device, device_id_type=MESH)
        for way in (0, 1):
            pl.when(place.can_send[way])(
                lambda way=way: pl.semaphore_signal(sem, inc=1, device_id=place.ahead[way], device_id_type=MESH)
            )

    def await_release(stage):
        senders = 2 + place.can_send[0].astype(jnp.int32) + place.can_send[1].astype(jnp.int32)
        pl.semaphore_wait(free_sem.at[stage], senders)

    cuts = [(2 * half, 2 * half), (4 * half, 2 * half + DK), (0, half), (half, half)]
    later = Scatter(place, w_ref, total, cuts, (mid, far, path), sems[8:])
    for step in before:
        step()
    release(0)
    await_release(0)
    later.begin(0)
    weigh_front(4 * half, 2 * half + DK)
    later.begin(1)
    weigh_front(0, 2 * half)
    load_front.wait()

    def outputs(index, carry):
        rows = chunk_rows(index)
        both = attn_own[rows, :].astype(F32) + attn_in[rows, :].astype(F32)
        out_ref[rows, :] = (middle_ref[rows, :] + both).astype(BF)
        return carry

    def nb_copy(index):
        rows = chunk_rows(index)
        return remote(in_own.at[rows], in_in.at[rows], n_send.at[index], n_recv.at[index], place.peer)

    def project_back(index):
        rows = pair_rows(index)
        in_own[rows, :] = product(work[rows, 0:front_width], flat(fw_ref, 0, front_width), NT).astype(BF)
        nb_copy(2 * index).start()
        nb_copy(2 * index + 1).start()

    swap.wait_recv()
    project_back(0)
    later.merge(0, 0)
    later.merge(0, 1)
    for step in left + chains[3][:2]:
        step()
    for index in range(1, chunks // 2):
        project_back(index)
    later.merge(1, 0)
    later.merge(1, 1)
    chains[3][2]()
    lax.fori_loop(0, chunks, outputs, 0)
    for step in chains[3][3:]:
        step()
    release(1)
    await_release(1)
    later.begin(2)
    later.begin(3)
    gnorm_ref[...] = jnp.zeros_like(gnorm_ref)

    def finish_back(index, carry):
        rows = chunk_rows(index)
        nb_copy(index).wait_recv()
        back = in_own[rows, :].astype(F32) + in_in[rows, :].astype(F32)
        x = x_ref[rows, :].astype(F32)
        scale = lax.rsqrt(jnp.mean(x * x, axis=-1, keepdims=True) + 1e-06)
        unit = x * scale
        gnorm_ref[...] += jnp.sum(back * unit, axis=0, keepdims=True)
        back = back * norm_ref[...]
        total_back = back_ref[rows, :] + scale * (back - unit * jnp.mean(unit * back, axis=-1, keepdims=True))
        igrad_ref[rows, :] = total_back.astype(BF)
        return carry

    small_swaps = [
        remote(small, small_in.at[0], m_send.at[0], m_recv.at[0], place.sibling),
        remote(small_sum, small_in.at[1], m_send.at[1], m_recv.at[1], place.across),
    ]

    def line_copy(target):
        device = (target * 4 + place.x * 2 + place.c, side)
        return remote(small_line.at[place.z], small_line.at[place.z], l_send.at[target], l_recv.at[place.z], device)

    def line_from(source):
        device = (source * 4 + place.x * 2 + place.c, side)
        return remote(small_line.at[source], small_line.at[source], l_send.at[source], l_recv.at[source], device)

    def collect():
        mix_swap.wait_recv()
        small[0:5] = dconv_ref[...]
        for i in range(2):
            small[5, i : i + 1, :] = gnorm_ref[:, i * half : (i + 1) * half]
            small[5, 2 + i : 3 + i, :] = gffn_ref[:, i * half : (i + 1) * half]
        small[6] = jnp.zeros((KW, half), F32)
        small[6, 0:1, 0:DK] = dgain_ref[...] + mix_in[...]
        small[6, 0:1, DK : 2 * DK] = dscal_ref[0:1, :]
        small[6, 0:1, 2 * DK : 3 * DK] = dscal_ref[1:2, :]
        small_swaps[0].start()

    def collect_across():
        small_swaps[0].wait_recv()
        small_sum[...] = small[...] + small_in[0]
        small_swaps[1].start()

    def collect_line():
        small_swaps[1].wait_recv()
        small_line[place.z] = small_sum[...] + small_in[1]
        for target in range(line):
            pl.when(target != place.z)(lambda target=target: line_copy(target).start())

    home = [
        remote(
            total.at[:, pl.ds(pl.multiple_of((base + 1 - side) * half, half), half)],
            ref.at[:, pl.ds(pl.multiple_of(side * half, half), half)],
            h_send.at[i], h_recv.at[i], place.peer,
        )
        for i, (base, ref) in enumerate(((2, gk_ref), (4, gv_ref)))
    ]
    scal_home = remote(total.at[:, scal_at : scal_at + DK], scal_in, h_send.at[2], h_recv.at[2], place.peer)
    own_half = pl.ds(pl.multiple_of(side * half, half), half)

    def at_home(i):
        base, ref = ((2, gk_ref), (4, gv_ref))[i]
        home[i].start()
        ref[:, own_half] = total[:, pl.ds(pl.multiple_of((base + side) * half, half), half)]

    def at_home_value():
        at_home(1)
        scal_home.start()

    after = [later.stages(part) for part in range(4)]
    homes = [functools.partial(at_home, 0), at_home_value]
    merge = functools.partial
    slots = [
        [merge(later.merge, 2, 0), merge(later.merge, 2, 1)],
        [merge(later.merge, 3, 0), merge(later.merge, 3, 1)],
        after[0][:2],
        after[0][2:3],
    ]

    def finish_and(index, carry):
        finish_back(index, carry)
        run_slot(slots, index)
        return carry

    lax.fori_loop(0, chunks, finish_and, 0)
    rest = after[0][3:-1] + after[1][:2] + after[0][-1:] + homes[:1] + after[1][2:-1] + after[2][:2] + after[1][-1:]
    rest += homes[1:] + after[3][:2]
    for pair in zip(after[2][2:], after[3][2:]):
        rest += pair
    extra = [collect, collect_across, collect_line]
    for i, step in enumerate(rest):
        if i % 2 == 0 and extra:
            extra.pop(0)()
        step()
    for step in extra:
        step()
    for source in range(line):
        pl.when(source != place.z)(lambda source=source: line_from(source).wait_recv())
    summed = small_line[0]
    for source in range(1, line):
        summed = summed + small_line[source]
    small_sum_out = summed
    gcq_ref[...] = small_sum_out[0]
    small_swaps[0].wait_send()
    small_swaps[1].wait_send()
    small[...] = small_sum_out
    conv_home = [
        remote(
            small.at[base + 1 - side], ref.at[:, own_half], h_send.at[i], h_recv.at[i], place.peer
        )
        for i, (base, ref) in ((3, (1, gck_ref)), (4, (3, gcv_ref)))
    ]
    for copy in conv_home:
        copy.start()
    gck_ref[:, own_half] = small[1 + side]
    gcv_ref[:, own_half] = small[3 + side]
    for i in range(2):
        gnorm_ref[:, i * half : (i + 1) * half] = small_sum_out[5, i : i + 1]
        gffn_ref[:, i * half : (i + 1) * half] = small_sum_out[5, 2 + i : 3 + i]
    gtiny_ref[...] = small_sum_out[6, 0:1, 0 : 3 * DK]
    gq_ref[...] = total[:, 0:half]
    gg_ref[...] = total[:, half : 2 * half]
    scal_home.wait_recv()
    lanes = iota(scal_in.shape, 1)
    ours = total[:, scal_at : scal_at + DK]
    theirs = pltpu.roll(scal_in[...], DK - 2 * heads, 1)
    gs_ref[...] = jnp.where(lanes < 2 * heads, ours + theirs, ours)
    for copy in home + conv_home:
        copy.wait_recv()
    for copy in home + conv_home + [scal_home, mix_swap]:
        copy.wait_send()
    for target in range(line):
        pl.when(target != place.z)(lambda target=target: line_copy(target).wait_send())

    def sent(index, carry):
        nb_copy(index).wait_send()
        return carry

    lax.fori_loop(0, chunks, sent, 0)
    for part in range(4):
        later.drain_sibling(part)
        later.drain(part)
    swap.wait_send()


def rest_call(line, gated, x, cot, middle, domains, gain, norm, docs, conv, rates, mix, w, fw, pre, q, k, v, aux, mixed, inv, state, pseudo):
    seq, width = x.shape
    half = gated.shape[1]
    heads = half // DK
    depth, tail = w.shape[3:]
    columns = fw.shape[-1]
    ff = (tail - half) // 3
    shape = jax.ShapeDtypeStruct
    dma = pltpu.SemaphoreType.DMA
    chunks = seq // CHUNK
    span = 2 * STRETCH
    tiny = (7, KW, half)
    low = pltpu.VMEM((seq, width), BF)
    wide = pltpu.VMEM((seq, width), F32)
    return pl.pallas_call(
        functools.partial(rest_kernel, line, heads),
        out_shape=(
            shape((seq, width), BF),
            shape((seq, width), BF),
            shape((depth, tail), F32),
            shape((depth, half), F32),
            shape((depth, half), F32),
            shape((depth, 2 * half), F32),
            shape((depth, 2 * half), F32),
            shape((depth, DK), F32),
            shape((KW, half), F32),
            shape((KW, 2 * half), F32),
            shape((KW, 2 * half), F32),
            shape((1, width), F32),
            shape((1, width), F32),
            shape((1, 3 * DK), F32),
        ),
        in_specs=[VMEM] * 11 + [pl.BlockSpec(memory_space=pl.ANY)] * 11,
        out_specs=(VMEM,) * 14,
        scratch_shapes=[
            pltpu.VMEM(w.shape, BF),
            pltpu.VMEM(fw.shape, BF),
        ]
        + [low] * 6
        + [pltpu.VMEM((seq, 3 * ff), BF), wide, pltpu.VMEM((seq, half), F32)]
        + [
            pltpu.VMEM((heads, DK, DK), F32),
            pltpu.VMEM((seq + 2 * PAD, DK), F32),
            pltpu.VMEM((PAD, 5 * half), F32),
            pltpu.VMEM((5, KW, half), F32),
            pltpu.VMEM((2, DK), F32),
            pltpu.VMEM((1, DK), F32),
            pltpu.VMEM((depth, columns), F32),
        ]
        + scatter_scratch(line, depth, tail, False)
        + [
            pltpu.VMEM((2, STRETCH + PAD, columns), F32),
            pltpu.VMEM((2, STRETCH, half), F32),
            pltpu.VMEM((2, 2, STRETCH, half), BF),
            pltpu.VMEM((2, 2, STRETCH, half), BF),
            pltpu.VMEM((2, STRETCH, DK), F32),
            pltpu.VMEM((2, STRETCH, half), F32),
            pltpu.VMEM((2, heads, span, span), F32),
            pltpu.VMEM((2, heads, DK, DK), F32),
            pltpu.VMEM((2, heads, span, DK), F32),
        ]
        + [
            pltpu.VMEM(tiny, F32),
            pltpu.VMEM((2,) + tiny, F32),
            pltpu.VMEM((line,) + tiny, F32),
            pltpu.VMEM(tiny, F32),
            pltpu.VMEM((1, DK), F32),
            pltpu.VMEM((depth, DK), F32),
        ]
        + [dma((4,)), dma((2, 9))]
        + [dma((chunks,))] * 2
        + [dma, dma]
        + [dma((chunks,)), dma((chunks,)), dma((5,)), dma((5,)), dma((3,)), dma((3,)), dma((line,)), dma((line,))]
        + [pltpu.SemaphoreType.REGULAR((2,))]
        + scatter_sems(line, 4)
        + scatter_sems(line, 4),
        compiler_params=pltpu.CompilerParams(
            collective_id=1, has_side_effects=True, vmem_limit_bytes=63 << 20
        ),
        name="rest",
    )(gated, x, cot, middle, domains, gain, norm, docs, conv, rates, mix, w, fw, pre, q, k, v, aux, mixed, inv, state, pseudo)


def deliver_kernel(heads, *refs):
    count = (len(refs) - 21) // 2
    sources, outs, held, sems = refs[:count], refs[count : count + 20], refs[count + 20 : -1], refs[-1]
    copies = [pltpu.make_async_copy(src, dst, sems.at[i]) for i, (src, dst) in enumerate(zip(sources, held))]
    for copy in copies:
        copy.start()
    (
        out_ref, igrad_ref, sum_ref, gq_ref, gg_ref, gk_ref, gv_ref, gs_ref, gcq_ref, gck_ref, gcv_ref, gnorm_ref,
        gffn_ref, gtiny_ref,
    ) = held
    (
        output, input_grad, norm, query, outgate, key, value, beta, alpha, log, bias, c_query, c_key, c_value, mix,
        w_out, ffn, gate, up, down,
    ) = outs
    for copy in copies:
        copy.wait()
    output[0] = out_ref[...]
    input_grad[0] = igrad_ref[...]
    norm[...] = gnorm_ref[...]
    ffn[...] = gffn_ref[...]
    query[...] = gq_ref[...]
    outgate[...] = gg_ref[...]
    key[0] = gk_ref[...]
    value[0] = gv_ref[...]
    depth, half = query.shape
    ff = gate.shape[1]
    corner = (iota((depth, depth), 0) == iota((depth, depth), 1)).astype(F32)
    turned = dot6(gs_ref[...], corner, TN)
    beta[...] = turned[0 : 2 * heads]
    alpha[...] = turned[4 * heads : 5 * heads]
    here = slice(2 * heads, 3 * heads)
    log[...] = gtiny_ref[:, DK : 2 * DK][:, here]
    bias[...] = gtiny_ref[:, 2 * DK :][:, here]
    mix[...] = gtiny_ref[:, 0:DK]
    c_query[...] = gcq_ref[...]
    c_key[0] = gck_ref[...]
    c_value[0] = gcv_ref[...]
    w_out[...] = sum_ref[:, 0:half]
    gate[...] = sum_ref[:, half : half + ff]
    up[...] = sum_ref[:, half + ff : half + 2 * ff]
    down[...] = sum_ref[:, half + 2 * ff :]


def deliver_call(heads, *parts):
    seq, width = parts[0].shape
    depth, tail = parts[2].shape
    half = parts[3].shape[1]
    ff = (tail - half) // 3
    shape = lambda *dims: jax.ShapeDtypeStruct(dims, F32)
    low = jax.ShapeDtypeStruct((1, seq, width), BF)
    return pl.pallas_call(
        functools.partial(deliver_kernel, heads),
        out_shape=(
            low, low, shape(1, width), shape(depth, half), shape(depth, half), shape(1, depth, 2 * half),
            shape(1, depth, 2 * half), shape(2 * heads, depth), shape(heads, depth), shape(1, heads),
            shape(1, heads), shape(KW, half), shape(1, KW, 2 * half), shape(1, KW, 2 * half), shape(1, DK),
            shape(depth, half), shape(1, width), shape(depth, ff), shape(depth, ff), shape(depth, ff),
        ),
        in_specs=[pl.BlockSpec(memory_space=pl.ANY)] * 14,
        out_specs=(VMEM,) * 20,
        scratch_shapes=[pltpu.VMEM(part.shape, part.dtype) for part in parts]
        + [pltpu.SemaphoreType.DMA((len(parts),))],
        compiler_params=pltpu.CompilerParams(vmem_limit_bytes=63 << 20),
        name="deliver",
    )(*parts)


GROUPS = 8


def per_device(
    tokens,
    cotangent,
    domains,
    doc_ids,
    norm_gain,
    w_query,
    w_outgate,
    w_key,
    w_value,
    w_beta,
    w_alpha,
    decay_log,
    decay_bias,
    conv_query,
    conv_key,
    conv_value,
    mix_gain,
    w_out,
    ffn_gain,
    w_gate,
    w_up,
    w_down,
):
    line = lax.axis_size("dp") // 4
    by_place = lambda array: array.reshape((line, 2, 2) + array.shape[1:])
    gain_row = mix_gain[None]
    (
        gated, middle, conv, rates, mixed, inv, state, pseudo, pre, queries, keys, values, aux, front_w, back_w
    ) = front_call(
        line, tokens[0], doc_ids, norm_gain[None], w_query, w_outgate, w_key[0], w_value[0], w_beta[0].T, w_alpha.T,
        w_out.T, w_gate, w_up, w_down.T, decay_log[None], decay_bias[None], conv_query, conv_key[0], conv_value[0],
        gain_row,
    )
    parts = rest_call(
        line, gated, tokens[0], cotangent[0], middle, domains[None], ffn_gain[None], norm_gain[None], doc_ids, conv,
        rates, gain_row, by_place(back_w), by_place(front_w), pre, queries, keys, values, aux, mixed, inv, state,
        pseudo,
    )
    results = list(deliver_call(w_alpha.shape[1], *parts))
    for index in (2, 9, 10, 14, 16):
        results[index] = results[index][0]
    for index in (8, 15, 19):
        results[index] = results[index].T
    results[7] = results[7].T[None]
    return tuple(results)


def solution(mesh):
    return jax.shard_map(
        per_device,
        mesh=mesh,
        in_specs=(
            P("dp", None, None),
            P("dp", None, None),
            P(),
            P("dp", None),
            P(),
            P("dp", "step"),
            P("dp", "step"),
            P("step", "dp", None),
            P("step", "dp", None),
            P("step", "dp", None),
            P("dp", "step"),
            P("step"),
            P("step"),
            P(None, "step"),
            P("step", None, None),
            P("step", None, None),
            P(),
            P("step", "dp"),
            P(),
            P("dp", "step"),
            P("dp", "step"),
            P("step", "dp"),
        ),
        out_specs=(
            P("dp", None, None),
            P("dp", None, None),
            P(),
            P("dp", "step"),
            P("dp", "step"),
            P("step", "dp", None),
            P("step", "dp", None),
            P("step", "dp", None),
            P("dp", "step"),
            P("step"),
            P("step"),
            P(None, "step"),
            P("step", None, None),
            P("step", None, None),
            P(),
            P("step", "dp"),
            P(),
            P("dp", "step"),
            P("dp", "step"),
            P("step", "dp"),
        ),
        check_vma=False,
    )
```
